128 devices in a mesh: dp: 8 (over z_lo, x), seq: 16 (over y, z_hi, core).
Axes of the slice: x: 4, y: 4, z: 4 (z_hi: 2, z_lo: 2; z = z_hi * 2 + z_lo), core: 2. Of those that a mesh axis runs over, the one named last changes fastest.
Arguments:
- tokens: bfloat16 [8, 2048, 512], P('dp', 'seq'), may hold values from -6 to 6
- lengths: int32 [8], P('dp'), may hold values from 1408 to 2048, as said below
- norm1_gain: bfloat16 [512], P(('dp', 'seq')), may hold values from 0.099609375 to 1.8984375
- norm1_bias: bfloat16 [512], P(('dp', 'seq')), may hold values from -2 to 2
- w_query: bfloat16 [512, 512], P(('dp', 'seq')), may hold values from -0.375 to 0.375
- w_key: bfloat16 [512, 512], P(('dp', 'seq')), may hold values from -0.375 to 0.375
- w_value: bfloat16 [512, 512], P(('dp', 'seq')), may hold values from -0.25 to 0.25
- w_output: bfloat16 [512, 512], P(('dp', 'seq')), may hold values from -1.5 to 1.5
- norm2_gain: bfloat16 [512], P(('dp', 'seq')), may hold values from 0.099609375 to 1.8984375
- norm2_bias: bfloat16 [512], P(('dp', 'seq')), may hold values from -2 to 2
- w_gate: bfloat16 [512, 2048], P(('dp', 'seq')), may hold values from -0.25 to 0.25
- w_up: bfloat16 [512, 2048], P(('dp', 'seq')), may hold values from -0.25 to 0.25
- w_down: bfloat16 [2048, 512], P(('dp', 'seq')), may hold values from -0.25 to 0.25
- cotangent: bfloat16 [8, 2048, 512], P('dp', 'seq'), may hold values from -6 to 6
Outputs:
- layer_output: bfloat16 [8, 2048, 512], P('dp', 'seq')
- grad_tokens: float32 [8, 2048, 512], P('dp', 'seq')
- grad_norm1_gain: float32 [512], P(('dp', 'seq'))
- grad_norm1_bias: float32 [512], P(('dp', 'seq'))
- grad_w_query: float32 [512, 512], P(('dp', 'seq'))
- grad_w_key: float32 [512, 512], P(('dp', 'seq'))
- grad_w_value: float32 [512, 512], P(('dp', 'seq'))
- grad_w_output: float32 [512, 512], P(('dp', 'seq'))
- grad_norm2_gain: float32 [512], P(('dp', 'seq'))
- grad_norm2_bias: float32 [512], P(('dp', 'seq'))
- grad_w_gate: float32 [512, 2048], P(('dp', 'seq'))
- grad_w_up: float32 [512, 2048], P(('dp', 'seq'))
- grad_w_down: float32 [2048, 512], P(('dp', 'seq'))
The draws below stay inside these ranges and needn't reach their ends.
Inputs may be any that keep to these rules, and one draw needn't show every extreme that they name: `lengths`: in each group of 1 consecutive windows one window is longer than 1920, and some window has length 2048.
All inputs are finite; a program needn't handle non-finite values.
Results may differ from the reference program's by a relative error of at most 0.025.
Values may be sent and summed in bfloat16 or wider, within the bound.
No kernel may reach another device: no remote copies, remote signals or barrier semaphores. Data moves between devices by JAX's collectives and lax.ppermute only.
A program may use at most 128 MiB of HBM per device.

```python
import math
import jax
import jax.numpy as jnp
from jax import lax

D = 512
FF = 2048
HEADS = 16
HEAD = 32
LEN = 2048
WIN_DEV = 1
WINDOWS = 8


def draw_lengths(key, part):
    key = jax.random.fold_in(key, 11)
    first_key, second_key, third_key, fourth_key = jax.random.split(key, 4)
    base_len = jax.random.randint(first_key, (WINDOWS,), LEN * 11 // 16, LEN + 1)
    long_len = jax.random.randint(second_key, (WINDOWS,), LEN - LEN // 16 + 1, LEN + 1)
    chosen = jax.random.randint(third_key, (WINDOWS // WIN_DEV,), 0, WIN_DEV)
    slot_index = jnp.arange(WINDOWS) % WIN_DEV
    is_long = slot_index == jnp.repeat(chosen, WIN_DEV)
    picked = jnp.where(is_long, long_len, base_len)
    full_window = jax.random.randint(fourth_key, (), 0, WINDOWS)
    return jnp.where(jnp.arange(WINDOWS) == full_window, LEN, picked).astype(jnp.int32)


def block_scale(rng, extent, shards, low, high):
    gain, own = 1.0, jax.random.fold_in(rng, 6)
    for axis_at, parts in shards:
        steps = jnp.exp(jax.random.uniform(jax.random.fold_in(own, axis_at), (parts,), jnp.float32, low / len(shards), high / len(shards)))
        gain = gain * jnp.repeat(steps, extent[axis_at] // parts).reshape([-1 if axis == axis_at else 1 for axis in range(len(extent))])
    return gain


def scatter_about(rng, shape, width, bound, shards=(), kind=jnp.bfloat16):
    factor_of = block_scale(rng, shape, shards, -0.22, 0.18) if shards else 1.0
    array = jax.random.normal(rng, shape, jnp.float32) * width * factor_of
    return jnp.minimum(jnp.maximum(array, -bound), bound).astype(kind)


def setup_inputs(seed: int = 0) -> dict:
    streams_of = jax.random.split(jax.random.key(seed), 15)
    tokens = scatter_about(streams_of[0], (WINDOWS, LEN, D), 1.0, 6.0, ((0, 8), (1, 16)))
    lengths = draw_lengths(jax.random.fold_in(streams_of[14], 71), 0)
    norm1_gain = jnp.clip(1.0 + 0.18 * jax.random.normal(streams_of[2], (D,), jnp.float32), 0.099609375, 1.8984375).astype(jnp.bfloat16)
    norm1_bias = scatter_about(streams_of[3], (D,), 0.3, 2.0, ((0, 128),))
    w_query = scatter_about(streams_of[4], (D, D), (D // 2) ** -0.5, 0.375, ((0, 128),))
    w_key = scatter_about(streams_of[5], (D, D), (D // 2) ** -0.5, 0.375, ((0, 128),))
    w_value = scatter_about(streams_of[6], (D, D), D ** -0.5, 0.25, ((0, 128),))
    w_output = scatter_about(streams_of[7], (D, D), (D // 32) ** -0.5, 1.5, ((0, 128),))
    norm2_gain = jnp.clip(1.0 + 0.18 * jax.random.normal(streams_of[8], (D,), jnp.float32), 0.099609375, 1.8984375).astype(jnp.bfloat16)
    norm2_bias = scatter_about(streams_of[9], (D,), 0.3, 2.0, ((0, 128),))
    w_gate = scatter_about(streams_of[10], (D, FF), D ** -0.5, 0.25, ((0, 128),))
    w_up = scatter_about(streams_of[11], (D, FF), D ** -0.5, 0.25, ((0, 128),))
    w_down = scatter_about(streams_of[12], (FF, D), (FF // 4) ** -0.5, 0.25, ((0, 128),))
    cotangent = scatter_about(streams_of[13], (WINDOWS, LEN, D), 1.0, 6.0, ((0, 8), (1, 16)))
    return {"tokens": tokens, "lengths": lengths, "norm1_gain": norm1_gain, "norm1_bias": norm1_bias, "w_query": w_query, "w_key": w_key, "w_value": w_value, "w_output": w_output, "norm2_gain": norm2_gain, "norm2_bias": norm2_bias, "w_gate": w_gate, "w_up": w_up, "w_down": w_down, "cotangent": cotangent}


@jax.custom_vjp
def low(v):
    return lax.optimization_barrier(v.astype(jnp.bfloat16)).astype(jnp.float32)

@jax.custom_vjp
def low_back(v):
    return v

def low_keep(v):
    return (low(v), None)

def low_pass(kept, grad):
    return (grad,)

def back_keep(v):
    return (v, None)

def back_low(kept, grad):
    return (low(grad),)
low.defvjp(low_keep, low_pass)
low_back.defvjp(back_keep, back_low)
eps_norm = 1e-05
masked_score = -1000000000.0
highest = lax.Precision.HIGHEST

def matmul(left, right):
    return jnp.dot(left, right, precision=highest, preferred_element_type=jnp.float32)

def layer_norm(values, norm_gain, norm_bias):
    row_mean = lax.optimization_barrier(jnp.mean(values, -1, keepdims=True))
    centered = values - row_mean
    variance = lax.optimization_barrier(jnp.mean(centered * centered, -1, keepdims=True))
    return centered * lax.rsqrt(variance + eps_norm) * norm_gain + norm_bias

def rotate(values, positions, sign_value):
    half_size = HEAD // 2
    frequency = 10000.0 ** (-2.0 * jnp.arange(half_size, dtype=jnp.float32) / HEAD)
    angles = positions.astype(jnp.float32)[:, None] * frequency[None, :]
    cosine = jnp.cos(angles)[:, None, :]
    sine_part = sign_value * jnp.sin(angles)[:, None, :]
    shaped = values.reshape(values.shape[0], -1, HEAD)
    first_half = shaped[..., :half_size]
    second_half = shaped[..., half_size:]
    turned = jnp.concatenate([first_half * cosine - second_half * sine_part, second_half * cosine + first_half * sine_part], -1)
    return turned.reshape(values.shape)

def window_forward(tokens_w, length, params):
    norm1_gain, norm1_bias, w_query, w_key, w_value, w_output, norm2_gain, norm2_bias, w_gate, w_up, w_down = params
    positions = jnp.arange(LEN)
    normed = low(layer_norm(tokens_w, norm1_gain, norm1_bias))
    queries = low(rotate(low_back(matmul(normed, w_query)), positions, 1.0))
    keys_all = low(rotate(low_back(matmul(normed, w_key)), positions, 1.0))
    values_all = low(low_back(matmul(normed, w_value)))
    key_heads = keys_all.reshape(LEN, HEADS, HEAD)
    value_heads = values_all.reshape(LEN, HEADS, HEAD)
    keep_keys = positions < length
    block_rows = math.gcd(512, LEN)

    def attend_block(query_block):
        query_heads = query_block.reshape(block_rows, HEADS, HEAD)
        scores = jnp.einsum('qhd,khd->hqk', query_heads, key_heads, precision=highest) * HEAD ** (-0.5)
        scores = low_back(jnp.where(keep_keys[None, None, :], scores, masked_score))
        row_max = lax.optimization_barrier(jnp.max(scores, -1, keepdims=True))
        weights = jnp.exp(scores - row_max)
        soft_weights = weights / lax.optimization_barrier(jnp.sum(weights, -1, keepdims=True))
        mixed_rows = jnp.einsum('hqk,khd->qhd', low(soft_weights), value_heads, precision=highest)
        return mixed_rows.reshape(block_rows, HEADS * HEAD)
    attended = lax.map(jax.checkpoint(attend_block), queries.reshape(LEN // block_rows, block_rows, HEADS * HEAD))
    attended = attended.reshape(LEN, HEADS * HEAD)
    branch = low_back(matmul(low(low_back(attended)), w_output))
    middle = tokens_w + branch
    second_normed = low(layer_norm(middle, norm2_gain, norm2_bias))
    gate_lin = low_back(matmul(second_normed, w_gate))
    up_lin = low_back(matmul(second_normed, w_up))
    hidden = low(gate_lin * jax.nn.sigmoid(gate_lin) * up_lin)
    return (middle + matmul(hidden, w_down)) * keep_keys.astype(jnp.float32)[:, None]

def reference(tokens, lengths, norm1_gain, norm1_bias, w_query, w_key, w_value, w_output, norm2_gain, norm2_bias, w_gate, w_up, w_down, cotangent):
    params = tuple((item_param.astype(jnp.float32) for item_param in (norm1_gain, norm1_bias, w_query, w_key, w_value, w_output, norm2_gain, norm2_bias, w_gate, w_up, w_down)))

    def window_step(summed, window_inputs):
        tokens_w, length, cot_w = window_inputs

        def forward_of(tokens_f, params_f):
            return window_forward(tokens_f, length, params_f)
        result, pullback = jax.vjp(forward_of, tokens_w.astype(jnp.float32), params)
        grad_tokens, grad_params = pullback(cot_w.astype(jnp.float32))
        summed = jax.tree.map(lambda left, right: left + right, summed, grad_params)
        return (summed, (result.astype(jnp.bfloat16), grad_tokens))
    zero_grads = tuple((jnp.zeros_like(item_param) for item_param in params))
    summed, (layer_output, grad_tokens) = lax.scan(window_step, zero_grads, (tokens, lengths, cotangent))
    return (layer_output, grad_tokens) + tuple(summed)
```

```python
import math

import jax
import jax.numpy as jnp
import numpy as np
from jax import lax
from jax.experimental import pallas as pl
from jax.experimental.pallas import tpu as pltpu
from jax.sharding import PartitionSpec as P

HEADS = 16
HEAD = 32
HALF = HEAD // 2
D = 512
FF = 2048
LEN = 2048
ROWS = 128
TEAM = 4
TEAM_ROWS = TEAM * ROWS
FF_PART = FF // TEAM
DEVICES = 128
SEQ = 16
DP = 8
AUG = 48

EPS = 1e-05
MASKED = -1.0e9
SCALE = HEAD**-0.5
LOG2E = math.log2(math.e)
LN2 = math.log(2.0)

f32 = jnp.float32
bf16 = jnp.bfloat16
BOTH = ("dp", "seq")


def nn(a, b):
    return lax.dot_general(a, b, (((1,), (0,)), ((), ())), preferred_element_type=f32)


def nt(a, b):
    return lax.dot_general(a, b, (((1,), (1,)), ((), ())), preferred_element_type=f32)


def tn(a, b):
    return lax.dot_general(a, b, (((0,), (0,)), ((), ())), preferred_element_type=f32)


def norm_parts(x):
    centered = x - jnp.mean(x, -1, keepdims=True)
    inv = lax.rsqrt(jnp.mean(centered * centered, -1, keepdims=True) + EPS)
    return centered * inv, inv


def norm_back(grad, scaled, inv, gain):
    e = grad * gain
    return inv * (
        e - jnp.mean(e, -1, keepdims=True) - scaled * jnp.mean(e * scaled, -1, keepdims=True)
    )


def split3(row):
    hi = row.astype(bf16)
    rest = row - hi.astype(f32)
    mid = rest.astype(bf16)
    low = (rest - mid.astype(f32)).astype(bf16)
    return [hi.astype(f32), mid.astype(f32), low.astype(f32)]


def key_columns(keys_t, length):
    place = lax.broadcasted_iota(jnp.int32, (1, LEN), 1)
    mask = jnp.where(place < length, 0.0, MASKED).astype(f32)
    ones = jnp.ones((3, LEN), f32)
    pad = jnp.zeros((128 - HEAD - 4, LEN), f32)
    return jnp.concatenate([keys_t, mask, ones, pad], 0).T.astype(bf16)[:, :AUG]


def with_rows(data_t, rows):
    pad = jnp.zeros((AUG - HEAD - len(rows), data_t.shape[1]), f32)
    return jnp.concatenate([data_t.astype(f32)] + rows + [pad], 0).astype(bf16)


def attend_kernel(
    place, length, near, far, head_cols, cos, sin,
    sent, q_out, k_out, v_out, o_out, lse_out, team_tokens,
    q_t, k_t, v_t,
):
    core = place[0]
    team = place[1]
    cols = head_cols[...].astype(f32).T
    gain = cols[96:97, :]
    bias = cols[97:98, :]
    weights_t = cols[0:96, :].astype(bf16)
    for which, source in ((0, near), (1, far)):
        parity = core if which == 0 else 1 - core
        for pair in range(4):
            x = source[2 * pair : 2 * pair + 2].reshape(2 * ROWS, D).astype(f32)
            scaled, _ = norm_parts(x)
            normed = (scaled * gain + bias).astype(bf16)
            lin = nt(weights_t, normed)
            for one in range(2):
                at = pl.multiple_of((2 * (2 * pair + one) + parity) * ROWS, ROWS)
                here = pl.ds(at, ROWS)
                part = lin[:, one * ROWS : (one + 1) * ROWS]
                c = cos[:, here]
                s = sin[:, here]
                q1, q2 = part[0:16], part[16:32]
                k1, k2 = part[32:48], part[48:64]
                fold = SCALE * LOG2E
                q_t[:, here] = (
                    jnp.concatenate([q1 * c - q2 * s, q2 * c + q1 * s], 0) * fold
                ).astype(bf16)
                k_t[:, here] = jnp.concatenate([k1 * c - k2 * s, k2 * c + k1 * s], 0).astype(bf16)
                v_t[:, here] = part[64:96].astype(bf16)
        for one in range(2):
            team_tokens[2 * one + parity] = source[2 * team + one]
    q_out[...] = q_t[...]
    k_out[...] = k_t[...]
    v_out[...] = v_t[...]
    keys = key_columns(k_t[...].astype(f32), length[0])
    one_row = jnp.ones((1, LEN), f32)
    values_t = with_rows(v_t[...], [one_row])
    tile = TEAM_ROWS
    for i in range(LEN // tile):
        here = slice(i * tile, (i + 1) * tile)
        queries_t = with_rows(q_t[:, here], [jnp.ones((1, tile), f32)])
        scores = nn(keys, queries_t)
        top = jnp.max(scores, axis=0, keepdims=True)
        weights = jnp.exp2(scores - top).astype(bf16)
        mixed = nn(values_t, weights)
        total = mixed[HEAD : HEAD + 1]
        out = mixed[:HEAD] / total
        o_out[:, here] = out
        lse_out[:, here] = top + jnp.log2(total)
        low = out.astype(bf16)
        for t in range(TEAM):
            sent[TEAM * i + t] = low


def feed_kernel(place, length, mixed, tokens, cot, weights, head_cols, sent, swapped, grads, norm_rows):
    team = place[1]
    member = place[2]
    cols = head_cols[...].astype(f32).T
    gain = cols[98:99, :]
    bias = cols[99:100, :]
    w_gate = weights[:, 0:512]
    w_up = weights[:, 512:1024]
    w_down = weights[:, 1024:1536]
    w_out = weights[:, 1536:2048]
    mixed_t = mixed[...].reshape(D, TEAM_ROWS)
    row = lax.broadcasted_iota(jnp.int32, (TEAM_ROWS, 1), 0)
    live = (team * TEAM_ROWS + row) < length[0]
    own = (row // ROWS) == member
    middle = tokens[...].reshape(TEAM_ROWS, D).astype(f32) + tn(mixed_t, w_out)
    scaled, inv = norm_parts(middle)
    normed = (scaled * gain + bias).astype(bf16)
    gate = nn(normed, w_gate)
    up = nn(normed, w_up)
    sig = jax.nn.sigmoid(gate)
    act = gate * sig
    hidden = (act * up).astype(bf16)
    out_part = nn(hidden, w_down) + jnp.where(own, middle, 0.0)
    d_out = jnp.where(live, cot[...].reshape(TEAM_ROWS, D).astype(f32), 0.0)
    d_out_low = d_out.astype(bf16)
    d_hidden = nt(d_out_low, w_down)
    d_up = (d_hidden * act).astype(bf16)
    d_gate = (d_hidden * up * sig * (1.0 + gate * (1.0 - sig))).astype(bf16)
    d_normed = nt(d_gate, w_gate) + nt(d_up, w_up)
    d_middle = jnp.where(own, d_out, 0.0) + norm_back(d_normed, scaled, inv, gain)
    d_middle_low = d_middle.astype(bf16)
    sent[...] = nt(w_out, d_middle_low).astype(bf16).reshape(HEADS, HEAD, TEAM_ROWS)
    swapped[:, :, 0:D] = d_middle_low.reshape(TEAM, ROWS, D)
    swapped[:, :, D : 2 * D] = out_part.astype(bf16).reshape(TEAM, ROWS, D)
    grads[:, 0:512] = tn(normed, d_gate).astype(bf16)
    grads[:, 512:1024] = tn(normed, d_up).astype(bf16)
    grads[:, 1024:1536] = tn(hidden, d_out_low).astype(bf16)
    grads[:, 1536:2048] = nn(mixed_t, d_middle_low).astype(bf16)
    norm_rows[0:1, :] = jnp.sum(d_normed * scaled, 0, keepdims=True)
    norm_rows[1:2, :] = jnp.sum(d_normed, 0, keepdims=True)
    norm_rows[2:8, :] = jnp.zeros((6, D), f32)


def attend_back_kernel(
    length, d_mixed, q_in, k_in, v_in, o_in, lse_in, cos, sin, sent, d_o, probs, d_scores, dq, dk, dv
):
    for y in range(LEN // TEAM_ROWS):
        total = d_mixed[TEAM * y].astype(f32)
        for t in range(1, TEAM):
            total = total + d_mixed[TEAM * y + t].astype(f32)
        d_o[:, y * TEAM_ROWS : (y + 1) * TEAM_ROWS] = total.astype(bf16)
    keys_t = k_in[...]
    keys = key_columns(keys_t.astype(f32), length[0])
    ones = jnp.ones((4, LEN), f32)
    pad = jnp.zeros((128 - HEAD - 4, LEN), f32)
    values = jnp.concatenate([v_in[...].astype(f32), ones, pad], 0).T.astype(bf16)[:, :AUG]
    d_o_t = d_o[...]
    inner = jnp.sum(d_o_t.astype(f32) * o_in[...], 0, keepdims=True)
    zero_row = jnp.zeros((1, LEN), f32)
    one_row = jnp.ones((1, LEN), f32)
    q_rows = with_rows(q_in[...], [one_row] + split3(-lse_in[...]))
    do_rows = with_rows(d_o_t, [zero_row] + split3(-inner))
    tile = 512
    for i in range(LEN // tile):
        here = slice(i * tile, (i + 1) * tile)
        p = jnp.exp2(nn(keys, q_rows[:, here]))
        ds = (p * nn(values, do_rows[:, here])).astype(bf16)
        probs[:, here] = p.astype(bf16)
        d_scores[:, here] = ds
        dq[:, here] = nn(keys_t, ds) * SCALE
    dk[...] = nt(q_in[...], d_scores[...]) * LN2
    dv[...] = nt(d_o_t, probs[...])
    c = cos[...]
    s = sin[...]
    q1, q2 = dq[0:HALF], dq[HALF:HEAD]
    k1, k2 = dk[0:HALF], dk[HALF:HEAD]
    dq_t = jnp.concatenate([q1 * c + q2 * s, q2 * c - q1 * s], 0).astype(bf16)
    dk_t = jnp.concatenate([k1 * c + k2 * s, k2 * c - k1 * s], 0).astype(bf16)
    dv_t = dv[...].astype(bf16)
    for b in range(SEQ):
        here = slice(b * ROWS, (b + 1) * ROWS)
        sent[b, 0:32] = dq_t[:, here]
        sent[b, 32:64] = dk_t[:, here]
        sent[b, 64:96] = dv_t[:, here]


def head_grad_kernel(place, near, far, head_cols, d_lin, norm_rows, sent):
    core = place[0]
    cols = head_cols[...].astype(f32).T
    gain = cols[96:97, :]
    bias = cols[97:98, :]
    weights_t = cols[0:96, :].astype(bf16)
    total = jnp.zeros((96, D), f32)
    d_gain = jnp.zeros((1, D), f32)
    d_bias = jnp.zeros((1, D), f32)
    for which, source in ((0, near), (1, far)):
        parity = core if which == 0 else 1 - core
        for pair in range(4):
            x = source[2 * pair : 2 * pair + 2].reshape(2 * ROWS, D).astype(f32)
            scaled, _ = norm_parts(x)
            normed = (scaled * gain + bias).astype(bf16)
            d_part = jnp.concatenate(
                [d_lin[2 * (2 * pair) + parity], d_lin[2 * (2 * pair + 1) + parity]], 1
            )
            total = total + nn(d_part, normed)
            d_normed = tn(d_part, weights_t)
            d_gain = d_gain + jnp.sum(d_normed * scaled, 0, keepdims=True)
            d_bias = d_bias + jnp.sum(d_normed, 0, keepdims=True)
    pad = jnp.zeros((28, D), f32)
    sent[...] = jnp.concatenate([total, d_gain, d_bias, norm_rows[0:2, :], pad], 0).T


def input_grad_kernel(place, length, tokens, d_lin, weights, swapped, head_cols, grad_tokens, layer_output):
    seq = place[3]
    cols = head_cols[...].astype(f32).T
    gain = cols[96:97, :]
    scaled, inv = norm_parts(tokens[0].astype(f32))
    d_t = jnp.zeros((D, ROWS), f32)
    for part in range(3):
        d_part = d_lin[:, part * HEAD : (part + 1) * HEAD, :].reshape(D, ROWS)
        d_t = d_t + nn(weights[:, part * D : (part + 1) * D], d_part)
    total = swapped[0].astype(f32)
    for t in range(1, TEAM):
        total = total + swapped[t].astype(f32)
    grad_tokens[0] = total[:, 0:D] + norm_back(d_t.T, scaled, inv, gain)
    row = lax.broadcasted_iota(jnp.int32, (ROWS, 1), 0)
    live = (seq * ROWS + row) < length[0]
    layer_output[0] = jnp.where(live, total[:, D : 2 * D], 0.0).astype(bf16)


VM = pl.BlockSpec(memory_space=pltpu.VMEM)
SM = pl.BlockSpec(memory_space=pltpu.SMEM)


def call(kernel, specs, outs, scratch=(), flops=0, size=0):
    return pl.pallas_call(
        kernel,
        out_shape=tuple(jax.ShapeDtypeStruct(shape, kind) for shape, kind in outs),
        in_specs=specs,
        out_specs=tuple(VM for _ in outs),
        scratch_shapes=[pltpu.VMEM(shape, kind) for shape, kind in scratch],
        compiler_params=pltpu.CompilerParams(vmem_limit_bytes=56 * 2**20),
        cost_estimate=pl.CostEstimate(flops=flops, bytes_accessed=size, transcendentals=0),
    )


def rope_tables():
    freq = 10000.0 ** (-2.0 * np.arange(HALF) / HEAD)
    angles = freq[:, None] * np.arange(LEN)[None, :]
    return np.cos(angles).astype(np.float32), np.sin(angles).astype(np.float32)


def column_order():
    order = np.arange(512).reshape(4, 8, TEAM, 4).transpose(2, 0, 1, 3).reshape(-1)
    table = np.zeros((512, 512), np.float32)
    table[order, np.arange(512)] = 1.0
    return table


def exchange(value, axes, groups=None):
    return lax.all_to_all(value, axes, 0, 0, tiled=True, axis_index_groups=groups)


def shards(
    tokens, lengths, norm1_gain, norm1_bias, w_query, w_key, w_value, w_output,
    norm2_gain, norm2_bias, w_gate, w_up, w_down, cotangent,
):
    seq = lax.axis_index("seq")
    place = jnp.stack([seq % 2, seq // TEAM, seq % TEAM, seq]).astype(jnp.int32)
    cos, sin = (jnp.asarray(t) for t in rope_tables())
    order = column_order()

    same_core = [[2 * chip + core for chip in range(8)] for core in range(2)]
    near = exchange(jnp.broadcast_to(tokens, (8, ROWS, D)), "seq", same_core)
    far = lax.ppermute(near, "seq", [(i, i ^ 1) for i in range(SEQ)])

    by_head = [w.reshape(4, HEADS, HEAD).transpose(1, 0, 2) for w in (w_query, w_key, w_value)]
    norms = jnp.stack([norm1_gain, norm1_bias, norm2_gain, norm2_bias], 1)
    norms = jnp.broadcast_to(norms[None], (HEADS, 4, 4))
    pad = jnp.zeros((HEADS, 4, 28), bf16)
    head_msg = jnp.concatenate(by_head + [norms, pad], 2)
    head_msg = jnp.broadcast_to(head_msg[None], (DP, HEADS, 4, 128)).reshape(DEVICES, 4, 128)
    head_cols = exchange(head_msg, BOTH).reshape(D, 128)

    wide = jnp.concatenate([w_gate, w_up], 0).reshape(2 * 4 * 4, 512)
    wide = jnp.dot(wide, jnp.asarray(order, bf16), preferred_element_type=f32).astype(bf16)
    wide = wide.reshape(2, 4, 4, TEAM, 128).transpose(3, 1, 0, 2, 4).reshape(TEAM, 4, 1024)
    down = w_down.reshape(TEAM, 4, D)
    out = jnp.broadcast_to(w_output[None], (TEAM, 4, D))
    feed_msg = jnp.concatenate([wide, down, out], 2)
    feed_msg = jnp.broadcast_to(feed_msg[None], (DEVICES // TEAM, TEAM, 4, 2048))
    feed_weights = exchange(feed_msg.reshape(DEVICES, 4, 2048), BOTH).reshape(D, 2048)

    teams = [[TEAM * j + t for t in range(TEAM)] for j in range(SEQ // TEAM)]
    team_cot = exchange(jnp.broadcast_to(cotangent, (TEAM, ROWS, D)), "seq", teams)

    sent, q_t, k_t, v_t, o_t, lse, team_tokens = call(
        attend_kernel,
        [SM, SM] + [VM] * 5,
        [
            ((SEQ, HEAD, TEAM_ROWS), bf16),
            ((HEAD, LEN), bf16),
            ((HEAD, LEN), bf16),
            ((HEAD, LEN), bf16),
            ((HEAD, LEN), f32),
            ((1, LEN), f32),
            ((TEAM, ROWS, D), bf16),
        ],
        [((HEAD, LEN), bf16)] * 3,
        flops=8 * 10**9,
        size=8 * 10**6,
    )(place, lengths, near, far, head_cols, cos, sin)
    mixed = exchange(sent, "seq")

    rows_msg = jnp.concatenate([w_query, w_key, w_value], 1)
    rows_msg = jnp.broadcast_to(rows_msg[None], (DEVICES, 4, 3 * D))
    row_weights = exchange(rows_msg, BOTH).reshape(D, 3 * D)

    d_sent, swapped, grads, norm_rows = call(
        feed_kernel,
        [SM, SM] + [VM] * 5,
        [
            ((HEADS, HEAD, TEAM_ROWS), bf16),
            ((TEAM, ROWS, 2 * D), bf16),
            ((D, 2048), bf16),
            ((8, D), f32),
        ],
        flops=4 * 10**9,
        size=10 * 10**6,
    )(place, lengths, mixed, team_tokens, team_cot, feed_weights, head_cols)
    d_mixed = exchange(d_sent, "seq")
    feed_grads = exchange(grads.reshape(DEVICES, 4, 2048), BOTH)
    swapped = exchange(swapped, "seq", teams)

    (lin_sent,) = call(
        attend_back_kernel,
        [SM] + [VM] * 8,
        [((SEQ, 96, ROWS), bf16)],
        [
            ((HEAD, LEN), bf16),
            ((LEN, LEN), bf16),
            ((LEN, LEN), bf16),
            ((HEAD, LEN), f32),
            ((HEAD, LEN), f32),
            ((HEAD, LEN), f32),
        ],
        flops=12 * 10**9,
        size=8 * 10**6,
    )(lengths, d_mixed, q_t, k_t, v_t, o_t, lse, cos, sin)
    d_lin = exchange(lin_sent, "seq")

    (head_grads,) = call(
        head_grad_kernel,
        [SM] + [VM] * 5,
        [((D, 128), f32)],
        flops=2 * 10**9,
        size=5 * 10**6,
    )(place, near, far, head_cols, lin_sent, norm_rows)
    head_grads = exchange(head_grads.reshape(DEVICES, 4, 128), BOTH)

    grad_tokens, layer_output = call(
        input_grad_kernel,
        [SM, SM] + [VM] * 5,
        [((1, ROWS, D), f32), ((1, ROWS, D), bf16)],
        flops=10**9,
        size=4 * 10**6,
    )(place, lengths, tokens, d_lin, row_weights, swapped, head_cols)

    summed = jnp.sum(feed_grads.reshape(DEVICES // TEAM, TEAM, 4, 2048).astype(f32), 0)
    grad_output = jnp.sum(summed[:, :, 1536:], 0)
    grad_down = summed[:, :, 1024:1536].reshape(16, D)
    wide = summed[:, :, :1024].reshape(TEAM, 4, 2, 4, 128).transpose(2, 1, 3, 0, 4)
    wide = jnp.dot(
        wide.reshape(2 * 4 * 4, 512),
        jnp.asarray(order.T),
        precision=lax.Precision.HIGHEST,
        preferred_element_type=f32,
    ).reshape(2, 4, FF)
    per_head = jnp.sum(head_grads.reshape(DP, HEADS, 4, 128), 0)
    grad_query, grad_key, grad_value = (
        per_head[:, :, i * HEAD : (i + 1) * HEAD].transpose(1, 0, 2).reshape(4, D) for i in range(3)
    )
    norm_grads = jnp.sum(per_head[:, :, 96:100], 0)
    return (
        layer_output,
        grad_tokens,
        norm_grads[:, 0],
        norm_grads[:, 1],
        grad_query,
        grad_key,
        grad_value,
        grad_output,
        norm_grads[:, 2],
        norm_grads[:, 3],
        wide[0],
        wide[1],
        grad_down,
    )


def solution(mesh):
    flat = P(BOTH)
    rows = P(BOTH, None)
    blocks = P("dp", "seq", None)
    return jax.shard_map(
        shards,
        mesh=mesh,
        in_specs=(
            blocks, P("dp"), flat, flat, rows, rows, rows, rows, flat, flat, rows, rows, rows, blocks,
        ),
        out_specs=(
            blocks, blocks, flat, flat, rows, rows, rows, rows, flat, flat, rows, rows, rows,
        ),
        check_vma=False,
    )
```

```python
import math

import jax
import jax.numpy as jnp
import numpy as np
from jax import lax
from jax.experimental import pallas as pl
from jax.experimental.pallas import tpu as pltpu
from jax.sharding import Mesh
from jax.sharding import PartitionSpec as P

HEADS = 16
HEAD = 32
HALF = HEAD // 2
D = 512
FF = 2048
LEN = 2048
ROWS = 128
TEAM = 4
TEAM_ROWS = TEAM * ROWS
FF_PART = FF // TEAM
DEVICES = 128
SEQ = 16
DP = 8
AUG = 48

EPS = 1e-05
MASKED = -1.0e9
SCALE = HEAD**-0.5
LOG2E = math.log2(math.e)
LN2 = math.log(2.0)

f32 = jnp.float32
bf16 = jnp.bfloat16
WINDOW = ("y", "z", "core")
CHIPS = ("y", "z")
SLICE = ("z_lo", "y", "z", "core")
ALL = ("z_lo", "x", "y", "z", "core")


def nn(a, b):
    return lax.dot_general(a, b, (((1,), (0,)), ((), ())), preferred_element_type=f32)


def nt(a, b):
    return lax.dot_general(a, b, (((1,), (1,)), ((), ())), preferred_element_type=f32)


def tn(a, b):
    return lax.dot_general(a, b, (((0,), (0,)), ((), ())), preferred_element_type=f32)


def norm_parts(x):
    centered = x - jnp.mean(x, -1, keepdims=True)
    inv = lax.rsqrt(jnp.mean(centered * centered, -1, keepdims=True) + EPS)
    return centered * inv, inv


def norm_back(grad, scaled, inv, gain):
    e = grad * gain
    return inv * (
        e - jnp.mean(e, -1, keepdims=True) - scaled * jnp.mean(e * scaled, -1, keepdims=True)
    )


def split3(row):
    hi = row.astype(bf16)
    rest = row - hi.astype(f32)
    mid = rest.astype(bf16)
    low = (rest - mid.astype(f32)).astype(bf16)
    return [hi.astype(f32), mid.astype(f32), low.astype(f32)]


def key_columns(keys_t, length):
    place = lax.broadcasted_iota(jnp.int32, (1, LEN), 1)
    mask = jnp.where(place < length, 0.0, MASKED).astype(f32)
    ones = jnp.ones((3, LEN), f32)
    pad = jnp.zeros((128 - HEAD - 4, LEN), f32)
    return jnp.concatenate([keys_t, mask, ones, pad], 0).T.astype(bf16)[:, :AUG]


def with_rows(data_t, rows):
    pad = jnp.zeros((AUG - HEAD - len(rows), data_t.shape[1]), f32)
    return jnp.concatenate([data_t.astype(f32)] + rows + [pad], 0).astype(bf16)


def after(value, *others):
    def kernel(*refs):
        pass

    return pl.pallas_call(
        kernel,
        out_shape=jax.ShapeDtypeStruct(value.shape, value.dtype),
        in_specs=[pl.BlockSpec(memory_space=pl.ANY)] * (1 + len(others)),
        out_specs=pl.BlockSpec(memory_space=pl.ANY),
        input_output_aliases={0: 0},
    )(value, *others)


def copy_after(value, other):
    def kernel(value_ref, other_ref, out_ref):
        out_ref[...] = value_ref[...]

    return call(kernel, [VM, HBM], [(value.shape, value.dtype)])(value, other)[0]


FEED_LANES = FF_PART * 3 + D
GRAD_LANES = FEED_LANES + 128
MSG_ROWS = ROWS + 48


def pack_kernel(
    tokens, w_query, w_key, w_value, w_output, w_gate, w_up, w_down, gain1, bias1, gain2, bias2,
    order, sent,
):
    narrow = [w[...].astype(f32) for w in (w_query, w_key, w_value)]
    gate = w_gate[...].astype(f32)
    up = w_up[...].astype(f32)
    down = w_down[...].astype(f32)
    pieces = []
    for u in range(4):
        here = slice(512 * u, 512 * (u + 1))
        pieces.append(jnp.concatenate([gate[:, here], up[:, here]], 0))
    wide = nn(jnp.concatenate(pieces, 0).astype(bf16), order[...])
    lane = lax.broadcasted_iota(jnp.int32, (4, 128), 1)
    row = lax.broadcasted_iota(jnp.int32, (4, 128), 0)
    norms = jnp.zeros((4, 128), f32)
    for n, ref in enumerate((gain1, bias1, gain2, bias2)):
        for i in range(4):
            value = ref[i : i + 1].astype(f32).reshape(1, 1)
            norms = norms + jnp.where((lane == 96 + n) & (row == i), value, 0.0)
    out = w_output[...].astype(f32)
    nothing = jnp.zeros((4, 512), f32)
    for z in range(2):
        mine = []
        for t in (2 * z, 2 * z + 1):
            cols = slice(128 * t, 128 * (t + 1))
            mine.append(jnp.concatenate([wide[8 * u : 8 * u + 4, cols] for u in range(4)], 1))
            mine.append(jnp.concatenate([wide[8 * u + 4 : 8 * u + 8, cols] for u in range(4)], 1))
            mine.append(down[4 * t : 4 * t + 4])
        mine = jnp.concatenate(mine + [out] + narrow, 0)
        for y in range(4):
            tile = slice(128 * y, 128 * (y + 1))
            heads = []
            for t in (2 * z, 2 * z + 1):
                q, k, v = (
                    pltpu.roll(w[:, tile], (HEAD * (i - t)) % 128, 1)
                    for i, w in enumerate(narrow)
                )
                heads.append(
                    jnp.where(
                        lane < 32, q, jnp.where(lane < 64, k, jnp.where(lane < 96, v, norms))
                    )
                )
            heads = jnp.concatenate(heads + [nothing[:, :256]], 1)
            low = jnp.concatenate([mine, heads, nothing], 0).astype(bf16)
            sent[2 * y + z, 0:ROWS, :] = tokens[0]
            sent[2 * y + z, ROWS:, :] = low


def unpack_kernel(place, near, far, cot, feed, head, whole, rows, arrived):
    loads = [
        pltpu.make_async_copy(source.at[:, ROWS:, :], rows.at[i], arrived.at[i])
        for i, source in enumerate((near, far))
    ]
    for load in loads:
        load.start()
    for load in loads:
        load.wait()
    second = place[0] == 1
    for group in range(4):
        blocks = []
        for chip in (2 * group, 2 * group + 1):
            own = rows[0, chip].astype(f32)
            other = rows[1, chip].astype(f32)
            blocks += [jnp.where(second, other, own), jnp.where(second, own, other)]
        here = slice(16 * group, 16 * (group + 1))
        for i in range(3):
            cols = jnp.concatenate(
                [
                    jnp.where(second, b[4 * (i + 3) : 4 * (i + 4)], b[4 * i : 4 * (i + 1)])
                    for b in blocks
                ],
                0,
            )
            feed[0, here, D * i : D * (i + 1)] = cols.astype(bf16)
        for i in range(4):
            cols = jnp.concatenate([b[4 * (i + 6) : 4 * (i + 7)] for b in blocks], 0).astype(bf16)
            if i == 0:
                feed[0, here, 3 * D : 4 * D] = cols
            else:
                whole[0, here, D * (i - 1) : D * i] = cols
        cols = jnp.concatenate(
            [jnp.where(second, b[40:44, 128:256], b[40:44, 0:128]) for b in blocks], 0
        )
        head[0, here, :] = cols.astype(bf16)


def block_of(place, chip, other):
    return 2 * chip + (place[0] ^ other)


def attend_kernel(
    place, length, near, far, h0, h1, h2, h3, h4, h5, h6, h7, cos, sin,
    sent, q_out, k_out, v_out, o_out, lse_out, cols_out,
    q_t, k_t, v_t, head_cols,
):
    for step, head in enumerate((h0, h1, h2, h3, h4, h5, h6, h7)):
        k, by = step // 4, step % 4
        head_cols[(place[5] ^ k) * 4 + lax.rem(place[4] + 4 - by, 4)] = head[0]
    cols = head_cols[...].reshape(D, 128).astype(f32).T
    cols_out[...] = cols
    gain = cols[96:97, :]
    bias = cols[97:98, :]
    weights_t = cols[0:96, :].astype(bf16)
    for index in range(8):
        source, first = (near, far)[index // 4], 2 * (index % 4)
        x = source[first : first + 2, 0:ROWS, :].reshape(2 * ROWS, D).astype(f32)
        scaled, _ = norm_parts(x)
        normed = (scaled * gain + bias).astype(bf16)
        lin = nt(weights_t, normed)
        for one in range(2):
            block = block_of(place, first + one, index // 4)
            here = pl.ds(pl.multiple_of(block * ROWS, ROWS), ROWS)
            part = lin[:, one * ROWS : (one + 1) * ROWS]
            c = cos[:, here]
            s = sin[:, here]
            q1, q2 = part[0:16], part[16:32]
            k1, k2 = part[32:48], part[48:64]
            fold = SCALE * LOG2E
            q_t[:, here] = (
                jnp.concatenate([q1 * c - q2 * s, q2 * c + q1 * s], 0) * fold
            ).astype(bf16)
            k_t[:, here] = jnp.concatenate([k1 * c - k2 * s, k2 * c + k1 * s], 0).astype(bf16)
            v_t[:, here] = part[64:96].astype(bf16)
    q_out[...] = q_t[...]
    k_out[...] = k_t[...]
    v_out[...] = v_t[...]
    keys = key_columns(k_t[...].astype(f32), length[0])
    one_row = jnp.ones((1, LEN), f32)
    values_t = with_rows(v_t[...], [one_row])
    tile = TEAM_ROWS
    for i in range(LEN // tile):
        here = slice(i * tile, (i + 1) * tile)
        queries_t = with_rows(q_t[:, here], [jnp.ones((1, tile), f32)])
        scores = nn(keys, queries_t)
        top = jnp.max(scores, axis=0, keepdims=True)
        weights = jnp.exp2(scores - top).astype(bf16)
        mixed = nn(values_t, weights)
        total = mixed[HEAD : HEAD + 1]
        out = mixed[:HEAD] / total
        o_out[:, here] = out
        lse_out[:, here] = top + jnp.log2(total)
        low = out.astype(bf16)
        for t in range(TEAM):
            sent[TEAM * i + t] = low


def load_part(place, weights, parts, arrived, i):
    return [
        pltpu.make_async_copy(
            weights.at[x, place[5] ^ k, :, 512 * i : 512 * (i + 1)],
            parts.at[i, k, x],
            arrived.at[8 * i + 4 * k + x],
        )
        for k in range(2)
        for x in range(4)
    ]


def finish(copies):
    for copy in copies:
        copy.wait()


def feed_kernel(
    place, length, mixed, near, far, cot_near, cot_far, weights, head_cols, other,
    sent, kept, swapped, grads, norm_rows,
    tokens, cot, back, ahead, parts, arrived, tokens_arrived,
):
    core, team, z = place[0], place[1], place[2]
    token_loads = []
    for one in range(2):
        for other, source in enumerate((near, far)):
            here = pl.ds(pl.multiple_of((2 * (z ^ one) + (core ^ other)) * ROWS, ROWS), ROWS)
            token_loads.append(
                pltpu.make_async_copy(
                    source.at[2 * team + (z ^ one), 0:ROWS, :],
                    tokens.at[here, :],
                    tokens_arrived.at[2 * one + other],
                )
            )
    for load in token_loads:
        load.start()
    member = 2 * z + core
    for one in range(2):
        here = pl.ds(pl.multiple_of((2 * (z ^ one) + core) * ROWS, ROWS), ROWS)
        there = pl.ds(pl.multiple_of((2 * (z ^ one) + 1 - core) * ROWS, ROWS), ROWS)
        cot[here, :] = cot_near[one]
        cot[there, :] = cot_far[one]
    gain = head_cols[98:99, :]
    bias = head_cols[99:100, :]
    loads = [load_part(place, weights, parts, arrived, i) for i in (3, 0, 1, 2)]
    for load in loads:
        for copy in load:
            copy.start()
    mixed_t = mixed[...].reshape(D, TEAM_ROWS)
    finish(token_loads)
    finish(loads[0])
    w_out = parts[3].reshape(D, D)
    row = lax.broadcasted_iota(jnp.int32, (TEAM_ROWS, 1), 0)
    live = (team * TEAM_ROWS + row) < length[0]
    own = (row // ROWS) == member
    middle = tokens[...].astype(f32) + tn(mixed_t, w_out)
    scaled, inv = norm_parts(middle)
    normed = (scaled * gain + bias).astype(bf16)
    finish(loads[1])
    w_gate = parts[0].reshape(D, FF_PART)
    gate = nn(normed, w_gate)
    finish(loads[2])
    w_up = parts[1].reshape(D, FF_PART)
    up = nn(normed, w_up)
    finish(loads[3])
    w_down = parts[2].reshape(FF_PART, D)
    sig = jax.nn.sigmoid(gate)
    act = gate * sig
    hidden = (act * up).astype(bf16)
    out_part = nn(hidden, w_down) + jnp.where(own, middle, 0.0)
    d_out = jnp.where(live, cot[...].astype(f32), 0.0)
    d_out_low = d_out.astype(bf16)
    d_hidden = nt(d_out_low, w_down)
    d_up = (d_hidden * act).astype(bf16)
    d_gate = (d_hidden * up * sig * (1.0 + gate * (1.0 - sig))).astype(bf16)
    d_normed = nt(d_gate, w_gate) + nt(d_up, w_up)
    d_middle = jnp.where(own, d_out, 0.0) + norm_back(d_normed, scaled, inv, gain)
    d_middle_low = d_middle.astype(bf16)
    sent[...] = nt(w_out, d_middle_low).astype(bf16).reshape(HEADS, HEAD, TEAM_ROWS)
    back[...] = d_middle_low
    ahead[...] = out_part.astype(bf16)
    for one in range(2):
        for target, other in ((kept, core), (swapped, 1 - core)):
            here = pl.ds(pl.multiple_of((2 * (z ^ one) + other) * ROWS, ROWS), ROWS)
            target[one, :, 0:D] = back[here, :]
            target[one, :, D : 2 * D] = ahead[here, :]
    for i, grad in enumerate(
        (
            tn(normed, d_gate),
            tn(normed, d_up),
            tn(hidden, d_out_low),
            nn(mixed_t, d_middle_low),
        )
    ):
        low = grad.astype(bf16)
        for k in range(2):
            for x in range(4):
                at = 64 * (4 * k + x)
                grads[x, k, :, D * i : D * (i + 1)] = low[at : at + 64]
    norm_rows[0:1, :] = jnp.sum(d_normed * scaled, 0, keepdims=True)
    norm_rows[1:2, :] = jnp.sum(d_normed, 0, keepdims=True)
    norm_rows[2:8, :] = jnp.zeros((6, D), f32)


def add_kernel(kept, arrived, own, other):
    own[...] = (kept[0].astype(f32) + arrived[0].astype(f32)).astype(bf16)
    other[...] = (kept[1].astype(f32) + arrived[1].astype(f32)).astype(bf16)


def attend_back_kernel(
    length, d_mixed, q_in, k_in, v_in, o_in, lse_in, cos, sin, sent, d_o, probs, d_scores, dq, dk, dv
):
    for y in range(LEN // TEAM_ROWS):
        total = d_mixed[TEAM * y].astype(f32)
        for t in range(1, TEAM):
            total = total + d_mixed[TEAM * y + t].astype(f32)
        d_o[:, y * TEAM_ROWS : (y + 1) * TEAM_ROWS] = total.astype(bf16)
    keys_t = k_in[...]
    keys = key_columns(keys_t.astype(f32), length[0])
    ones = jnp.ones((4, LEN), f32)
    pad = jnp.zeros((128 - HEAD - 4, LEN), f32)
    values = jnp.concatenate([v_in[...].astype(f32), ones, pad], 0).T.astype(bf16)[:, :AUG]
    d_o_t = d_o[...]
    inner = jnp.sum(d_o_t.astype(f32) * o_in[...], 0, keepdims=True)
    zero_row = jnp.zeros((1, LEN), f32)
    one_row = jnp.ones((1, LEN), f32)
    q_rows = with_rows(q_in[...], [one_row] + split3(-lse_in[...]))
    do_rows = with_rows(d_o_t, [zero_row] + split3(-inner))
    tile = 512
    for i in range(LEN // tile):
        here = slice(i * tile, (i + 1) * tile)
        p = jnp.exp2(nn(keys, q_rows[:, here]))
        ds = (p * nn(values, do_rows[:, here])).astype(bf16)
        probs[:, here] = p.astype(bf16)
        d_scores[:, here] = ds
        dq[:, here] = nn(keys_t, ds) * SCALE
    dk[...] = nt(q_in[...], d_scores[...]) * LN2
    dv[...] = nt(d_o_t, probs[...])
    c = cos[...]
    s = sin[...]
    q1, q2 = dq[0:HALF], dq[HALF:HEAD]
    k1, k2 = dk[0:HALF], dk[HALF:HEAD]
    dq_t = jnp.concatenate([q1 * c + q2 * s, q2 * c - q1 * s], 0).astype(bf16)
    dk_t = jnp.concatenate([k1 * c + k2 * s, k2 * c - k1 * s], 0).astype(bf16)
    dv_t = dv[...].astype(bf16)
    for b in range(SEQ):
        here = slice(b * ROWS, (b + 1) * ROWS)
        sent[b, 0:32] = dq_t[:, here]
        sent[b, 32:64] = dk_t[:, here]
        sent[b, 64:96] = dv_t[:, here]


def head_grad_kernel(
    near, far, head_cols, d_lin, norm_rows, place, sent0, sent1, sent2, sent3, table
):
    gain = head_cols[96:97, :]
    bias = head_cols[97:98, :]
    weights_t = head_cols[0:96, :].astype(bf16)
    total = jnp.zeros((96, D), f32)
    d_gain = jnp.zeros((1, D), f32)
    d_bias = jnp.zeros((1, D), f32)
    for index in range(8):
        source, first = (near, far)[index // 4], 2 * (index % 4)
        x = source[first : first + 2, 0:ROWS, :].reshape(2 * ROWS, D).astype(f32)
        scaled, _ = norm_parts(x)
        normed = (scaled * gain + bias).astype(bf16)
        d_part = jnp.concatenate(
            [d_lin[block_of(place, first + one, index // 4)] for one in range(2)], 1
        )
        total = total + nn(d_part, normed)
        d_normed = tn(d_part, weights_t)
        d_gain = d_gain + jnp.sum(d_normed * scaled, 0, keepdims=True)
        d_bias = d_bias + jnp.sum(d_normed, 0, keepdims=True)
    pad = jnp.zeros((28, D), f32)
    table[...] = jnp.concatenate([total, d_gain, d_bias, norm_rows[0:2, :], pad], 0).T
    for step, sent in enumerate((sent0, sent1, sent2, sent3)):
        x = lax.rem(place[4] + step, 4)
        for k in range(2):
            at = pl.multiple_of((4 * k + x) * 64, 64)
            sent[k] = table[pl.ds(at, 64), :].astype(bf16)


def regroup_kernel(part0, part1, part2, part3, feed, sent):
    heads = part0[...].astype(f32)
    for part in (part1, part2, part3):
        heads = heads + part[...].astype(f32)
    total = jnp.concatenate([feed[...].astype(f32), heads.reshape(128, 128)], 1)
    for d in range(SEQ * 2):
        sent[d] = total[4 * d : 4 * d + 4].astype(bf16)


def input_grad_kernel(
    place, length, tokens, d_lin, weights, w0, w1, head_cols,
    grad_tokens, layer_output,
    parts, arrived,
):
    loads = [load_part(place, weights, parts, arrived, i) for i in range(3)]
    for load in loads:
        for copy in load:
            copy.start()
    seq = place[3]
    gain = head_cols[96:97, :]
    scaled, inv = norm_parts(tokens[0].astype(f32))
    d_t = jnp.zeros((D, ROWS), f32)
    for part, load in enumerate(loads):
        d_part = d_lin[:, part * HEAD : (part + 1) * HEAD, :].reshape(D, ROWS)
        finish(load)
        d_t = d_t + nn(parts[part].reshape(D, D), d_part)
    total = w0[...].astype(f32) + w1[...].astype(f32)
    grad_tokens[0] = total[:, 0:D] + norm_back(d_t.T, scaled, inv, gain)
    row = lax.broadcasted_iota(jnp.int32, (ROWS, 1), 0)
    live = (seq * ROWS + row) < length[0]
    layer_output[0] = jnp.where(live, total[:, D : 2 * D], 0.0).astype(bf16)


def sum_kernel(
    parts, order, gain1, bias1, grad_query, grad_key, grad_value, grad_output, gain2, bias2,
    grad_gate, grad_up, grad_down,
):
    members = []
    for t in range(TEAM):
        total = parts[t, :, :FEED_LANES].astype(f32)
        for other in range(1, 2 * SEQ // TEAM):
            total = total + parts[TEAM * other + t, :, :FEED_LANES].astype(f32)
        members.append(total)
        grad_down[4 * t : 4 * t + 4, :] = total[:, 1024:1536]
    grad_output[...] = sum(m[:, 1536:2048] for m in members)
    pieces = []
    for u in range(4):
        for at in (128 * u, 512 + 128 * u):
            pieces.append(jnp.concatenate([m[:, at : at + 128] for m in members], 1))
    wide = jnp.concatenate(pieces, 0)
    high = wide.astype(bf16)
    low = (wide - high.astype(f32)).astype(bf16)
    wide = nt(high, order[...]) + nt(low, order[...])
    for u in range(4):
        here = slice(512 * u, 512 * (u + 1))
        grad_gate[:, here] = wide[8 * u : 8 * u + 4]
        grad_up[:, here] = wide[8 * u + 4 : 8 * u + 8]
    heads = [
        parts[h, :, FEED_LANES:].astype(f32) + parts[SEQ + h, :, FEED_LANES:].astype(f32)
        for h in range(HEADS)
    ]
    lane = lax.broadcasted_iota(jnp.int32, (4, 128), 1)
    row = lax.broadcasted_iota(jnp.int32, (4, 128), 0)
    for i, grad in enumerate((grad_query, grad_key, grad_value)):
        for u in range(4):
            tile = jnp.zeros((4, 128), f32)
            for r in range(4):
                moved = pltpu.roll(heads[4 * u + r], (HEAD * (r - i)) % 128, 1)
                tile = jnp.where(lane // HEAD == r, moved, tile)
            grad[:, 128 * u : 128 * (u + 1)] = tile
    norms = sum(heads)
    for n, grad in enumerate((gain1, bias1, gain2, bias2)):
        column = jnp.where(lane == row, norms[:, 96 + n : 97 + n], 0.0)
        grad[...] = jnp.sum(column, 0)[0:4]


VM = pl.BlockSpec(memory_space=pltpu.VMEM)
SM = pl.BlockSpec(memory_space=pltpu.SMEM)
HBM = pl.BlockSpec(memory_space=pl.ANY)


def call(kernel, specs, outs, scratch=()):
    return pl.pallas_call(
        kernel,
        out_shape=tuple(jax.ShapeDtypeStruct(shape, kind) for shape, kind in outs),
        in_specs=specs,
        out_specs=tuple(VM for _ in outs),
        scratch_shapes=[
            pltpu.SemaphoreType.DMA((s,)) if isinstance(s, int) else pltpu.VMEM(*s) for s in scratch
        ],
        compiler_params=pltpu.CompilerParams(vmem_limit_bytes=56 * 2**20),
        cost_estimate=pl.CostEstimate(flops=0, bytes_accessed=0, transcendentals=0),
    )


def rope_tables():
    freq = 10000.0 ** (-2.0 * np.arange(HALF) / HEAD)
    angles = freq[:, None] * np.arange(LEN)[None, :]
    return np.cos(angles).astype(np.float32), np.sin(angles).astype(np.float32)


def column_order():
    order = np.arange(512).reshape(4, 8, TEAM, 4).transpose(2, 0, 1, 3).reshape(-1)
    table = np.zeros((512, 512), np.float32)
    table[order, np.arange(512)] = 1.0
    return table


def exchange(value, axes):
    return lax.all_to_all(value, axes, 0, 0, tiled=True)


def swap(value, axis):
    return lax.ppermute(value, axis, [(0, 1), (1, 0)])


def step_dp(value, k, by):
    if k == by == 0:
        return value
    moves = [
        (4 * z + x, 4 * (z ^ k) + (x + by) % 4) for z in range(2) for x in range(4)
    ]
    return lax.ppermute(value, ("z_lo", "x"), moves)


def shift(value, by):
    return lax.ppermute(value, "x", [(i, (i + by) % 4) for i in range(4)])


def shards(
    tokens, lengths, norm1_gain, norm1_bias, w_query, w_key, w_value, w_output,
    norm2_gain, norm2_bias, w_gate, w_up, w_down, cotangent,
):
    y = lax.axis_index("y")
    z = lax.axis_index("z")
    core = lax.axis_index("core")
    place = jnp.stack([core, y, z, 4 * y + 2 * z + core, lax.axis_index("x"), lax.axis_index("z_lo")]).astype(jnp.int32)
    cos, sin = (jnp.asarray(table) for table in rope_tables())
    order = jnp.asarray(column_order(), bf16)

    (packed,) = call(
        pack_kernel,
        [VM] * 13,
        [((8, MSG_ROWS, D), bf16)],
    )(
        tokens, w_query, w_key, w_value, w_output, w_gate, w_up, w_down,
        norm1_gain, norm1_bias, norm2_gain, norm2_bias, order,
    )
    near = exchange(packed, CHIPS)
    cot_pair = jnp.concatenate([cotangent, swap(cotangent, "z")], 0)
    near = after(near, cot_pair)
    far = swap(near, "core")
    cot_far = swap(cot_pair, "core")

    feed_rows, head, whole = call(
        unpack_kernel,
        [SM, HBM, HBM, HBM],
        [((1, 64, FEED_LANES), bf16), ((1, 64, 128), bf16), ((1, 64, 3 * D), bf16)],
        [((2, 8, 48, D), bf16), 2],
    )(place, near, far, cot_far)
    heads = [step_dp(head, k, by) for k in range(2) for by in range(4)]
    feed_rows = jnp.concatenate([feed_rows, swap(feed_rows, "z_lo")], 0)
    feed_weights = lax.all_gather(after(feed_rows, *heads[1:]), "x")
    whole_other = swap(whole, "z_lo")

    sent, q_t, k_t, v_t, o_t, lse, head_cols = call(
        attend_kernel,
        [SM, SM] + [VM] * 12,
        [
            ((SEQ, HEAD, TEAM_ROWS), bf16),
            ((HEAD, LEN), bf16),
            ((HEAD, LEN), bf16),
            ((HEAD, LEN), bf16),
            ((HEAD, LEN), f32),
            ((1, LEN), f32),
            ((128, D), f32),
        ],
        [((HEAD, LEN), bf16)] * 3
        + [((DP, 64, 128), bf16)],
    )(place, lengths, near, far, *heads, cos, sin)
    mixed = exchange(after(sent, whole_other), WINDOW)
    whole = jnp.concatenate([whole, whole_other], 0)
    d_sent, kept, swapped, grads, norm_rows = call(
        feed_kernel,
        [SM, SM, VM, HBM, HBM, VM, VM, HBM, VM, HBM],
        [((HEADS, HEAD, TEAM_ROWS), bf16)]
        + [((2, ROWS, 2 * D), bf16)] * 2
        + [((4, 2, 64, FEED_LANES), bf16), ((8, D), f32)],
        [((TEAM_ROWS, D), bf16)] * 4 + [((4, 2, 4, 64, 512), bf16), 32, 4],
    )(
        place, lengths, mixed, near, far, cot_pair, cot_far,
        feed_weights, head_cols, whole,
    )
    row_weights = lax.all_gather(after(whole, grads), "x")
    d_mixed = exchange(d_sent, WINDOW)
    feed_grads = lax.psum_scatter(
        grads.reshape(D, FEED_LANES), "x", scatter_dimension=0, tiled=True
    )
    w0, w1 = call(add_kernel, [VM] * 2, [((ROWS, 2 * D), bf16)] * 2)(kept, swap(swapped, "core"))
    w1 = swap(w1, "z")
    (lin_sent,) = call(
        attend_back_kernel,
        [SM] + [VM] * 8,
        [((SEQ, 96, ROWS), bf16)],
        [
            ((HEAD, LEN), bf16),
            ((LEN, LEN), bf16),
            ((LEN, LEN), bf16),
            ((HEAD, LEN), f32),
            ((HEAD, LEN), f32),
            ((HEAD, LEN), f32),
        ],
    )(lengths, d_mixed, q_t, k_t, v_t, o_t, lse, cos, sin)
    lin_sent = after(lin_sent, w1)
    back = exchange(lin_sent, WINDOW)
    head_grads = call(
        head_grad_kernel,
        [VM] * 5 + [SM],
        [((2, 64, 128), bf16)] * 4,
        [((D, 128), f32)],
    )(near, far, head_cols, lin_sent, norm_rows, place)
    head_grads = [head_grads[0]] + [shift(head_grads[step], step) for step in range(1, 4)]
    (grad_sent,) = call(
        regroup_kernel,
        [VM] * 5,
        [((2 * SEQ, 4, GRAD_LANES), bf16)],
    )(*head_grads, feed_grads)
    grad_parts = exchange(after(grad_sent, back), SLICE)

    grad_tokens, layer_output = call(
        input_grad_kernel,
        [SM, SM] + [VM] * 2 + [HBM] + [VM] * 3,
        [((1, ROWS, D), f32), ((1, ROWS, D), bf16)],
        [((3, 2, 4, 64, 512), bf16), 24],
    )(place, lengths, tokens, back, row_weights, w0, w1, head_cols)
    weight_grads = call(
        sum_kernel,
        [VM] * 2,
        [((4,), f32)] * 2 + [((4, D), f32)] * 4 + [((4,), f32)] * 2
        + [((4, FF), f32)] * 2 + [((16, D), f32)],
    )(grad_parts, order)
    return (layer_output, grad_tokens) + tuple(weight_grads)


def solution(mesh):
    flat = P(ALL)
    rows = P(ALL, None)
    blocks = P(("z_lo", "x"), WINDOW, None)
    return jax.shard_map(
        shards,
        mesh=Mesh(mesh.devices.reshape(2, 4, 4, 2, 2), ALL),
        in_specs=(
            blocks, P(("z_lo", "x")), flat, flat, rows, rows, rows, rows, flat, flat, rows, rows, rows, blocks,
        ),
        out_specs=(
            blocks, blocks, flat, flat, rows, rows, rows, rows, flat, flat, rows, rows, rows,
        ),
        check_vma=False,
    )
```

```python
import math

import jax
import jax.numpy as jnp
import numpy as np
from jax import lax
from jax.experimental import pallas as pl
from jax.experimental.pallas import tpu as pltpu
from jax.sharding import Mesh
from jax.sharding import PartitionSpec as P

HEADS = 16
HEAD = 32
HALF = HEAD // 2
D = 512
FF = 2048
LEN = 2048
ROWS = 128
TEAM = 4
TEAM_ROWS = TEAM * ROWS
FF_PART = FF // TEAM
DEVICES = 128
SEQ = 16
DP = 8
AUG = 48

EPS = 1e-05
MASKED = -1.0e9
SCALE = HEAD**-0.5
LOG2E = math.log2(math.e)
LN2 = math.log(2.0)

f32 = jnp.float32
bf16 = jnp.bfloat16
WINDOW = ("y", "z", "core")
CHIPS = ("y", "z")
SLICE = ("z_lo", "y", "z", "core")
WINDOWS = ("z_lo", "x")
ALL = ("z_lo", "x", "y", "z", "core")


def nn(a, b):
    return lax.dot_general(a, b, (((1,), (0,)), ((), ())), preferred_element_type=f32)


def nt(a, b):
    return lax.dot_general(a, b, (((1,), (1,)), ((), ())), preferred_element_type=f32)


def tn(a, b):
    return lax.dot_general(a, b, (((0,), (0,)), ((), ())), preferred_element_type=f32)


def norm_parts(x):
    centered = x - jnp.mean(x, -1, keepdims=True)
    inv = lax.rsqrt(jnp.mean(centered * centered, -1, keepdims=True) + EPS)
    return centered * inv, inv


def norm_back(grad, scaled, inv, gain):
    e = grad * gain
    return inv * (
        e - jnp.mean(e, -1, keepdims=True) - scaled * jnp.mean(e * scaled, -1, keepdims=True)
    )


def split3(row):
    hi = row.astype(bf16)
    rest = row - hi.astype(f32)
    mid = rest.astype(bf16)
    low = (rest - mid.astype(f32)).astype(bf16)
    return [hi.astype(f32), mid.astype(f32), low.astype(f32)]


def key_columns(keys_t, length):
    place = lax.broadcasted_iota(jnp.int32, (1, LEN), 1)
    mask = jnp.where(place < length, 0.0, MASKED).astype(f32)
    ones = jnp.ones((3, LEN), f32)
    pad = jnp.zeros((128 - HEAD - 4, LEN), f32)
    return jnp.concatenate([keys_t, mask, ones, pad], 0).T.astype(bf16)[:, :AUG]


def with_rows(data_t, rows):
    pad = jnp.zeros((AUG - HEAD - len(rows), data_t.shape[1]), f32)
    return jnp.concatenate([data_t.astype(f32)] + rows + [pad], 0).astype(bf16)


def after(value, *others, place=pltpu.HBM):
    def kernel(*refs):
        pass

    return pl.pallas_call(
        kernel,
        out_shape=place(value.shape, value.dtype),
        in_specs=[pl.BlockSpec(memory_space=pl.ANY)] * (1 + len(others)),
        out_specs=pl.BlockSpec(memory_space=pl.ANY),
        input_output_aliases={0: 0},
        compiler_params=pltpu.CompilerParams(vmem_limit_bytes=2**20),
        cost_estimate=pl.CostEstimate(flops=0, bytes_accessed=0, transcendentals=0),
    )(pltpu.with_memory_space_constraint(value, place), *others)


FEED_LANES = FF_PART * 3 + D
GRAD_LANES = FEED_LANES + 128
MSG_ROWS = ROWS + 48


def pack_kernel(
    tokens, w_query, w_key, w_value, w_output, w_gate, w_up, w_down, gain1, bias1, gain2, bias2,
    order, sent,
):
    narrow = [w[...].astype(f32) for w in (w_query, w_key, w_value)]
    gate = w_gate[...].astype(f32)
    up = w_up[...].astype(f32)
    down = w_down[...].astype(f32)
    pieces = []
    for u in range(4):
        here = slice(512 * u, 512 * (u + 1))
        pieces.append(jnp.concatenate([gate[:, here], up[:, here]], 0))
    wide = nn(jnp.concatenate(pieces, 0).astype(bf16), order[...])
    lane = lax.broadcasted_iota(jnp.int32, (4, 128), 1)
    row = lax.broadcasted_iota(jnp.int32, (4, 128), 0)
    norms = jnp.zeros((4, 128), f32)
    for n, ref in enumerate((gain1, bias1, gain2, bias2)):
        for i in range(4):
            value = ref[i : i + 1].astype(f32).reshape(1, 1)
            norms = norms + jnp.where((lane == 96 + n) & (row == i), value, 0.0)
    out = w_output[...].astype(f32)
    nothing = jnp.zeros((4, 512), f32)
    for z in range(2):
        mine = []
        for t in (2 * z, 2 * z + 1):
            cols = slice(128 * t, 128 * (t + 1))
            mine.append(jnp.concatenate([wide[8 * u : 8 * u + 4, cols] for u in range(4)], 1))
            mine.append(jnp.concatenate([wide[8 * u + 4 : 8 * u + 8, cols] for u in range(4)], 1))
            mine.append(down[4 * t : 4 * t + 4])
        mine = jnp.concatenate(mine + [out] + narrow, 0)
        for y in range(4):
            tile = slice(128 * y, 128 * (y + 1))
            heads = []
            for t in (2 * z, 2 * z + 1):
                q, k, v = (
                    pltpu.roll(w[:, tile], (HEAD * (i - t)) % 128, 1)
                    for i, w in enumerate(narrow)
                )
                heads.append(
                    jnp.where(
                        lane < 32, q, jnp.where(lane < 64, k, jnp.where(lane < 96, v, norms))
                    )
                )
            heads = jnp.concatenate(heads + [nothing[:, :256]], 1)
            low = jnp.concatenate([mine, heads, nothing], 0).astype(bf16)
            sent[2 * y + z, 0:ROWS, :] = tokens[0]
            sent[2 * y + z, ROWS:, :] = low


def unpack_kernel(place, near, far, cot, feed, heads, whole, rows, arrived):
    loads = [
        pltpu.make_async_copy(source.at[:, ROWS:, :], rows.at[i], arrived.at[i])
        for i, source in enumerate((near, far))
    ]
    for load in loads:
        load.start()
    for load in loads:
        load.wait()
    second = place[0] == 1
    for group in range(4):
        blocks = []
        for chip in (2 * group, 2 * group + 1):
            own = rows[0, chip].astype(f32)
            other = rows[1, chip].astype(f32)
            blocks += [jnp.where(second, other, own), jnp.where(second, own, other)]
        here = slice(16 * group, 16 * (group + 1))
        for i in range(3):
            cols = jnp.concatenate(
                [
                    jnp.where(second, b[4 * (i + 3) : 4 * (i + 4)], b[4 * i : 4 * (i + 1)])
                    for b in blocks
                ],
                0,
            )
            feed[0, here, D * i : D * (i + 1)] = cols.astype(bf16)
        for i in range(4):
            cols = jnp.concatenate([b[4 * (i + 6) : 4 * (i + 7)] for b in blocks], 0).astype(bf16)
            if i == 0:
                feed[0, here, 3 * D : 4 * D] = cols
            else:
                whole[0, here, D * (i - 1) : D * i] = cols
        cols = jnp.concatenate(
            [jnp.where(second, b[40:44, 128:256], b[40:44, 0:128]) for b in blocks], 0
        )
        cols = cols.astype(bf16)
        for w in range(DP):
            heads[w, here, :] = cols


def block_of(place, chip, other):
    return 2 * chip + (place[0] ^ other)


def attend_kernel(
    place, length, near, far, head_cols, cos, sin,
    sent, q_out, k_out, v_out, o_out, lse_out, cols_out,
    q_t, k_t, v_t,
):
    cols = head_cols[...].reshape(D, 128).astype(f32).T
    cols_out[...] = cols
    gain = cols[96:97, :]
    bias = cols[97:98, :]
    weights_t = cols[0:96, :].astype(bf16)
    for index in range(8):
        source, first = (near, far)[index // 4], 2 * (index % 4)
        x = source[first : first + 2, 0:ROWS, :].reshape(2 * ROWS, D).astype(f32)
        scaled, _ = norm_parts(x)
        normed = (scaled * gain + bias).astype(bf16)
        lin = nt(weights_t, normed)
        for one in range(2):
            block = block_of(place, first + one, index // 4)
            here = pl.ds(pl.multiple_of(block * ROWS, ROWS), ROWS)
            part = lin[:, one * ROWS : (one + 1) * ROWS]
            c = cos[:, here]
            s = sin[:, here]
            q1, q2 = part[0:16], part[16:32]
            k1, k2 = part[32:48], part[48:64]
            fold = SCALE * LOG2E
            q_t[:, here] = (
                jnp.concatenate([q1 * c - q2 * s, q2 * c + q1 * s], 0) * fold
            ).astype(bf16)
            k_t[:, here] = jnp.concatenate([k1 * c - k2 * s, k2 * c + k1 * s], 0).astype(bf16)
            v_t[:, here] = part[64:96].astype(bf16)
    q_out[...] = q_t[...]
    k_out[...] = k_t[...]
    v_out[...] = v_t[...]
    keys = key_columns(k_t[...].astype(f32), length[0])
    one_row = jnp.ones((1, LEN), f32)
    values_t = with_rows(v_t[...], [one_row])
    tile = TEAM_ROWS
    for i in range(LEN // tile):
        here = slice(i * tile, (i + 1) * tile)
        queries_t = with_rows(q_t[:, here], [jnp.ones((1, tile), f32)])
        scores = nn(keys, queries_t)
        top = jnp.max(scores, axis=0, keepdims=True)
        weights = jnp.exp2(scores - top).astype(bf16)
        mixed = nn(values_t, weights)
        total = mixed[HEAD : HEAD + 1]
        out = mixed[:HEAD] / total
        o_out[:, here] = out
        lse_out[:, here] = top + jnp.log2(total)
        low = out.astype(bf16)
        for t in range(TEAM):
            sent[TEAM * i + t] = low


def load_part(place, weights, parts, arrived, i):
    return [
        pltpu.make_async_copy(
            weights.at[x, place[5] ^ k, :, 512 * i : 512 * (i + 1)],
            parts.at[i, k, x],
            arrived.at[8 * i + 4 * k + x],
        )
        for k in range(2)
        for x in range(4)
    ]


def finish(copies):
    for copy in copies:
        copy.wait()


def feed_kernel(
    place, length, mixed, near, far, cot_near, cot_far, weights, head_cols, other,
    sent, kept, swapped, grads, norm_rows,
    tokens, cot, back, ahead, parts, arrived, tokens_arrived,
):
    core, team, z = place[0], place[1], place[2]
    token_loads = []
    for one in range(2):
        for other, source in enumerate((near, far)):
            here = pl.ds(pl.multiple_of((2 * (z ^ one) + (core ^ other)) * ROWS, ROWS), ROWS)
            token_loads.append(
                pltpu.make_async_copy(
                    source.at[2 * team + (z ^ one), 0:ROWS, :],
                    tokens.at[here, :],
                    tokens_arrived.at[2 * one + other],
                )
            )
    for load in token_loads:
        load.start()
    member = 2 * z + core
    for one in range(2):
        here = pl.ds(pl.multiple_of((2 * (z ^ one) + core) * ROWS, ROWS), ROWS)
        there = pl.ds(pl.multiple_of((2 * (z ^ one) + 1 - core) * ROWS, ROWS), ROWS)
        cot[here, :] = cot_near[one]
        cot[there, :] = cot_far[one]
    gain = head_cols[98:99, :]
    bias = head_cols[99:100, :]
    loads = [load_part(place, weights, parts, arrived, i) for i in (3, 0, 1, 2)]
    for load in loads:
        for copy in load:
            copy.start()
    mixed_t = mixed[...].reshape(D, TEAM_ROWS)
    finish(token_loads)
    finish(loads[0])
    w_out = parts[3].reshape(D, D)
    row = lax.broadcasted_iota(jnp.int32, (TEAM_ROWS, 1), 0)
    live = (team * TEAM_ROWS + row) < length[0]
    own = (row // ROWS) == member
    middle = tokens[...].astype(f32) + tn(mixed_t, w_out)
    scaled, inv = norm_parts(middle)
    normed = (scaled * gain + bias).astype(bf16)
    finish(loads[1])
    w_gate = parts[0].reshape(D, FF_PART)
    gate = nn(normed, w_gate)
    finish(loads[2])
    w_up = parts[1].reshape(D, FF_PART)
    up = nn(normed, w_up)
    finish(loads[3])
    w_down = parts[2].reshape(FF_PART, D)
    sig = jax.nn.sigmoid(gate)
    act = gate * sig
    hidden = (act * up).astype(bf16)
    out_part = nn(hidden, w_down) + jnp.where(own, middle, 0.0)
    d_out = jnp.where(live, cot[...].astype(f32), 0.0)
    d_out_low = d_out.astype(bf16)
    d_hidden = nt(d_out_low, w_down)
    d_up = (d_hidden * act).astype(bf16)
    d_gate = (d_hidden * up * sig * (1.0 + gate * (1.0 - sig))).astype(bf16)
    d_normed = nt(d_gate, w_gate) + nt(d_up, w_up)
    d_middle = jnp.where(own, d_out, 0.0) + norm_back(d_normed, scaled, inv, gain)
    d_middle_low = d_middle.astype(bf16)
    sent[...] = nt(w_out, d_middle_low).astype(bf16).reshape(HEADS, HEAD, TEAM_ROWS)
    back[...] = d_middle_low
    ahead[...] = out_part.astype(bf16)
    for one in range(2):
        for target, other in ((kept, core), (swapped, 1 - core)):
            here = pl.ds(pl.multiple_of((2 * (z ^ one) + other) * ROWS, ROWS), ROWS)
            target[one, :, 0:D] = back[here, :]
            target[one, :, D : 2 * D] = ahead[here, :]
    for i, grad in enumerate(
        (
            tn(normed, d_gate),
            tn(normed, d_up),
            tn(hidden, d_out_low),
            nn(mixed_t, d_middle_low),
        )
    ):
        low = grad.astype(bf16)
        for k in range(2):
            for x in range(4):
                at = 64 * (4 * k + x)
                grads[x, k, :, D * i : D * (i + 1)] = low[at : at + 64]
    norm_rows[0:1, :] = jnp.sum(d_normed * scaled, 0, keepdims=True)
    norm_rows[1:2, :] = jnp.sum(d_normed, 0, keepdims=True)
    norm_rows[2:8, :] = jnp.zeros((6, D), f32)


def add_kernel(kept, arrived, own, other):
    own[...] = (kept[0].astype(f32) + arrived[0].astype(f32)).astype(bf16)
    other[...] = (kept[1].astype(f32) + arrived[1].astype(f32)).astype(bf16)


def attend_back_kernel(
    length, d_mixed, q_in, k_in, v_in, o_in, lse_in, cos, sin, sent, d_o, probs, d_scores, dq, dk, dv
):
    for y in range(LEN // TEAM_ROWS):
        total = d_mixed[TEAM * y].astype(f32)
        for t in range(1, TEAM):
            total = total + d_mixed[TEAM * y + t].astype(f32)
        d_o[:, y * TEAM_ROWS : (y + 1) * TEAM_ROWS] = total.astype(bf16)
    keys_t = k_in[...]
    keys = key_columns(keys_t.astype(f32), length[0])
    ones = jnp.ones((4, LEN), f32)
    pad = jnp.zeros((128 - HEAD - 4, LEN), f32)
    values = jnp.concatenate([v_in[...].astype(f32), ones, pad], 0).T.astype(bf16)[:, :AUG]
    d_o_t = d_o[...]
    inner = jnp.sum(d_o_t.astype(f32) * o_in[...], 0, keepdims=True)
    zero_row = jnp.zeros((1, LEN), f32)
    one_row = jnp.ones((1, LEN), f32)
    q_rows = with_rows(q_in[...], [one_row] + split3(-lse_in[...]))
    do_rows = with_rows(d_o_t, [zero_row] + split3(-inner))
    tile = 512
    for i in range(LEN // tile):
        here = slice(i * tile, (i + 1) * tile)
        p = jnp.exp2(nn(keys, q_rows[:, here]))
        ds = (p * nn(values, do_rows[:, here])).astype(bf16)
        probs[:, here] = p.astype(bf16)
        d_scores[:, here] = ds
        dq[:, here] = nn(keys_t, ds) * SCALE
    dk[...] = nt(q_in[...], d_scores[...]) * LN2
    dv[...] = nt(d_o_t, probs[...])
    c = cos[...]
    s = sin[...]
    q1, q2 = dq[0:HALF], dq[HALF:HEAD]
    k1, k2 = dk[0:HALF], dk[HALF:HEAD]
    dq_t = jnp.concatenate([q1 * c + q2 * s, q2 * c - q1 * s], 0).astype(bf16)
    dk_t = jnp.concatenate([k1 * c + k2 * s, k2 * c - k1 * s], 0).astype(bf16)
    dv_t = dv[...].astype(bf16)
    for b in range(SEQ):
        here = slice(b * ROWS, (b + 1) * ROWS)
        sent[b, 0:32] = dq_t[:, here]
        sent[b, 32:64] = dk_t[:, here]
        sent[b, 64:96] = dv_t[:, here]


def head_grad_kernel(
    near, far, head_cols, d_lin, norm_rows, place, sent0, sent1, sent2, sent3, table
):
    gain = head_cols[96:97, :]
    bias = head_cols[97:98, :]
    weights_t = head_cols[0:96, :].astype(bf16)
    total = jnp.zeros((96, D), f32)
    d_gain = jnp.zeros((1, D), f32)
    d_bias = jnp.zeros((1, D), f32)
    for index in range(8):
        source, first = (near, far)[index // 4], 2 * (index % 4)
        x = source[first : first + 2, 0:ROWS, :].reshape(2 * ROWS, D).astype(f32)
        scaled, _ = norm_parts(x)
        normed = (scaled * gain + bias).astype(bf16)
        d_part = jnp.concatenate(
            [d_lin[block_of(place, first + one, index // 4)] for one in range(2)], 1
        )
        total = total + nn(d_part, normed)
        d_normed = tn(d_part, weights_t)
        d_gain = d_gain + jnp.sum(d_normed * scaled, 0, keepdims=True)
        d_bias = d_bias + jnp.sum(d_normed, 0, keepdims=True)
    pad = jnp.zeros((28, D), f32)
    table[...] = jnp.concatenate([total, d_gain, d_bias, norm_rows[0:2, :], pad], 0).T
    for step, sent in enumerate((sent0, sent1, sent2, sent3)):
        x = lax.rem(place[4] + step, 4)
        for k in range(2):
            at = pl.multiple_of((4 * k + x) * 64, 64)
            sent[k] = table[pl.ds(at, 64), :].astype(bf16)


def regroup_kernel(part0, part1, part2, part3, feed, sent):
    heads = part0[...].astype(f32)
    for part in (part1, part2, part3):
        heads = heads + part[...].astype(f32)
    total = jnp.concatenate([feed[...].astype(f32), heads.reshape(128, 128)], 1)
    for d in range(SEQ * 2):
        sent[d] = total[4 * d : 4 * d + 4].astype(bf16)


def input_grad_kernel(
    place, length, tokens, d_lin, weights, w0, w1, head_cols,
    grad_tokens, layer_output,
    parts, arrived,
):
    loads = [load_part(place, weights, parts, arrived, i) for i in range(3)]
    for load in loads:
        for copy in load:
            copy.start()
    seq = place[3]
    gain = head_cols[96:97, :]
    scaled, inv = norm_parts(tokens[0].astype(f32))
    d_t = jnp.zeros((D, ROWS), f32)
    for part, load in enumerate(loads):
        d_part = d_lin[:, part * HEAD : (part + 1) * HEAD, :].reshape(D, ROWS)
        finish(load)
        d_t = d_t + nn(parts[part].reshape(D, D), d_part)
    total = w0[...].astype(f32) + w1[...].astype(f32)
    grad_tokens[0] = total[:, 0:D] + norm_back(d_t.T, scaled, inv, gain)
    row = lax.broadcasted_iota(jnp.int32, (ROWS, 1), 0)
    live = (seq * ROWS + row) < length[0]
    layer_output[0] = jnp.where(live, total[:, D : 2 * D], 0.0).astype(bf16)


def sum_kernel(
    parts, order, gain1, bias1, grad_query, grad_key, grad_value, grad_output, gain2, bias2,
    grad_gate, grad_up, grad_down,
):
    members = []
    for t in range(TEAM):
        total = parts[t, :, :FEED_LANES].astype(f32)
        for other in range(1, 2 * SEQ // TEAM):
            total = total + parts[TEAM * other + t, :, :FEED_LANES].astype(f32)
        members.append(total)
        grad_down[4 * t : 4 * t + 4, :] = total[:, 1024:1536]
    grad_output[...] = sum(m[:, 1536:2048] for m in members)
    pieces = []
    for u in range(4):
        for at in (128 * u, 512 + 128 * u):
            pieces.append(jnp.concatenate([m[:, at : at + 128] for m in members], 1))
    wide = jnp.concatenate(pieces, 0)
    high = wide.astype(bf16)
    low = (wide - high.astype(f32)).astype(bf16)
    wide = nt(high, order[...]) + nt(low, order[...])
    for u in range(4):
        here = slice(512 * u, 512 * (u + 1))
        grad_gate[:, here] = wide[8 * u : 8 * u + 4]
        grad_up[:, here] = wide[8 * u + 4 : 8 * u + 8]
    heads = [
        parts[h, :, FEED_LANES:].astype(f32) + parts[SEQ + h, :, FEED_LANES:].astype(f32)
        for h in range(HEADS)
    ]
    lane = lax.broadcasted_iota(jnp.int32, (4, 128), 1)
    row = lax.broadcasted_iota(jnp.int32, (4, 128), 0)
    for i, grad in enumerate((grad_query, grad_key, grad_value)):
        for u in range(4):
            tile = jnp.zeros((4, 128), f32)
            for r in range(4):
                moved = pltpu.roll(heads[4 * u + r], (HEAD * (r - i)) % 128, 1)
                tile = jnp.where(lane // HEAD == r, moved, tile)
            grad[:, 128 * u : 128 * (u + 1)] = tile
    norms = sum(heads)
    for n, grad in enumerate((gain1, bias1, gain2, bias2)):
        column = jnp.where(lane == row, norms[:, 96 + n : 97 + n], 0.0)
        grad[...] = jnp.sum(column, 0)[0:4]


def call(kernel, ins, outs, scratch=(), vmem=8):
    places = {"V": pltpu.VMEM, "H": pltpu.VMEM, "A": pl.ANY, "P": pl.ANY, "S": pltpu.SMEM}
    inner = pl.pallas_call(
        kernel,
        out_shape=tuple(
            (pltpu.VMEM if where == "V" else pltpu.HBM)(shape, kind) for shape, kind, where in outs
        ),
        in_specs=[pl.BlockSpec(memory_space=places[where]) for where in ins],
        out_specs=tuple(pl.BlockSpec(memory_space=pltpu.VMEM) for _ in outs),
        scratch_shapes=[
            pltpu.SemaphoreType.DMA((s,)) if isinstance(s, int) else pltpu.VMEM(*s) for s in scratch
        ],
        compiler_params=pltpu.CompilerParams(vmem_limit_bytes=vmem * 2**20),
        cost_estimate=pl.CostEstimate(flops=0, bytes_accessed=0, transcendentals=0),
    )

    def run(*args):
        assert len(args) == len(ins)
        return inner(
            *(
                pltpu.with_memory_space_constraint(x, pltpu.HBM) if where in "HA" else x
                for x, where in zip(args, ins)
            )
        )

    return run


def rope_tables():
    freq = 10000.0 ** (-2.0 * np.arange(HALF) / HEAD)
    angles = freq[:, None] * np.arange(LEN)[None, :]
    return np.cos(angles).astype(np.float32), np.sin(angles).astype(np.float32)


def column_order():
    order = np.arange(512).reshape(4, 8, TEAM, 4).transpose(2, 0, 1, 3).reshape(-1)
    table = np.zeros((512, 512), np.float32)
    table[order, np.arange(512)] = 1.0
    return table


def exchange(value, axes):
    return lax.all_to_all(value, axes, 0, 0, tiled=True)


def swap(value, axis):
    return lax.ppermute(value, axis, [(0, 1), (1, 0)])


def shift(value, by):
    return lax.ppermute(value, "x", [(i, (i + by) % 4) for i in range(4)])


def shards(
    tokens, lengths, norm1_gain, norm1_bias, w_query, w_key, w_value, w_output,
    norm2_gain, norm2_bias, w_gate, w_up, w_down, cotangent,
):
    y = lax.axis_index("y")
    z = lax.axis_index("z")
    core = lax.axis_index("core")
    place = jnp.stack([core, y, z, 4 * y + 2 * z + core, lax.axis_index("x"), lax.axis_index("z_lo")]).astype(jnp.int32)
    cos, sin = (jnp.asarray(table) for table in rope_tables())
    order = jnp.asarray(column_order(), bf16)

    (packed,) = call(
        pack_kernel,
        "H" * 13,
        [((8, MSG_ROWS, D), bf16, "H")],
    )(
        tokens, w_query, w_key, w_value, w_output, w_gate, w_up, w_down,
        norm1_gain, norm1_bias, norm2_gain, norm2_bias, order,
    )
    near = exchange(packed, CHIPS)
    cot_pair = jnp.concatenate([cotangent, swap(cotangent, "z")], 0)
    near = after(near, cot_pair, place=pltpu.VMEM)
    far = swap(near, "core")
    cot_far = swap(cot_pair, "core")

    feed_rows, heads, whole = call(
        unpack_kernel,
        "SPPP",
        [
            ((1, 64, FEED_LANES), bf16, "H"),
            ((DP, 64, 128), bf16, "H"),
            ((1, 64, 3 * D), bf16, "H"),
        ],
        [((2, 8, 48, D), bf16), 2],
    )(place, near, far, cot_far)
    head_cols = exchange(heads, WINDOWS).reshape(D, 128)
    feed_rows = jnp.concatenate([feed_rows, swap(feed_rows, "z_lo")], 0)
    feed_weights = lax.all_gather(after(feed_rows, head_cols), "x")
    whole_other = swap(whole, "z_lo")

    sent, q_t, k_t, v_t, o_t, lse, head_cols = call(
        attend_kernel,
        "SSVVVHH",
        [
            ((SEQ, HEAD, TEAM_ROWS), bf16, "H"),
            ((HEAD, LEN), bf16, "H"),
            ((HEAD, LEN), bf16, "H"),
            ((HEAD, LEN), bf16, "H"),
            ((HEAD, LEN), f32, "H"),
            ((1, LEN), f32, "H"),
            ((128, D), f32, "H"),
        ],
        [((HEAD, LEN), bf16)] * 3,
        vmem=24,
    )(place, lengths, near, far, head_cols, cos, sin)
    mixed = exchange(after(sent, whole_other), WINDOW)
    whole = jnp.concatenate([whole, whole_other], 0)

    d_sent, kept, swapped, grads, norm_rows = call(
        feed_kernel,
        "SSVPPHHAHA",
        [
            ((HEADS, HEAD, TEAM_ROWS), bf16, "H"),
            ((2, ROWS, 2 * D), bf16, "H"),
            ((2, ROWS, 2 * D), bf16, "H"),
            ((4, 2, 64, FEED_LANES), bf16, "H"),
            ((8, D), f32, "H"),
        ],
        [((TEAM_ROWS, D), bf16)] * 4 + [((4, 2, 4, 64, 512), bf16), 32, 4],
        vmem=24,
    )(
        place, lengths, mixed, near, far, cot_pair, cot_far, feed_weights, head_cols, whole,
    )
    d_mixed = exchange(d_sent, WINDOW)
    feed_grads = lax.psum_scatter(
        grads.reshape(D, FEED_LANES), "x", scatter_dimension=0, tiled=True
    )
    row_weights = lax.all_gather(after(whole, pltpu.with_memory_space_constraint(norm_rows, pltpu.HBM)), "x")
    w0, w1 = call(
        add_kernel, "HV", [((ROWS, 2 * D), bf16, "H")] * 2
    )(kept, swap(swapped, "core"))
    w1 = swap(w1, "z")

    (lin_sent,) = call(
        attend_back_kernel,
        "SVHHHHHHH",
        [((SEQ, 96, ROWS), bf16, "H")],
        [
            ((HEAD, LEN), bf16),
            ((LEN, LEN), bf16),
            ((LEN, LEN), bf16),
            ((HEAD, LEN), f32),
            ((HEAD, LEN), f32),
            ((HEAD, LEN), f32),
        ],
        vmem=40,
    )(lengths, d_mixed, q_t, k_t, v_t, o_t, lse, cos, sin)
    lin_sent = after(lin_sent, w1)
    back = exchange(lin_sent, WINDOW)
    head_grads = call(
        head_grad_kernel,
        "VVHHHS",
        [((2, 64, 128), bf16, "H")] * 4,
        [((D, 128), f32)],
        vmem=16,
    )(near, far, head_cols, lin_sent, norm_rows, place)
    head_grads = [head_grads[0]] + [shift(head_grads[step], step) for step in range(1, 4)]
    (grad_sent,) = call(
        regroup_kernel,
        "HVVVH",
        [((2 * SEQ, 4, GRAD_LANES), bf16, "H")],
    )(*head_grads, feed_grads)
    grad_parts = exchange(after(grad_sent, back), SLICE)

    grad_tokens, layer_output = call(
        input_grad_kernel,
        "SSHVAHHH",
        [((1, ROWS, D), f32, "H"), ((1, ROWS, D), bf16, "H")],
        [((3, 2, 4, 64, 512), bf16), 24],
    )(place, lengths, tokens, back, row_weights, w0, w1, head_cols)
    weight_grads = call(
        sum_kernel,
        "VH",
        [((4,), f32, "H")] * 2 + [((4, D), f32, "H")] * 4 + [((4,), f32, "H")] * 2
        + [((4, FF), f32, "H")] * 2 + [((16, D), f32, "H")],
    )(grad_parts, order)
    return (layer_output, grad_tokens) + tuple(weight_grads)


def solution(mesh):
    flat = P(ALL)
    rows = P(ALL, None)
    blocks = P(("z_lo", "x"), WINDOW, None)
    return jax.shard_map(
        shards,
        mesh=Mesh(mesh.devices.reshape(2, 4, 4, 2, 2), ALL),
        in_specs=(
            blocks, P(("z_lo", "x")), flat, flat, rows, rows, rows, rows, flat, flat, rows, rows, rows, blocks,
        ),
        out_specs=(
            blocks, blocks, flat, flat, rows, rows, rows, rows, flat, flat, rows, rows, rows,
        ),
        check_vma=False,
    )
```

```python
import math

import jax
import jax.numpy as jnp
import numpy as np
from jax import lax
from jax.experimental import pallas as pl
from jax.experimental.pallas import tpu as pltpu
from jax.sharding import Mesh
from jax.sharding import PartitionSpec as P

HEADS = 16
HEAD = 32
HALF = HEAD // 2
D = 512
FF = 2048
LEN = 2048
ROWS = 128
TEAM = 4
TEAM_ROWS = TEAM * ROWS
FF_PART = FF // TEAM
DEVICES = 128
SEQ = 16
DP = 8
AUG = 48

EPS = 1e-05
MASKED = -1.0e9
SCALE = HEAD**-0.5
LOG2E = math.log2(math.e)
LN2 = math.log(2.0)

f32 = jnp.float32
bf16 = jnp.bfloat16
WINDOW = ("y", "z", "core")
CHIPS = ("y", "z")
SLICE = ("z_lo", "y", "z", "core")
WINDOWS = ("z_lo", "x")
ALL = ("z_lo", "x", "y", "z", "core")


def nn(a, b):
    return lax.dot_general(a, b, (((1,), (0,)), ((), ())), preferred_element_type=f32)


def nt(a, b):
    return lax.dot_general(a, b, (((1,), (1,)), ((), ())), preferred_element_type=f32)


def tn(a, b):
    return lax.dot_general(a, b, (((0,), (0,)), ((), ())), preferred_element_type=f32)


def norm_parts(x):
    centered = x - jnp.mean(x, -1, keepdims=True)
    inv = lax.rsqrt(jnp.mean(centered * centered, -1, keepdims=True) + EPS)
    return centered * inv, inv


def norm_back(grad, scaled, inv, gain):
    e = grad * gain
    return inv * (
        e - jnp.mean(e, -1, keepdims=True) - scaled * jnp.mean(e * scaled, -1, keepdims=True)
    )


def split3(row):
    hi = row.astype(bf16)
    rest = row - hi.astype(f32)
    mid = rest.astype(bf16)
    low = (rest - mid.astype(f32)).astype(bf16)
    return [hi.astype(f32), mid.astype(f32), low.astype(f32)]


def key_columns(keys_t, length):
    place = lax.broadcasted_iota(jnp.int32, (1, LEN), 1)
    mask = jnp.where(place < length, 0.0, MASKED).astype(f32)
    ones = jnp.ones((3, LEN), f32)
    pad = jnp.zeros((128 - HEAD - 4, LEN), f32)
    return jnp.concatenate([keys_t, mask, ones, pad], 0).T.astype(bf16)[:, :AUG]


def with_rows(data_t, rows):
    pad = jnp.zeros((AUG - HEAD - len(rows), data_t.shape[1]), f32)
    return jnp.concatenate([data_t.astype(f32)] + rows + [pad], 0).astype(bf16)


def in_hbm(value):
    return pltpu.with_memory_space_constraint(value, pltpu.HBM)


def after(value, *others, place=pltpu.HBM):
    def kernel(*refs):
        pass

    return pl.pallas_call(
        kernel,
        out_shape=place(value.shape, value.dtype),
        in_specs=[pl.BlockSpec(memory_space=pl.ANY)] * (1 + len(others)),
        out_specs=pl.BlockSpec(memory_space=pl.ANY),
        input_output_aliases={0: 0},
        compiler_params=pltpu.CompilerParams(vmem_limit_bytes=2**20),
        cost_estimate=pl.CostEstimate(flops=0, bytes_accessed=0, transcendentals=0),
    )(pltpu.with_memory_space_constraint(value, place), *others)


FEED_LANES = FF_PART * 3 + D
GRAD_LANES = FEED_LANES + 128
MSG_ROWS = ROWS + 48


def pack_kernel(
    tokens, w_query, w_key, w_value, w_output, w_gate, w_up, w_down, gain1, bias1, gain2, bias2,
    order, sent,
):
    narrow = [w[...].astype(f32) for w in (w_query, w_key, w_value)]
    gate = w_gate[...].astype(f32)
    up = w_up[...].astype(f32)
    down = w_down[...].astype(f32)
    pieces = []
    for u in range(4):
        here = slice(512 * u, 512 * (u + 1))
        pieces.append(jnp.concatenate([gate[:, here], up[:, here]], 0))
    wide = nn(jnp.concatenate(pieces, 0).astype(bf16), order[...])
    lane = lax.broadcasted_iota(jnp.int32, (4, 128), 1)
    row = lax.broadcasted_iota(jnp.int32, (4, 128), 0)
    norms = jnp.zeros((4, 128), f32)
    for n, ref in enumerate((gain1, bias1, gain2, bias2)):
        for i in range(4):
            value = ref[i : i + 1].astype(f32).reshape(1, 1)
            norms = norms + jnp.where((lane == 96 + n) & (row == i), value, 0.0)
    out = w_output[...].astype(f32)
    nothing = jnp.zeros((4, 512), f32)
    for z in range(2):
        mine = []
        for t in (2 * z, 2 * z + 1):
            cols = slice(128 * t, 128 * (t + 1))
            mine.append(jnp.concatenate([wide[8 * u : 8 * u + 4, cols] for u in range(4)], 1))
            mine.append(jnp.concatenate([wide[8 * u + 4 : 8 * u + 8, cols] for u in range(4)], 1))
            mine.append(down[4 * t : 4 * t + 4])
        mine = jnp.concatenate(mine + [out] + narrow, 0)
        for y in range(4):
            tile = slice(128 * y, 128 * (y + 1))
            heads = []
            for t in (2 * z, 2 * z + 1):
                q, k, v = (
                    pltpu.roll(w[:, tile], (HEAD * (i - t)) % 128, 1)
                    for i, w in enumerate(narrow)
                )
                heads.append(
                    jnp.where(
                        lane < 32, q, jnp.where(lane < 64, k, jnp.where(lane < 96, v, norms))
                    )
                )
            heads = jnp.concatenate(heads + [nothing[:, :256]], 1)
            low = jnp.concatenate([mine, heads, nothing], 0).astype(bf16)
            sent[2 * y + z, 0:ROWS, :] = tokens[0]
            sent[2 * y + z, ROWS:, :] = low


def unpack_kernel(place, near, far, cot, feed, heads, whole, rows, arrived):
    loads = [
        pltpu.make_async_copy(source.at[:, ROWS:, :], rows.at[i], arrived.at[i])
        for i, source in enumerate((near, far))
    ]
    for load in loads:
        load.start()
    for load in loads:
        load.wait()
    second = place[0] == 1
    for group in range(4):
        blocks = []
        for chip in (2 * group, 2 * group + 1):
            own = rows[0, chip].astype(f32)
            other = rows[1, chip].astype(f32)
            blocks += [jnp.where(second, other, own), jnp.where(second, own, other)]
        here = slice(16 * group, 16 * (group + 1))
        for i in range(3):
            cols = jnp.concatenate(
                [
                    jnp.where(second, b[4 * (i + 3) : 4 * (i + 4)], b[4 * i : 4 * (i + 1)])
                    for b in blocks
                ],
                0,
            )
            feed[0, here, D * i : D * (i + 1)] = cols.astype(bf16)
        for i in range(4):
            cols = jnp.concatenate([b[4 * (i + 6) : 4 * (i + 7)] for b in blocks], 0).astype(bf16)
            if i == 0:
                feed[0, here, 3 * D : 4 * D] = cols
            else:
                whole[0, here, D * (i - 1) : D * i] = cols
        cols = jnp.concatenate(
            [jnp.where(second, b[40:44, 128:256], b[40:44, 0:128]) for b in blocks], 0
        )
        cols = cols.astype(bf16)
        for w in range(DP):
            heads[w, here, :] = cols


def block_of(place, chip, other):
    return 2 * chip + (place[0] ^ other)


def attend_kernel(
    place, length, near, far, head_cols, cos, sin,
    sent, q_out, k_out, v_out, o_out, lse_out, cols_out,
    q_t, k_t, v_t,
):
    cols = head_cols[...].reshape(D, 128).astype(f32).T
    cols_out[...] = cols
    gain = cols[96:97, :]
    bias = cols[97:98, :]
    weights_t = cols[0:96, :].astype(bf16)
    for index in range(8):
        source, first = (near, far)[index // 4], 2 * (index % 4)
        x = source[first : first + 2, 0:ROWS, :].reshape(2 * ROWS, D).astype(f32)
        scaled, _ = norm_parts(x)
        normed = (scaled * gain + bias).astype(bf16)
        lin = nt(weights_t, normed)
        for one in range(2):
            block = block_of(place, first + one, index // 4)
            here = pl.ds(pl.multiple_of(block * ROWS, ROWS), ROWS)
            part = lin[:, one * ROWS : (one + 1) * ROWS]
            c = cos[:, here]
            s = sin[:, here]
            q1, q2 = part[0:16], part[16:32]
            k1, k2 = part[32:48], part[48:64]
            fold = SCALE * LOG2E
            q_t[:, here] = (
                jnp.concatenate([q1 * c - q2 * s, q2 * c + q1 * s], 0) * fold
            ).astype(bf16)
            k_t[:, here] = jnp.concatenate([k1 * c - k2 * s, k2 * c + k1 * s], 0).astype(bf16)
            v_t[:, here] = part[64:96].astype(bf16)
    q_out[...] = q_t[...]
    k_out[...] = k_t[...]
    v_out[...] = v_t[...]
    keys = key_columns(k_t[...].astype(f32), length[0])
    one_row = jnp.ones((1, LEN), f32)
    values_t = with_rows(v_t[...], [one_row])
    tile = TEAM_ROWS
    for i in range(LEN // tile):
        here = slice(i * tile, (i + 1) * tile)
        queries_t = with_rows(q_t[:, here], [jnp.ones((1, tile), f32)])
        scores = nn(keys, queries_t)
        top = jnp.max(scores, axis=0, keepdims=True)
        weights = jnp.exp2(scores - top).astype(bf16)
        mixed = nn(values_t, weights)
        total = mixed[HEAD : HEAD + 1]
        out = mixed[:HEAD] / total
        o_out[:, here] = out
        lse_out[:, here] = top + jnp.log2(total)
        low = out.astype(bf16)
        for t in range(TEAM):
            sent[TEAM * i + t] = low


def load_part(place, weights, parts, arrived, i):
    return [
        pltpu.make_async_copy(
            weights.at[x, place[5] ^ k, :, 512 * i : 512 * (i + 1)],
            parts.at[i, k, x],
            arrived.at[8 * i + 4 * k + x],
        )
        for k in range(2)
        for x in range(4)
    ]


def finish(copies):
    for copy in copies:
        copy.wait()


def feed_kernel(
    place, length, mixed, near, far, cot_near, cot_far, weights, head_cols, other1, other2,
    sent, kept, swapped, grads, norm_rows,
    tokens, cot, back, ahead, parts, arrived, tokens_arrived,
):
    core, team, z = place[0], place[1], place[2]
    token_loads = []
    for one in range(2):
        for other, source in enumerate((near, far)):
            here = pl.ds(pl.multiple_of((2 * (z ^ one) + (core ^ other)) * ROWS, ROWS), ROWS)
            token_loads.append(
                pltpu.make_async_copy(
                    source.at[2 * team + (z ^ one), 0:ROWS, :],
                    tokens.at[here, :],
                    tokens_arrived.at[2 * one + other],
                )
            )
    for load in token_loads:
        load.start()
    member = 2 * z + core
    for one in range(2):
        here = pl.ds(pl.multiple_of((2 * (z ^ one) + core) * ROWS, ROWS), ROWS)
        there = pl.ds(pl.multiple_of((2 * (z ^ one) + 1 - core) * ROWS, ROWS), ROWS)
        cot[here, :] = cot_near[one]
        cot[there, :] = cot_far[one]
    gain = head_cols[98:99, :]
    bias = head_cols[99:100, :]
    loads = [load_part(place, weights, parts, arrived, i) for i in (3, 0, 1, 2)]
    for load in loads:
        for copy in load:
            copy.start()
    mixed_t = mixed[...].reshape(D, TEAM_ROWS)
    finish(token_loads)
    finish(loads[0])
    w_out = parts[3].reshape(D, D)
    row = lax.broadcasted_iota(jnp.int32, (TEAM_ROWS, 1), 0)
    live = (team * TEAM_ROWS + row) < length[0]
    own = (row // ROWS) == member
    middle = tokens[...].astype(f32) + tn(mixed_t, w_out)
    scaled, inv = norm_parts(middle)
    normed = (scaled * gain + bias).astype(bf16)
    finish(loads[1])
    w_gate = parts[0].reshape(D, FF_PART)
    gate = nn(normed, w_gate)
    finish(loads[2])
    w_up = parts[1].reshape(D, FF_PART)
    up = nn(normed, w_up)
    finish(loads[3])
    w_down = parts[2].reshape(FF_PART, D)
    sig = jax.nn.sigmoid(gate)
    act = gate * sig
    hidden = (act * up).astype(bf16)
    out_part = nn(hidden, w_down) + jnp.where(own, middle, 0.0)
    d_out = jnp.where(live, cot[...].astype(f32), 0.0)
    d_out_low = d_out.astype(bf16)
    d_hidden = nt(d_out_low, w_down)
    d_up = (d_hidden * act).astype(bf16)
    d_gate = (d_hidden * up * sig * (1.0 + gate * (1.0 - sig))).astype(bf16)
    d_normed = nt(d_gate, w_gate) + nt(d_up, w_up)
    d_middle = jnp.where(own, d_out, 0.0) + norm_back(d_normed, scaled, inv, gain)
    d_middle_low = d_middle.astype(bf16)
    sent[...] = nt(w_out, d_middle_low).astype(bf16).reshape(HEADS, HEAD, TEAM_ROWS)
    back[...] = d_middle_low
    ahead[...] = out_part.astype(bf16)
    for one in range(2):
        for target, other in ((kept, core), (swapped, 1 - core)):
            here = pl.ds(pl.multiple_of((2 * (z ^ one) + other) * ROWS, ROWS), ROWS)
            target[one, :, 0:D] = back[here, :]
            target[one, :, D : 2 * D] = ahead[here, :]
    for i, grad in enumerate(
        (
            tn(normed, d_gate),
            tn(normed, d_up),
            tn(hidden, d_out_low),
            nn(mixed_t, d_middle_low),
        )
    ):
        low = grad.astype(bf16)
        for k in range(2):
            for x in range(4):
                at = 64 * (4 * k + x)
                grads[x, k, :, D * i : D * (i + 1)] = low[at : at + 64]
    norm_rows[0:1, :] = jnp.sum(d_normed * scaled, 0, keepdims=True)
    norm_rows[1:2, :] = jnp.sum(d_normed, 0, keepdims=True)
    norm_rows[2:8, :] = jnp.zeros((6, D), f32)


def add_kernel(kept, arrived, own, other):
    own[...] = (kept[0].astype(f32) + arrived[0].astype(f32)).astype(bf16)
    other[...] = (kept[1].astype(f32) + arrived[1].astype(f32)).astype(bf16)


def scale_kernel(place, near, far, other, scaled):
    for index in range(8):
        source, first = (near, far)[index // 4], 2 * (index % 4)
        x = source[first : first + 2, 0:ROWS, :].reshape(2 * ROWS, D).astype(f32)
        low = norm_parts(x)[0].astype(bf16)
        for one in range(2):
            block = block_of(place, first + one, index // 4)
            scaled[block] = low[one * ROWS : (one + 1) * ROWS]


def attend_back_kernel(
    place, length, d_mixed, q_in, k_in, v_in, o_in, lse_in, cos, sin, scaled, head_cols, norm_rows,
    sent, sent0, sent1, sent2, sent3,
    d_o, probs, d_scores, dq, dk, dv, table, normal, here_now,
):
    load = pltpu.make_async_copy(scaled, normal, here_now.at[0])
    load.start()
    for y in range(LEN // TEAM_ROWS):
        total = d_mixed[TEAM * y].astype(f32)
        for t in range(1, TEAM):
            total = total + d_mixed[TEAM * y + t].astype(f32)
        d_o[:, y * TEAM_ROWS : (y + 1) * TEAM_ROWS] = total.astype(bf16)
    keys_t = k_in[...]
    keys = key_columns(keys_t.astype(f32), length[0])
    ones = jnp.ones((4, LEN), f32)
    pad = jnp.zeros((128 - HEAD - 4, LEN), f32)
    values = jnp.concatenate([v_in[...].astype(f32), ones, pad], 0).T.astype(bf16)[:, :AUG]
    d_o_t = d_o[...]
    inner = jnp.sum(d_o_t.astype(f32) * o_in[...], 0, keepdims=True)
    zero_row = jnp.zeros((1, LEN), f32)
    one_row = jnp.ones((1, LEN), f32)
    q_rows = with_rows(q_in[...], [one_row] + split3(-lse_in[...]))
    do_rows = with_rows(d_o_t, [zero_row] + split3(-inner))
    tile = 512
    for i in range(LEN // tile):
        here = slice(i * tile, (i + 1) * tile)
        p = jnp.exp2(nn(keys, q_rows[:, here]))
        ds = (p * nn(values, do_rows[:, here])).astype(bf16)
        probs[:, here] = p.astype(bf16)
        d_scores[:, here] = ds
        dq[:, here] = nn(keys_t, ds) * SCALE
    dk[...] = nt(q_in[...], d_scores[...]) * LN2
    dv[...] = nt(d_o_t, probs[...])
    c = cos[...]
    s = sin[...]
    q1, q2 = dq[0:HALF], dq[HALF:HEAD]
    k1, k2 = dk[0:HALF], dk[HALF:HEAD]
    dq_t = jnp.concatenate([q1 * c + q2 * s, q2 * c - q1 * s], 0).astype(bf16)
    dk_t = jnp.concatenate([k1 * c + k2 * s, k2 * c - k1 * s], 0).astype(bf16)
    dv_t = dv[...].astype(bf16)
    for b in range(SEQ):
        here = slice(b * ROWS, (b + 1) * ROWS)
        sent[b, 0:32] = dq_t[:, here]
        sent[b, 32:64] = dk_t[:, here]
        sent[b, 64:96] = dv_t[:, here]
    d_lin = jnp.concatenate([dq_t, dk_t, dv_t], 0)
    load.wait()
    product = nn(d_lin, normal[...].reshape(LEN, D))
    total = jnp.sum(d_lin.astype(f32), 1, keepdims=True)
    weights = head_cols[0:96, :]
    gain = head_cols[96:97, :]
    bias = head_cols[97:98, :]
    rows = [
        product * gain + total * bias,
        jnp.sum(product * weights, 0, keepdims=True),
        jnp.sum(total * weights, 0, keepdims=True),
        norm_rows[0:2, :],
        jnp.zeros((28, D), f32),
    ]
    table[...] = jnp.concatenate(rows, 0).T
    for step, part in enumerate((sent0, sent1, sent2, sent3)):
        x = lax.rem(place[4] + step, 4)
        for k in range(2):
            at = pl.multiple_of((4 * k + x) * 64, 64)
            part[k] = table[pl.ds(at, 64), :].astype(bf16)


def regroup_kernel(part0, part1, part2, part3, feed, sent):
    heads = part0[...].astype(f32)
    for part in (part1, part2, part3):
        heads = heads + part[...].astype(f32)
    total = jnp.concatenate([feed[...].astype(f32), heads.reshape(128, 128)], 1)
    for d in range(SEQ * 2):
        sent[d] = total[4 * d : 4 * d + 4].astype(bf16)


def input_grad_kernel(
    place, length, tokens, d_lin, weights, w0, w1, head_cols,
    grad_tokens, layer_output,
    parts, arrived,
):
    loads = [load_part(place, weights, parts, arrived, i) for i in range(3)]
    for load in loads:
        for copy in load:
            copy.start()
    seq = place[3]
    gain = head_cols[96:97, :]
    scaled, inv = norm_parts(tokens[0].astype(f32))
    d_t = jnp.zeros((D, ROWS), f32)
    for part, load in enumerate(loads):
        d_part = d_lin[:, part * HEAD : (part + 1) * HEAD, :].reshape(D, ROWS)
        finish(load)
        d_t = d_t + nn(parts[part].reshape(D, D), d_part)
    total = w0[...].astype(f32) + w1[...].astype(f32)
    grad_tokens[0] = total[:, 0:D] + norm_back(d_t.T, scaled, inv, gain)
    row = lax.broadcasted_iota(jnp.int32, (ROWS, 1), 0)
    live = (seq * ROWS + row) < length[0]
    layer_output[0] = jnp.where(live, total[:, D : 2 * D], 0.0).astype(bf16)


def sum_kernel(
    parts, order, gain1, bias1, grad_query, grad_key, grad_value, grad_output, gain2, bias2,
    grad_gate, grad_up, grad_down,
):
    members = []
    for t in range(TEAM):
        total = parts[t, :, :FEED_LANES].astype(f32)
        for other in range(1, 2 * SEQ // TEAM):
            total = total + parts[TEAM * other + t, :, :FEED_LANES].astype(f32)
        members.append(total)
        grad_down[4 * t : 4 * t + 4, :] = total[:, 1024:1536]
    grad_output[...] = sum(m[:, 1536:2048] for m in members)
    pieces = []
    for u in range(4):
        for at in (128 * u, 512 + 128 * u):
            pieces.append(jnp.concatenate([m[:, at : at + 128] for m in members], 1))
    wide = jnp.concatenate(pieces, 0)
    high = wide.astype(bf16)
    low = (wide - high.astype(f32)).astype(bf16)
    wide = nt(high, order[...]) + nt(low, order[...])
    for u in range(4):
        here = slice(512 * u, 512 * (u + 1))
        grad_gate[:, here] = wide[8 * u : 8 * u + 4]
        grad_up[:, here] = wide[8 * u + 4 : 8 * u + 8]
    heads = [
        parts[h, :, FEED_LANES:].astype(f32) + parts[SEQ + h, :, FEED_LANES:].astype(f32)
        for h in range(HEADS)
    ]
    lane = lax.broadcasted_iota(jnp.int32, (4, 128), 1)
    row = lax.broadcasted_iota(jnp.int32, (4, 128), 0)
    for i, grad in enumerate((grad_query, grad_key, grad_value)):
        for u in range(4):
            tile = jnp.zeros((4, 128), f32)
            for r in range(4):
                moved = pltpu.roll(heads[4 * u + r], (HEAD * (r - i)) % 128, 1)
                tile = jnp.where(lane // HEAD == r, moved, tile)
            grad[:, 128 * u : 128 * (u + 1)] = tile
    norms = sum(heads)
    for n, grad in enumerate((gain1, bias1, gain2, bias2)):
        column = jnp.where(lane == row, norms[:, 96 + n : 97 + n], 0.0)
        grad[...] = jnp.sum(column, 0)[0:4]


def call(kernel, ins, outs, scratch=(), vmem=8, flops=0):
    places = {"V": pltpu.VMEM, "U": pltpu.VMEM, "H": pltpu.VMEM, "A": pl.ANY, "P": pl.ANY, "S": pltpu.SMEM}
    inner = pl.pallas_call(
        kernel,
        out_shape=tuple(
            (pltpu.VMEM if where == "V" else pltpu.HBM)(shape, kind) for shape, kind, where in outs
        ),
        in_specs=[pl.BlockSpec(memory_space=places[where]) for where in ins],
        out_specs=tuple(pl.BlockSpec(memory_space=places[where]) for _, _, where in outs),
        scratch_shapes=[
            pltpu.SemaphoreType.DMA((s,)) if isinstance(s, int) else pltpu.VMEM(*s) for s in scratch
        ],
        compiler_params=pltpu.CompilerParams(vmem_limit_bytes=vmem * 2**20),
        cost_estimate=pl.CostEstimate(flops=flops, bytes_accessed=0, transcendentals=0),
    )

    def run(*args):
        assert len(args) == len(ins)
        return inner(
            *(
                pltpu.with_memory_space_constraint(x, pltpu.HBM if where in "HA" else pltpu.VMEM)
                if where in "HAV"
                else x
                for x, where in zip(args, ins)
            )
        )

    return run


def rope_tables():
    freq = 10000.0 ** (-2.0 * np.arange(HALF) / HEAD)
    angles = freq[:, None] * np.arange(LEN)[None, :]
    return np.cos(angles).astype(np.float32), np.sin(angles).astype(np.float32)


def column_order():
    order = np.arange(512).reshape(4, 8, TEAM, 4).transpose(2, 0, 1, 3).reshape(-1)
    table = np.zeros((512, 512), np.float32)
    table[order, np.arange(512)] = 1.0
    return table


def exchange(value, axes):
    return lax.all_to_all(value, axes, 0, 0, tiled=True)


def swap(value, axis):
    return lax.ppermute(value, axis, [(0, 1), (1, 0)])


def shift(value, by):
    return lax.ppermute(value, "x", [(i, (i + by) % 4) for i in range(4)])


def shards(
    tokens, lengths, norm1_gain, norm1_bias, w_query, w_key, w_value, w_output,
    norm2_gain, norm2_bias, w_gate, w_up, w_down, cotangent,
):
    y = lax.axis_index("y")
    z = lax.axis_index("z")
    core = lax.axis_index("core")
    place = jnp.stack([core, y, z, 4 * y + 2 * z + core, lax.axis_index("x"), lax.axis_index("z_lo")]).astype(jnp.int32)
    cos, sin = (jnp.asarray(table) for table in rope_tables())
    order = jnp.asarray(column_order(), bf16)

    (packed,) = call(
        pack_kernel,
        "H" * 13,
        [((8, MSG_ROWS, D), bf16, "H")],
    )(
        tokens, w_query, w_key, w_value, w_output, w_gate, w_up, w_down,
        norm1_gain, norm1_bias, norm2_gain, norm2_bias, order,
    )
    near = exchange(packed, CHIPS)
    cot_pair = jnp.concatenate([cotangent, swap(cotangent, "z")], 0)
    near = after(near, cot_pair, place=pltpu.VMEM)
    far = swap(near, "core")
    cot_far = swap(cot_pair, "core")

    feed_rows, heads, whole = call(
        unpack_kernel,
        "SPPP",
        [
            ((1, 64, FEED_LANES), bf16, "V"),
            ((DP, 64, 128), bf16, "H"),
            ((1, 64, 3 * D), bf16, "H"),
        ],
        [((2, 8, 48, D), bf16), 2],
    )(place, near, far, cot_far)
    head_cols = exchange(heads, WINDOWS).reshape(D, 128)
    feed_rows = jnp.concatenate([feed_rows, swap(feed_rows, "z_lo")], 0)
    feed_weights = lax.all_gather(after(feed_rows, head_cols), "x")
    whole_other = swap(whole, "z_lo")

    sent, q_t, k_t, v_t, o_t, lse, head_cols = call(
        attend_kernel,
        "SSVVVHH",
        [
            ((SEQ, HEAD, TEAM_ROWS), bf16, "H"),
            ((HEAD, LEN), bf16, "H"),
            ((HEAD, LEN), bf16, "H"),
            ((HEAD, LEN), bf16, "H"),
            ((HEAD, LEN), f32, "H"),
            ((1, LEN), f32, "H"),
            ((128, D), f32, "H"),
        ],
        [((HEAD, LEN), bf16)] * 3,
        vmem=24,
    )(place, lengths, near, far, head_cols, cos, sin)
    sent = after(sent, whole_other)
    (scaled,) = call(
        scale_kernel, "SUUA", [((SEQ, ROWS, D), bf16, "H")], vmem=12
    )(place, near, far, sent)
    mixed = exchange(sent, WINDOW)
    whole = jnp.concatenate([whole, whole_other], 0)

    d_sent, kept, swapped, grads, norm_rows = call(
        feed_kernel,
        "SSHPPHHAHAA",
        [
            ((HEADS, HEAD, TEAM_ROWS), bf16, "H"),
            ((2, ROWS, 2 * D), bf16, "H"),
            ((2, ROWS, 2 * D), bf16, "V"),
            ((4, 2, 64, FEED_LANES), bf16, "H"),
            ((8, D), f32, "H"),
        ],
        [((TEAM_ROWS, D), bf16)] * 4 + [((4, 2, 4, 64, 512), bf16), 32, 4],
        vmem=24,
    )(
        place, lengths, mixed, near, far, cot_pair, cot_far, feed_weights, head_cols, whole, scaled,
    )
    d_mixed = exchange(d_sent, WINDOW)
    feed_grads = lax.psum_scatter(
        grads.reshape(D, FEED_LANES), "x", scatter_dimension=0, tiled=True
    )
    row_weights = lax.all_gather(after(whole, pltpu.with_memory_space_constraint(norm_rows, pltpu.HBM)), "x")
    w0, w1 = call(
        add_kernel, "HV", [((ROWS, 2 * D), bf16, "H")] * 2
    )(kept, swap(swapped, "core"))
    w1 = swap(w1, "z")

    lin_sent, *head_grads = call(
        attend_back_kernel,
        "SSVHHHHHHHAHH",
        [((SEQ, 96, ROWS), bf16, "H")] + [((2, 64, 128), bf16, "V")] * 4,
        [
            ((HEAD, LEN), bf16),
            ((LEN, LEN), bf16),
            ((LEN, LEN), bf16),
            ((HEAD, LEN), f32),
            ((HEAD, LEN), f32),
            ((HEAD, LEN), f32),
            ((D, 128), f32),
            ((SEQ, ROWS, D), bf16),
            1,
        ],
        vmem=40,
    )(place, lengths, d_mixed, q_t, k_t, v_t, o_t, lse, cos, sin, scaled, head_cols, norm_rows)
    lin_sent = after(lin_sent, w1)
    back = exchange(lin_sent, WINDOW)
    head_grads = [head_grads[0]] + [shift(head_grads[step], step) for step in range(1, 4)]
    (grad_sent,) = call(
        regroup_kernel,
        "UUUUH",
        [((2 * SEQ, 4, GRAD_LANES), bf16, "H")],
    )(*head_grads, feed_grads)
    grad_parts = exchange(after(grad_sent, back), SLICE)

    grad_tokens, layer_output = call(
        input_grad_kernel,
        "SSHVAHHH",
        [((1, ROWS, D), f32, "H"), ((1, ROWS, D), bf16, "H")],
        [((3, 2, 4, 64, 512), bf16), 24],
    )(place, lengths, tokens, back, row_weights, w0, w1, head_cols)
    weight_grads = call(
        sum_kernel,
        "VH",
        [((4,), f32, "H")] * 2 + [((4, D), f32, "H")] * 4 + [((4,), f32, "H")] * 2
        + [((4, FF), f32, "H")] * 2 + [((16, D), f32, "H")],
    )(grad_parts, order)
    return (layer_output, grad_tokens) + tuple(weight_grads)


def solution(mesh):
    flat = P(ALL)
    rows = P(ALL, None)
    blocks = P(("z_lo", "x"), WINDOW, None)
    return jax.shard_map(
        shards,
        mesh=Mesh(mesh.devices.reshape(2, 4, 4, 2, 2), ALL),
        in_specs=(
            blocks, P(("z_lo", "x")), flat, flat, rows, rows, rows, rows, flat, flat, rows, rows, rows, blocks,
        ),
        out_specs=(
            blocks, blocks, flat, flat, rows, rows, rows, rows, flat, flat, rows, rows, rows,
        ),
        check_vma=False,
    )
```

```python
import math

import jax
import jax.numpy as jnp
import numpy as np
from jax import lax
from jax.experimental import pallas as pl
from jax.experimental.pallas import tpu as pltpu
from jax.sharding import Mesh
from jax.sharding import PartitionSpec as P

HEADS = 16
HEAD = 32
HALF = HEAD // 2
D = 512
FF = 2048
LEN = 2048
ROWS = 128
TEAM = 4
TEAM_ROWS = TEAM * ROWS
FF_PART = FF // TEAM
DEVICES = 128
SEQ = 16
DP = 8
KEY_CHUNK = 256
AUG = 48

EPS = 1e-05
MASKED = -1.0e9
SCALE = HEAD**-0.5
LOG2E = math.log2(math.e)
LN2 = math.log(2.0)

f32 = jnp.float32
bf16 = jnp.bfloat16
WINDOW = ("y", "z", "core")
CHIPS = ("y", "z")
SLICE = ("z_lo", "y", "z", "core")
WINDOWS = ("z_lo", "x")
ALL = ("z_lo", "x", "y", "z", "core")


def nn(a, b):
    return lax.dot_general(a, b, (((1,), (0,)), ((), ())), preferred_element_type=f32)


def nt(a, b):
    return lax.dot_general(a, b, (((1,), (1,)), ((), ())), preferred_element_type=f32)


def tn(a, b):
    return lax.dot_general(a, b, (((0,), (0,)), ((), ())), preferred_element_type=f32)


def norm_parts(x):
    centered = x - jnp.mean(x, -1, keepdims=True)
    inv = lax.rsqrt(jnp.mean(centered * centered, -1, keepdims=True) + EPS)
    return centered * inv, inv


def norm_back(grad, scaled, inv, gain):
    e = grad * gain
    return inv * (
        e - jnp.mean(e, -1, keepdims=True) - scaled * jnp.mean(e * scaled, -1, keepdims=True)
    )


def split3(row):
    hi = row.astype(bf16)
    rest = row - hi.astype(f32)
    mid = rest.astype(bf16)
    low = (rest - mid.astype(f32)).astype(bf16)
    return [hi.astype(f32), mid.astype(f32), low.astype(f32)]


def key_columns(keys_t, length):
    place = lax.broadcasted_iota(jnp.int32, (1, LEN), 1)
    mask = jnp.where(place < length, 0.0, MASKED).astype(f32)
    ones = jnp.ones((3, LEN), f32)
    pad = jnp.zeros((128 - HEAD - 4, LEN), f32)
    return jnp.concatenate([keys_t, mask, ones, pad], 0).T.astype(bf16)[:, :AUG]


def with_rows(data_t, rows):
    pad = jnp.zeros((AUG - HEAD - len(rows), data_t.shape[1]), f32)
    return jnp.concatenate([data_t.astype(f32)] + rows + [pad], 0).astype(bf16)


def in_hbm(value):
    return pltpu.with_memory_space_constraint(value, pltpu.HBM)


def after(value, *others, place=pltpu.HBM):
    def kernel(*refs):
        pass

    return pl.pallas_call(
        kernel,
        out_shape=place(value.shape, value.dtype),
        in_specs=[pl.BlockSpec(memory_space=pl.ANY)] * (1 + len(others)),
        out_specs=pl.BlockSpec(memory_space=pl.ANY),
        input_output_aliases={0: 0},
        compiler_params=pltpu.CompilerParams(vmem_limit_bytes=2**20),
        cost_estimate=pl.CostEstimate(flops=0, bytes_accessed=0, transcendentals=0),
    )(pltpu.with_memory_space_constraint(value, place), *others)


FEED_LANES = FF_PART * 3 + D
GRAD_LANES = FEED_LANES + 128
MSG_ROWS = ROWS + 48


def column_order():
    n = lax.broadcasted_iota(jnp.int32, (512, 1), 0)
    to = ((n >> 2) & 3) * 128 + (n >> 7) * 32 + ((n >> 4) & 7) * 4 + (n & 3)
    lane = lax.broadcasted_iota(jnp.int32, (512, 512), 1)
    return jnp.where(lane == to, 1.0, 0.0).astype(bf16)


def pack_kernel(
    tokens, w_query, w_key, w_value, w_output, w_gate, w_up, w_down, gain1, bias1, gain2, bias2,
    sent,
    rows, left,
):
    leaving = [
        pltpu.make_async_copy(tokens.at[0], sent.at[chip, 0:ROWS, :], left.at[chip])
        for chip in range(8)
    ]
    for copy in leaving:
        copy.start()
    narrow = [w[...].astype(f32) for w in (w_query, w_key, w_value)]
    gate = w_gate[...].astype(f32)
    up = w_up[...].astype(f32)
    down = w_down[...].astype(f32)
    pieces = []
    for u in range(4):
        here = slice(512 * u, 512 * (u + 1))
        pieces.append(jnp.concatenate([gate[:, here], up[:, here]], 0))
    wide = nn(jnp.concatenate(pieces, 0).astype(bf16), column_order())
    lane = lax.broadcasted_iota(jnp.int32, (4, 128), 1)
    row = lax.broadcasted_iota(jnp.int32, (4, 128), 0)
    norms = jnp.zeros((4, 128), f32)
    for n, ref in enumerate((gain1, bias1, gain2, bias2)):
        for i in range(4):
            value = ref[i : i + 1].astype(f32).reshape(1, 1)
            norms = norms + jnp.where((lane == 96 + n) & (row == i), value, 0.0)
    out = w_output[...].astype(f32)
    nothing = jnp.zeros((4, 512), f32)
    for z in range(2):
        mine = []
        for t in (2 * z, 2 * z + 1):
            cols = slice(128 * t, 128 * (t + 1))
            mine.append(jnp.concatenate([wide[8 * u : 8 * u + 4, cols] for u in range(4)], 1))
            mine.append(jnp.concatenate([wide[8 * u + 4 : 8 * u + 8, cols] for u in range(4)], 1))
            mine.append(down[4 * t : 4 * t + 4])
        mine = jnp.concatenate(mine + [out] + narrow, 0)
        for y in range(4):
            tile = slice(128 * y, 128 * (y + 1))
            heads = []
            for t in (2 * z, 2 * z + 1):
                q, k, v = (
                    pltpu.roll(w[:, tile], (HEAD * (i - t)) % 128, 1)
                    for i, w in enumerate(narrow)
                )
                heads.append(
                    jnp.where(
                        lane < 32, q, jnp.where(lane < 64, k, jnp.where(lane < 96, v, norms))
                    )
                )
            heads = jnp.concatenate(heads + [nothing[:, :256]], 1)
            low = jnp.concatenate([mine, heads, nothing], 0).astype(bf16)
            rows[2 * y + z] = low
    copy = pltpu.make_async_copy(rows, sent.at[:, ROWS:, :], left.at[8])
    copy.start()
    leaving.append(copy)
    finish(leaving)


def unpack_kernel(place, near, far, cot, feed, heads, whole, rows, arrived):
    loads = [
        pltpu.make_async_copy(source.at[:, ROWS:, :], rows.at[i], arrived.at[i])
        for i, source in enumerate((near, far))
    ]
    for load in loads:
        load.start()
    for load in loads:
        load.wait()
    second = place[0] == 1
    for group in range(4):
        blocks = []
        for chip in (2 * group, 2 * group + 1):
            own = rows[0, chip].astype(f32)
            other = rows[1, chip].astype(f32)
            blocks += [jnp.where(second, other, own), jnp.where(second, own, other)]
        here = slice(16 * group, 16 * (group + 1))
        for i in range(3):
            cols = jnp.concatenate(
                [
                    jnp.where(second, b[4 * (i + 3) : 4 * (i + 4)], b[4 * i : 4 * (i + 1)])
                    for b in blocks
                ],
                0,
            )
            feed[0, here, D * i : D * (i + 1)] = cols.astype(bf16)
        for i in range(4):
            cols = jnp.concatenate([b[4 * (i + 6) : 4 * (i + 7)] for b in blocks], 0).astype(bf16)
            if i == 0:
                feed[0, here, 3 * D : 4 * D] = cols
            else:
                whole[0, here, D * (i - 1) : D * i] = cols
        cols = jnp.concatenate(
            [jnp.where(second, b[40:44, 128:256], b[40:44, 0:128]) for b in blocks], 0
        )
        cols = cols.astype(bf16)
        for w in range(DP):
            heads[w, here, :] = cols


def join_kernel(own, other, feed, out):
    for i, rows in enumerate((own, other)):
        feed[i] = rows[0, :, 0 : 3 * D]
        out[i] = rows[0, :, 3 * D : 4 * D]


def block_of(place, chip, other):
    return 2 * chip + (place[0] ^ other)


def attend_kernel(
    place, length, near, far, head_cols, cos, sin,
    sent, q_out, k_out, v_out, o_out, lse_out, cols_out,
    q_t, k_t, v_t, own_cols, left,
):
    leaving = []

    def send(source, target):
        copy = pltpu.make_async_copy(source, target, left.at[len(leaving)])
        copy.start()
        leaving.append(copy)

    cols = head_cols[...].reshape(D, 128).astype(f32).T
    own_cols[...] = cols
    send(own_cols, cols_out)
    gain = cols[96:97, :]
    bias = cols[97:98, :]
    weights_t = cols[0:96, :].astype(bf16)
    for index in range(8):
        source, first = (near, far)[index // 4], 2 * (index % 4)
        x = source[first : first + 2, 0:ROWS, :].reshape(2 * ROWS, D).astype(f32)
        scaled, _ = norm_parts(x)
        normed = (scaled * gain + bias).astype(bf16)
        lin = nt(weights_t, normed)
        for one in range(2):
            block = block_of(place, first + one, index // 4)
            here = pl.ds(pl.multiple_of(block * ROWS, ROWS), ROWS)
            part = lin[:, one * ROWS : (one + 1) * ROWS]
            c = cos[:, here]
            s = sin[:, here]
            q1, q2 = part[0:16], part[16:32]
            k1, k2 = part[32:48], part[48:64]
            fold = SCALE * LOG2E
            q_t[:, here] = (
                jnp.concatenate([q1 * c - q2 * s, q2 * c + q1 * s], 0) * fold
            ).astype(bf16)
            k_t[:, here] = jnp.concatenate([k1 * c - k2 * s, k2 * c + k1 * s], 0).astype(bf16)
            v_t[:, here] = part[64:96].astype(bf16)
    send(q_t, q_out)
    send(k_t, k_out)
    send(v_t, v_out)
    keys = key_columns(k_t[...].astype(f32), length[0])
    one_row = jnp.ones((1, LEN), f32)
    values_t = with_rows(v_t[...], [one_row])
    queries_t = with_rows(q_t[...], [one_row])
    top = mixed = None
    for i in range(LEN // KEY_CHUNK):
        here = slice(i * KEY_CHUNK, (i + 1) * KEY_CHUNK)
        scores = nn(keys[here, :], queries_t)
        new_top = jnp.max(scores, axis=0, keepdims=True)
        if i:
            new_top = jnp.maximum(top, new_top)
        weights = jnp.exp2(scores - new_top).astype(bf16)
        added = nn(values_t[:, here], weights)
        mixed = mixed * jnp.exp2(top - new_top) + added if i else added
        top = new_top
    total = mixed[HEAD : HEAD + 1]
    out = mixed[:HEAD] / total
    o_out[...] = out
    lse_out[...] = top + jnp.log2(total)
    low = out.astype(bf16)
    for i in range(LEN // TEAM_ROWS):
        for t in range(TEAM):
            sent[TEAM * i + t] = low[:, i * TEAM_ROWS : (i + 1) * TEAM_ROWS]
    finish(leaving)


def load_part(place, weights, parts, arrived, i):
    return [
        pltpu.make_async_copy(
            weights.at[x, place[5] ^ k, :, 512 * i : 512 * (i + 1)],
            parts.at[i, k, x],
            arrived.at[8 * i + 4 * k + x],
        )
        for k in range(2)
        for x in range(4)
    ]


def finish(copies):
    for copy in copies:
        copy.wait()


def feed_kernel(
    place, length, mixed, near, far, cot_near, cot_far, weights, head_cols, other1, other2,
    out0, out1, out2, out3,
    sent, kept, swapped, grads, norm_rows,
    mixed_rows, tokens, cot, norms, back, ahead, parts, own_sent, own_kept, own_grads,
    arrived, tokens_arrived, left,
):
    core, team, z = place[0], place[1], place[2]
    first = [
        pltpu.make_async_copy(mixed, mixed_rows, tokens_arrived.at[8]),
        pltpu.make_async_copy(head_cols.at[96:104, :], norms, tokens_arrived.at[9]),
    ]
    later = []
    for one in range(2):
        for other in range(2):
            here = pl.ds(pl.multiple_of((2 * (z ^ one) + (core ^ other)) * ROWS, ROWS), ROWS)
            first.append(
                pltpu.make_async_copy(
                    (near, far)[other].at[2 * team + (z ^ one), 0:ROWS, :],
                    tokens.at[here, :],
                    tokens_arrived.at[2 * one + other],
                )
            )
            later.append(
                pltpu.make_async_copy(
                    (cot_near, cot_far)[other].at[one],
                    cot.at[here, :],
                    tokens_arrived.at[4 + 2 * one + other],
                )
            )
    loads = [
        [
            pltpu.make_async_copy(
                rows.at[place[5] ^ k],
                parts.at[3, k, lax.rem(place[4] + 4 - step, 4)],
                arrived.at[24 + 4 * k + step],
            )
            for k in range(2)
            for step, rows in enumerate((out0, out1, out2, out3))
        ]
    ]
    loads += [load_part(place, weights, parts, arrived, i) for i in range(3)]
    for load in [loads[0], first, *loads[1:], later]:
        for copy in load:
            copy.start()
    member = 2 * z + core
    row = lax.broadcasted_iota(jnp.int32, (TEAM_ROWS, 1), 0)
    live = (team * TEAM_ROWS + row) < length[0]
    own = (row // ROWS) == member
    finish(first)
    finish(loads[0])
    gain = norms[2:3, :]
    bias = norms[3:4, :]
    mixed_t = mixed_rows[...].reshape(D, TEAM_ROWS)
    w_out = parts[3].reshape(D, D)
    middle = tokens[...].astype(f32) + tn(mixed_t, w_out)
    scaled, inv = norm_parts(middle)
    normed = (scaled * gain + bias).astype(bf16)
    finish(loads[1])
    w_gate = parts[0].reshape(D, FF_PART)
    gate = nn(normed, w_gate)
    finish(loads[2])
    w_up = parts[1].reshape(D, FF_PART)
    up = nn(normed, w_up)
    finish(loads[3])
    finish(later)
    w_down = parts[2].reshape(FF_PART, D)
    d_out = jnp.where(live, cot[...].astype(f32), 0.0)
    d_out_low = d_out.astype(bf16)
    d_hidden = nt(d_out_low, w_down)
    sig = jax.nn.sigmoid(gate)
    act = gate * sig
    hidden = (act * up).astype(bf16)
    out_part = nn(hidden, w_down) + jnp.where(own, middle, 0.0)
    d_up = (d_hidden * act).astype(bf16)
    d_gate = (d_hidden * up * sig * (1.0 + gate * (1.0 - sig))).astype(bf16)
    d_normed = nt(d_gate, w_gate) + nt(d_up, w_up)

    leaving = []

    def send(source, target):
        copy = pltpu.make_async_copy(source, target, left.at[len(leaving)])
        copy.start()
        leaving.append(copy)

    def send_grad(i, grad):
        low = grad.astype(bf16)
        for k in range(2):
            for x in range(4):
                at = 64 * (4 * k + x)
                own_grads[i, x, k] = low[at : at + 64]
        send(own_grads.at[i], grads.at[:, :, :, D * i : D * (i + 1)])

    send_grad(2, tn(hidden, d_out_low))
    send_grad(0, tn(normed, d_gate))
    send_grad(1, tn(normed, d_up))
    d_middle = jnp.where(own, d_out, 0.0) + norm_back(d_normed, scaled, inv, gain)
    d_middle_low = d_middle.astype(bf16)
    own_sent[...] = nt(w_out, d_middle_low).astype(bf16).reshape(HEADS, HEAD, TEAM_ROWS)
    send(own_sent, sent)
    back[...] = d_middle_low
    ahead[...] = out_part.astype(bf16)
    for one in range(2):
        for target, other in ((own_kept, core), (swapped, 1 - core)):
            here = pl.ds(pl.multiple_of((2 * (z ^ one) + other) * ROWS, ROWS), ROWS)
            target[one, :, 0:D] = back[here, :]
            target[one, :, D : 2 * D] = ahead[here, :]
    send(own_kept, kept)
    send_grad(3, nn(mixed_t, d_middle_low))
    norm_rows[0:1, :] = jnp.sum(d_normed * scaled, 0, keepdims=True)
    norm_rows[1:2, :] = jnp.sum(d_normed, 0, keepdims=True)
    norm_rows[2:8, :] = jnp.zeros((6, D), f32)
    finish(leaving)


def add_kernel(kept, arrived, own, other):
    own[...] = (kept[0].astype(f32) + arrived[0].astype(f32)).astype(bf16)
    other[...] = (kept[1].astype(f32) + arrived[1].astype(f32)).astype(bf16)


def scale_kernel(place, near, far, other, scaled):
    for index in range(8):
        source, first = (near, far)[index // 4], 2 * (index % 4)
        x = source[first : first + 2, 0:ROWS, :].reshape(2 * ROWS, D).astype(f32)
        low = norm_parts(x)[0].astype(bf16)
        for one in range(2):
            block = block_of(place, first + one, index // 4)
            scaled[block] = low[one * ROWS : (one + 1) * ROWS]


def attend_back_kernel(
    place, length, d_mixed, q_in, k_in, v_in, o_in, lse_in, cos, sin, scaled, head_cols, norm_rows,
    sent, sent0, sent1, sent2, sent3,
    d_o, probs, d_scores, dq, dk, dv, table, normal, cos_now, sin_now, cols, norms, own_sent, here_now, left,
):
    loads = [
        pltpu.make_async_copy(source, target, here_now.at[i])
        for i, (source, target) in enumerate(
            (
                (cos, cos_now),
                (sin, sin_now),
                (scaled, normal),
                (head_cols.at[0:104, :], cols),
                (norm_rows, norms),
            )
        )
    ]
    for load in loads:
        load.start()
    for y in range(LEN // TEAM_ROWS):
        total = d_mixed[TEAM * y].astype(f32)
        for t in range(1, TEAM):
            total = total + d_mixed[TEAM * y + t].astype(f32)
        d_o[:, y * TEAM_ROWS : (y + 1) * TEAM_ROWS] = total.astype(bf16)
    keys_t = k_in[...]
    keys = key_columns(keys_t.astype(f32), length[0])
    ones = jnp.ones((4, LEN), f32)
    pad = jnp.zeros((128 - HEAD - 4, LEN), f32)
    values = jnp.concatenate([v_in[...].astype(f32), ones, pad], 0).T.astype(bf16)[:, :AUG]
    d_o_t = d_o[...]
    inner = jnp.sum(d_o_t.astype(f32) * o_in[...], 0, keepdims=True)
    zero_row = jnp.zeros((1, LEN), f32)
    one_row = jnp.ones((1, LEN), f32)
    q_rows = with_rows(q_in[...], [one_row] + split3(-lse_in[...]))
    do_rows = with_rows(d_o_t, [zero_row] + split3(-inner))
    tile = 512
    for i in range(LEN // tile):
        here = slice(i * tile, (i + 1) * tile)
        p = jnp.exp2(nn(keys, q_rows[:, here]))
        ds = (p * nn(values, do_rows[:, here])).astype(bf16)
        probs[:, here] = p.astype(bf16)
        d_scores[:, here] = ds
        dq[:, here] = nn(keys_t, ds) * SCALE
    dk[...] = nt(q_in[...], d_scores[...]) * LN2
    dv[...] = nt(d_o_t, probs[...])
    finish(loads)
    c = cos_now[...]
    s = sin_now[...]
    q1, q2 = dq[0:HALF], dq[HALF:HEAD]
    k1, k2 = dk[0:HALF], dk[HALF:HEAD]
    dq_t = jnp.concatenate([q1 * c + q2 * s, q2 * c - q1 * s], 0).astype(bf16)
    dk_t = jnp.concatenate([k1 * c + k2 * s, k2 * c - k1 * s], 0).astype(bf16)
    dv_t = dv[...].astype(bf16)
    for b in range(SEQ):
        here = slice(b * ROWS, (b + 1) * ROWS)
        own_sent[b, 0:32] = dq_t[:, here]
        own_sent[b, 32:64] = dk_t[:, here]
        own_sent[b, 64:96] = dv_t[:, here]
    leaving = pltpu.make_async_copy(own_sent, sent, left.at[0])
    leaving.start()
    d_lin = jnp.concatenate([dq_t, dk_t, dv_t], 0)
    product = nn(d_lin, normal[...].reshape(LEN, D))
    total = jnp.sum(d_lin.astype(f32), 1, keepdims=True)
    weights = cols[0:96, :]
    gain = cols[96:97, :]
    bias = cols[97:98, :]
    rows = [
        product * gain + total * bias,
        jnp.sum(product * weights, 0, keepdims=True),
        jnp.sum(total * weights, 0, keepdims=True),
        norms[0:2, :],
        jnp.zeros((28, D), f32),
    ]
    table[...] = jnp.concatenate(rows, 0).T
    for step, part in enumerate((sent0, sent1, sent2, sent3)):
        x = lax.rem(place[4] + step, 4)
        for k in range(2):
            at = pl.multiple_of((4 * k + x) * 64, 64)
            part[k] = table[pl.ds(at, 64), :].astype(bf16)
    leaving.wait()


def regroup_kernel(part0, part1, part2, part3, feed, sent):
    heads = part0[...].astype(f32)
    for part in (part1, part2, part3):
        heads = heads + part[...].astype(f32)
    total = jnp.concatenate([feed[...].astype(f32), heads.reshape(128, 128)], 1)
    for d in range(SEQ * 2):
        sent[d] = total[4 * d : 4 * d + 4].astype(bf16)


def input_grad_kernel(
    place, length, tokens, d_lin, weights, w0, w1, head_cols,
    grad_tokens, layer_output,
    parts, arrived,
):
    loads = [load_part(place, weights, parts, arrived, i) for i in range(3)]
    for load in loads:
        for copy in load:
            copy.start()
    seq = place[3]
    gain = head_cols[96:97, :]
    scaled, inv = norm_parts(tokens[0].astype(f32))
    d_t = jnp.zeros((D, ROWS), f32)
    for part, load in enumerate(loads):
        d_part = d_lin[:, part * HEAD : (part + 1) * HEAD, :].reshape(D, ROWS)
        finish(load)
        d_t = d_t + nn(parts[part].reshape(D, D), d_part)
    total = w0[...].astype(f32) + w1[...].astype(f32)
    grad_tokens[0] = total[:, 0:D] + norm_back(d_t.T, scaled, inv, gain)
    row = lax.broadcasted_iota(jnp.int32, (ROWS, 1), 0)
    live = (seq * ROWS + row) < length[0]
    layer_output[0] = jnp.where(live, total[:, D : 2 * D], 0.0).astype(bf16)


def sum_kernel(
    parts, gain1, bias1, grad_query, grad_key, grad_value, grad_output, gain2, bias2,
    grad_gate, grad_up, grad_down,
):
    members = []
    for t in range(TEAM):
        total = parts[t, :, :FEED_LANES].astype(f32)
        for other in range(1, 2 * SEQ // TEAM):
            total = total + parts[TEAM * other + t, :, :FEED_LANES].astype(f32)
        members.append(total)
        grad_down[4 * t : 4 * t + 4, :] = total[:, 1024:1536]
    grad_output[...] = sum(m[:, 1536:2048] for m in members)
    pieces = []
    for u in range(4):
        for at in (128 * u, 512 + 128 * u):
            pieces.append(jnp.concatenate([m[:, at : at + 128] for m in members], 1))
    wide = jnp.concatenate(pieces, 0)
    high = wide.astype(bf16)
    low = (wide - high.astype(f32)).astype(bf16)
    order = column_order()
    wide = nt(high, order) + nt(low, order)
    for u in range(4):
        here = slice(512 * u, 512 * (u + 1))
        grad_gate[:, here] = wide[8 * u : 8 * u + 4]
        grad_up[:, here] = wide[8 * u + 4 : 8 * u + 8]
    heads = [
        parts[h, :, FEED_LANES:].astype(f32) + parts[SEQ + h, :, FEED_LANES:].astype(f32)
        for h in range(HEADS)
    ]
    lane = lax.broadcasted_iota(jnp.int32, (4, 128), 1)
    row = lax.broadcasted_iota(jnp.int32, (4, 128), 0)
    for i, grad in enumerate((grad_query, grad_key, grad_value)):
        for u in range(4):
            tile = jnp.zeros((4, 128), f32)
            for r in range(4):
                moved = pltpu.roll(heads[4 * u + r], (HEAD * (r - i)) % 128, 1)
                tile = jnp.where(lane // HEAD == r, moved, tile)
            grad[:, 128 * u : 128 * (u + 1)] = tile
    norms = sum(heads)
    for n, grad in enumerate((gain1, bias1, gain2, bias2)):
        column = jnp.where(lane == row, norms[:, 96 + n : 97 + n], 0.0)
        grad[...] = jnp.sum(column, 0)[0:4]


def call(kernel, ins, outs, scratch=(), vmem=8, flops=0):
    places = {"V": pltpu.VMEM, "U": pltpu.VMEM, "H": pltpu.VMEM, "A": pl.ANY, "P": pl.ANY, "S": pltpu.SMEM}
    inner = pl.pallas_call(
        kernel,
        out_shape=tuple(
            (pltpu.VMEM if where == "V" else pltpu.HBM)(shape, kind) for shape, kind, where in outs
        ),
        in_specs=[pl.BlockSpec(memory_space=places[where]) for where in ins],
        out_specs=tuple(pl.BlockSpec(memory_space=places[where]) for _, _, where in outs),
        scratch_shapes=[
            pltpu.SemaphoreType.DMA((s,)) if isinstance(s, int) else pltpu.VMEM(*s) for s in scratch
        ],
        compiler_params=pltpu.CompilerParams(vmem_limit_bytes=vmem * 2**20),
        cost_estimate=pl.CostEstimate(flops=flops, bytes_accessed=0, transcendentals=0),
    )

    def run(*args):
        assert len(args) == len(ins)
        return inner(
            *(
                pltpu.with_memory_space_constraint(x, pltpu.HBM if where in "HA" else pltpu.VMEM)
                if where in "HAV"
                else x
                for x, where in zip(args, ins)
            )
        )

    return run


def rope_tables():
    freq = 10000.0 ** (-2.0 * np.arange(HALF) / HEAD)
    angles = freq[:, None] * np.arange(LEN)[None, :]
    return np.cos(angles).astype(np.float32), np.sin(angles).astype(np.float32)


def exchange(value, axes):
    return lax.all_to_all(value, axes, 0, 0, tiled=True)


def swap(value, axis):
    return lax.ppermute(value, axis, [(0, 1), (1, 0)])


def shift(value, by):
    return lax.ppermute(value, "x", [(i, (i + by) % 4) for i in range(4)])


def shards(
    tokens, lengths, norm1_gain, norm1_bias, w_query, w_key, w_value, w_output,
    norm2_gain, norm2_bias, w_gate, w_up, w_down, cotangent,
):
    y = lax.axis_index("y")
    z = lax.axis_index("z")
    core = lax.axis_index("core")
    place = jnp.stack([core, y, z, 4 * y + 2 * z + core, lax.axis_index("x"), lax.axis_index("z_lo")]).astype(jnp.int32)
    cos, sin = (jnp.asarray(table) for table in rope_tables())

    (packed,) = call(
        pack_kernel,
        "H" * 12,
        [((8, MSG_ROWS, D), bf16, "A")],
        [((8, MSG_ROWS - ROWS, D), bf16), 9],
    )(
        tokens, w_query, w_key, w_value, w_output, w_gate, w_up, w_down,
        norm1_gain, norm1_bias, norm2_gain, norm2_bias,
    )
    near = exchange(packed, CHIPS)
    cot_pair = jnp.concatenate([cotangent, swap(cotangent, "z")], 0)
    near = after(near, cot_pair, place=pltpu.VMEM)
    far = swap(near, "core")
    cot_far = swap(cot_pair, "core")

    feed_rows, heads, whole = call(
        unpack_kernel,
        "SPPP",
        [
            ((1, 64, FEED_LANES), bf16, "V"),
            ((DP, 64, 128), bf16, "H"),
            ((1, 64, 3 * D), bf16, "H"),
        ],
        [((2, 8, 48, D), bf16), 2],
    )(place, near, far, cot_far)
    head_cols = exchange(heads, WINDOWS).reshape(D, 128)
    feed_other = after(swap(feed_rows, "z_lo"), in_hbm(whole), place=pltpu.VMEM)
    feed_rows, out_rows = call(
        join_kernel, "UU", [((2, 64, 3 * D), bf16, "V"), ((2, 64, D), bf16, "V")]
    )(feed_rows, feed_other)
    feed_weights = lax.all_gather(feed_rows, "x")
    out_rows = [out_rows] + [shift(out_rows, step) for step in range(1, 4)]
    whole_other = swap(whole, "z_lo")

    sent, q_t, k_t, v_t, o_t, lse, head_cols = call(
        attend_kernel,
        "SSVVUHH",
        [
            ((SEQ, HEAD, TEAM_ROWS), bf16, "H"),
            ((HEAD, LEN), bf16, "A"),
            ((HEAD, LEN), bf16, "A"),
            ((HEAD, LEN), bf16, "A"),
            ((HEAD, LEN), f32, "H"),
            ((1, LEN), f32, "H"),
            ((128, D), f32, "A"),
        ],
        [
            ((HEAD, LEN), bf16),
            ((HEAD, LEN), bf16),
            ((HEAD, LEN), bf16),
            ((128, D), f32),
            4,
        ],
        vmem=24,
        flops=19 * 10**9,
    )(place, lengths, near, far, head_cols, cos, sin)
    sent = after(sent, whole_other, *out_rows[1:])
    (scaled,) = call(
        scale_kernel, "SUUA", [((SEQ, ROWS, D), bf16, "H")], vmem=12
    )(place, near, far, sent)
    mixed = exchange(sent, WINDOW)
    whole = jnp.concatenate([whole, whole_other], 0)

    d_sent, kept, swapped, grads, norm_rows = call(
        feed_kernel,
        "SSAPPAAAAAA" + "A" * 4,
        [
            ((HEADS, HEAD, TEAM_ROWS), bf16, "A"),
            ((2, ROWS, 2 * D), bf16, "A"),
            ((2, ROWS, 2 * D), bf16, "V"),
            ((4, 2, 64, FEED_LANES), bf16, "A"),
            ((8, D), f32, "H"),
        ],
        [
            ((HEADS, HEAD, TEAM_ROWS), bf16),
            ((TEAM_ROWS, D), bf16),
            ((TEAM_ROWS, D), bf16),
            ((8, D), f32),
            ((TEAM_ROWS, D), bf16),
            ((TEAM_ROWS, D), bf16),
            ((4, 2, 4, 64, 512), bf16),
            ((HEADS, HEAD, TEAM_ROWS), bf16),
            ((2, ROWS, 2 * D), bf16),
            ((4, 4, 2, 64, 512), bf16),
            32, 10, 6,
        ],
        vmem=28,
    )(
        place, lengths, mixed, near, far, cot_pair, cot_far, feed_weights, head_cols, whole, scaled,
        *out_rows,
    )
    d_mixed = exchange(d_sent, WINDOW)
    feed_grads = lax.psum_scatter(
        grads.reshape(D, FEED_LANES), "x", scatter_dimension=0, tiled=True
    )
    row_weights = lax.all_gather(after(whole, pltpu.with_memory_space_constraint(norm_rows, pltpu.HBM)), "x")
    w0, w1 = call(
        add_kernel, "HV", [((ROWS, 2 * D), bf16, "H")] * 2
    )(kept, swap(swapped, "core"))
    w1 = swap(w1, "z")

    lin_sent, *head_grads = call(
        attend_back_kernel,
        "SSVHHHHHAAAAA",
        [((SEQ, 96, ROWS), bf16, "A")] + [((2, 64, 128), bf16, "V")] * 4,
        [
            ((HEAD, LEN), bf16),
            ((LEN, LEN), bf16),
            ((LEN, LEN), bf16),
            ((HEAD, LEN), f32),
            ((HEAD, LEN), f32),
            ((HEAD, LEN), f32),
            ((D, 128), f32),
            ((SEQ, ROWS, D), bf16),
            ((HALF, LEN), f32),
            ((HALF, LEN), f32),
            ((104, D), f32),
            ((8, D), f32),
            ((SEQ, 96, ROWS), bf16),
            5, 1,
        ],
        vmem=42,
    )(place, lengths, d_mixed, q_t, k_t, v_t, o_t, lse, cos, sin, scaled, head_cols, norm_rows)
    lin_sent = after(lin_sent, w1)
    back = exchange(lin_sent, WINDOW)
    head_grads = [head_grads[0]] + [shift(head_grads[step], step) for step in range(1, 4)]
    (grad_sent,) = call(
        regroup_kernel,
        "UUUUH",
        [((2 * SEQ, 4, GRAD_LANES), bf16, "H")],
    )(*head_grads, feed_grads)
    grad_parts = exchange(after(grad_sent, back), SLICE)

    grad_tokens, layer_output = call(
        input_grad_kernel,
        "SSHVAHHH",
        [((1, ROWS, D), f32, "H"), ((1, ROWS, D), bf16, "H")],
        [((3, 2, 4, 64, 512), bf16), 24],
    )(place, lengths, tokens, back, row_weights, w0, w1, head_cols)
    weight_grads = call(
        sum_kernel,
        "V",
        [((4,), f32, "H")] * 2 + [((4, D), f32, "H")] * 4 + [((4,), f32, "H")] * 2
        + [((4, FF), f32, "H")] * 2 + [((16, D), f32, "H")],
    )(grad_parts)
    return (layer_output, grad_tokens) + tuple(weight_grads)


def solution(mesh):
    flat = P(ALL)
    rows = P(ALL, None)
    blocks = P(("z_lo", "x"), WINDOW, None)
    return jax.shard_map(
        shards,
        mesh=Mesh(mesh.devices.reshape(2, 4, 4, 2, 2), ALL),
        in_specs=(
            blocks, P(("z_lo", "x")), flat, flat, rows, rows, rows, rows, flat, flat, rows, rows, rows, blocks,
        ),
        out_specs=(
            blocks, blocks, flat, flat, rows, rows, rows, rows, flat, flat, rows, rows, rows,
        ),
        check_vma=False,
    )
```

```python
import math

import jax
import jax.numpy as jnp
import numpy as np
from jax import lax
from jax.experimental import pallas as pl
from jax.experimental.pallas import tpu as pltpu
from jax.sharding import Mesh
from jax.sharding import PartitionSpec as P

HEADS = 16
HEAD = 32
HALF = HEAD // 2
D = 512
FF = 2048
LEN = 2048
ROWS = 128
TEAM = 4
TEAM_ROWS = TEAM * ROWS
FF_PART = FF // TEAM
DEVICES = 128
SEQ = 16
DP = 8
KEY_CHUNK = 256
AUG = 48

EPS = 1e-05
MASKED = -1.0e9
SCALE = HEAD**-0.5
LOG2E = math.log2(math.e)
LN2 = math.log(2.0)

f32 = jnp.float32
bf16 = jnp.bfloat16
WINDOW = ("y", "z", "core")
CHIPS = ("y", "z")
SLICE = ("z_lo", "y", "z", "core")
WINDOWS = ("z_lo", "x")
ALL = ("z_lo", "x", "y", "z", "core")


def nn(a, b):
    return lax.dot_general(a, b, (((1,), (0,)), ((), ())), preferred_element_type=f32)


def nt(a, b):
    return lax.dot_general(a, b, (((1,), (1,)), ((), ())), preferred_element_type=f32)


def tn(a, b):
    return lax.dot_general(a, b, (((0,), (0,)), ((), ())), preferred_element_type=f32)


def norm_parts(x):
    centered = x - jnp.mean(x, -1, keepdims=True)
    inv = lax.rsqrt(jnp.mean(centered * centered, -1, keepdims=True) + EPS)
    return centered * inv, inv


def norm_back(grad, scaled, inv, gain):
    e = grad * gain
    return inv * (
        e - jnp.mean(e, -1, keepdims=True) - scaled * jnp.mean(e * scaled, -1, keepdims=True)
    )


def split3(row):
    hi = row.astype(bf16)
    rest = row - hi.astype(f32)
    mid = rest.astype(bf16)
    low = (rest - mid.astype(f32)).astype(bf16)
    return [hi.astype(f32), mid.astype(f32), low.astype(f32)]


def key_columns(keys_t, length):
    place = lax.broadcasted_iota(jnp.int32, (1, LEN), 1)
    mask = jnp.where(place < length, 0.0, MASKED).astype(f32)
    ones = jnp.ones((3, LEN), f32)
    pad = jnp.zeros((128 - HEAD - 4, LEN), f32)
    return jnp.concatenate([keys_t, mask, ones, pad], 0).T.astype(bf16)[:, :AUG]


def with_rows(data_t, rows):
    pad = jnp.zeros((AUG - HEAD - len(rows), data_t.shape[1]), f32)
    return jnp.concatenate([data_t.astype(f32)] + rows + [pad], 0).astype(bf16)


def in_hbm(value):
    return pltpu.with_memory_space_constraint(value, pltpu.HBM)


def after(value, *others, place=pltpu.HBM):
    def kernel(*refs):
        pass

    return pl.pallas_call(
        kernel,
        out_shape=place(value.shape, value.dtype),
        in_specs=[pl.BlockSpec(memory_space=pl.ANY)] * (1 + len(others)),
        out_specs=pl.BlockSpec(memory_space=pl.ANY),
        input_output_aliases={0: 0},
        compiler_params=pltpu.CompilerParams(vmem_limit_bytes=2**20),
        cost_estimate=pl.CostEstimate(flops=0, bytes_accessed=0, transcendentals=0),
    )(pltpu.with_memory_space_constraint(value, place), *others)


FEED_LANES = FF_PART * 3 + D
GRAD_LANES = FEED_LANES + 128
MSG_ROWS = ROWS + 48


def column_order():
    n = lax.broadcasted_iota(jnp.int32, (512, 1), 0)
    to = ((n >> 2) & 3) * 128 + (n >> 7) * 32 + ((n >> 4) & 7) * 4 + (n & 3)
    lane = lax.broadcasted_iota(jnp.int32, (512, 512), 1)
    return jnp.where(lane == to, 1.0, 0.0).astype(bf16)


def pack_kernel(
    tokens, w_query, w_key, w_value, w_output, w_gate, w_up, w_down, gain1, bias1, gain2, bias2,
    sent,
    rows, left,
):
    leaving = [
        pltpu.make_async_copy(tokens.at[0], sent.at[chip, 0:ROWS, :], left.at[chip])
        for chip in range(8)
    ]
    for copy in leaving:
        copy.start()
    narrow = [w[...].astype(f32) for w in (w_query, w_key, w_value)]
    gate = w_gate[...].astype(f32)
    up = w_up[...].astype(f32)
    down = w_down[...].astype(f32)
    pieces = []
    for u in range(4):
        here = slice(512 * u, 512 * (u + 1))
        pieces.append(jnp.concatenate([gate[:, here], up[:, here]], 0))
    wide = nn(jnp.concatenate(pieces, 0).astype(bf16), column_order())
    lane = lax.broadcasted_iota(jnp.int32, (4, 128), 1)
    row = lax.broadcasted_iota(jnp.int32, (4, 128), 0)
    norms = jnp.zeros((4, 128), f32)
    for n, ref in enumerate((gain1, bias1, gain2, bias2)):
        for i in range(4):
            value = ref[i : i + 1].astype(f32).reshape(1, 1)
            norms = norms + jnp.where((lane == 96 + n) & (row == i), value, 0.0)
    out = w_output[...].astype(f32)
    nothing = jnp.zeros((4, 512), f32)
    for z in range(2):
        mine = []
        for t in (2 * z, 2 * z + 1):
            cols = slice(128 * t, 128 * (t + 1))
            mine.append(jnp.concatenate([wide[8 * u : 8 * u + 4, cols] for u in range(4)], 1))
            mine.append(jnp.concatenate([wide[8 * u + 4 : 8 * u + 8, cols] for u in range(4)], 1))
            mine.append(down[4 * t : 4 * t + 4])
        mine = jnp.concatenate(mine + [out] + narrow, 0)
        for y in range(4):
            tile = slice(128 * y, 128 * (y + 1))
            heads = []
            for t in (2 * z, 2 * z + 1):
                q, k, v = (
                    pltpu.roll(w[:, tile], (HEAD * (i - t)) % 128, 1)
                    for i, w in enumerate(narrow)
                )
                heads.append(
                    jnp.where(
                        lane < 32, q, jnp.where(lane < 64, k, jnp.where(lane < 96, v, norms))
                    )
                )
            heads = jnp.concatenate(heads + [nothing[:, :256]], 1)
            low = jnp.concatenate([mine, heads, nothing], 0).astype(bf16)
            rows[2 * y + z] = low
    copy = pltpu.make_async_copy(rows, sent.at[:, ROWS:, :], left.at[8])
    copy.start()
    leaving.append(copy)
    finish(leaving)


def unpack_kernel(place, near, far, cot, feed, heads, whole, rows, arrived):
    loads = [
        pltpu.make_async_copy(source.at[:, ROWS:, :], rows.at[i], arrived.at[i])
        for i, source in enumerate((near, far))
    ]
    for load in loads:
        load.start()
    for load in loads:
        load.wait()
    second = place[0] == 1
    for group in range(4):
        blocks = []
        for chip in (2 * group, 2 * group + 1):
            own = rows[0, chip].astype(f32)
            other = rows[1, chip].astype(f32)
            blocks += [jnp.where(second, other, own), jnp.where(second, own, other)]
        here = slice(16 * group, 16 * (group + 1))
        for i in range(3):
            cols = jnp.concatenate(
                [
                    jnp.where(second, b[4 * (i + 3) : 4 * (i + 4)], b[4 * i : 4 * (i + 1)])
                    for b in blocks
                ],
                0,
            )
            feed[0, here, D * i : D * (i + 1)] = cols.astype(bf16)
        for i in range(4):
            cols = jnp.concatenate([b[4 * (i + 6) : 4 * (i + 7)] for b in blocks], 0).astype(bf16)
            if i == 0:
                feed[0, here, 3 * D : 4 * D] = cols
            else:
                whole[0, here, D * (i - 1) : D * i] = cols
        cols = jnp.concatenate(
            [jnp.where(second, b[40:44, 128:256], b[40:44, 0:128]) for b in blocks], 0
        )
        cols = cols.astype(bf16)
        for w in range(DP):
            heads[w, here, :] = cols


def join_kernel(own, other, feed, out):
    for i, rows in enumerate((own, other)):
        feed[i] = rows[0, :, 0 : 3 * D]
        out[i] = rows[0, :, 3 * D : 4 * D]


def block_of(place, chip, other):
    return 2 * chip + (place[0] ^ other)


def attend_kernel(
    place, length, near, far, head_cols, cos, sin,
    sent, q_out, k_out, v_out, o_out, lse_out, cols_out,
    q_t, k_t, v_t, own_cols, left,
):
    leaving = []

    def send(source, target):
        copy = pltpu.make_async_copy(source, target, left.at[len(leaving)])
        copy.start()
        leaving.append(copy)

    cols = head_cols[...].reshape(D, 128).astype(f32).T
    own_cols[...] = cols
    send(own_cols, cols_out)
    gain = cols[96:97, :]
    bias = cols[97:98, :]
    weights_t = cols[0:96, :].astype(bf16)
    for index in range(8):
        source, first = (near, far)[index // 4], 2 * (index % 4)
        x = source[first : first + 2, 0:ROWS, :].reshape(2 * ROWS, D).astype(f32)
        scaled, _ = norm_parts(x)
        normed = (scaled * gain + bias).astype(bf16)
        lin = nt(weights_t, normed)
        for one in range(2):
            block = block_of(place, first + one, index // 4)
            here = pl.ds(pl.multiple_of(block * ROWS, ROWS), ROWS)
            part = lin[:, one * ROWS : (one + 1) * ROWS]
            c = cos[:, here]
            s = sin[:, here]
            q1, q2 = part[0:16], part[16:32]
            k1, k2 = part[32:48], part[48:64]
            fold = SCALE * LOG2E
            q_t[:, here] = (
                jnp.concatenate([q1 * c - q2 * s, q2 * c + q1 * s], 0) * fold
            ).astype(bf16)
            k_t[:, here] = jnp.concatenate([k1 * c - k2 * s, k2 * c + k1 * s], 0).astype(bf16)
            v_t[:, here] = part[64:96].astype(bf16)
    send(q_t, q_out)
    send(k_t, k_out)
    send(v_t, v_out)
    keys = key_columns(k_t[...].astype(f32), length[0])
    one_row = jnp.ones((1, LEN), f32)
    values_t = with_rows(v_t[...], [one_row])
    queries_t = with_rows(q_t[...], [one_row])
    top = mixed = None
    for i in range(LEN // KEY_CHUNK):
        here = slice(i * KEY_CHUNK, (i + 1) * KEY_CHUNK)
        scores = nn(keys[here, :], queries_t)
        new_top = jnp.max(scores, axis=0, keepdims=True)
        if i:
            new_top = jnp.maximum(top, new_top)
        weights = jnp.exp2(scores - new_top).astype(bf16)
        added = nn(values_t[:, here], weights)
        mixed = mixed * jnp.exp2(top - new_top) + added if i else added
        top = new_top
    total = mixed[HEAD : HEAD + 1]
    out = mixed[:HEAD] / total
    o_out[...] = out
    lse_out[...] = top + jnp.log2(total)
    low = out.astype(bf16)
    for i in range(LEN // TEAM_ROWS):
        for t in range(TEAM):
            sent[TEAM * i + t] = low[:, i * TEAM_ROWS : (i + 1) * TEAM_ROWS]
    finish(leaving)


def load_part(place, weights, parts, arrived, i):
    return [
        pltpu.make_async_copy(
            weights.at[x, place[5] ^ k, :, 512 * i : 512 * (i + 1)],
            parts.at[i, k, x],
            arrived.at[8 * i + 4 * k + x],
        )
        for k in range(2)
        for x in range(4)
    ]


def finish(copies):
    for copy in copies:
        copy.wait()


def feed_kernel(
    place, length, mixed, near, far, cot_near, cot_far, weights, head_cols, other1, other2,
    out0, out1, out2, out3,
    sent, kept, swapped, grads, norm_rows,
    mixed_rows, tokens, cot, norms, back, ahead, parts, own_sent, own_kept, own_grads,
    arrived, tokens_arrived, left,
):
    core, team, z = place[0], place[1], place[2]
    first = [
        pltpu.make_async_copy(mixed, mixed_rows, tokens_arrived.at[8]),
        pltpu.make_async_copy(head_cols.at[96:104, :], norms, tokens_arrived.at[9]),
    ]
    later = []
    for one in range(2):
        for other in range(2):
            here = pl.ds(pl.multiple_of((2 * (z ^ one) + (core ^ other)) * ROWS, ROWS), ROWS)
            first.append(
                pltpu.make_async_copy(
                    (near, far)[other].at[2 * team + (z ^ one), 0:ROWS, :],
                    tokens.at[here, :],
                    tokens_arrived.at[2 * one + other],
                )
            )
            later.append(
                pltpu.make_async_copy(
                    (cot_near, cot_far)[other].at[one],
                    cot.at[here, :],
                    tokens_arrived.at[4 + 2 * one + other],
                )
            )
    loads = [
        [
            pltpu.make_async_copy(
                rows.at[place[5] ^ k],
                parts.at[3, k, lax.rem(place[4] + 4 - step, 4)],
                arrived.at[24 + 4 * k + step],
            )
            for k in range(2)
            for step, rows in enumerate((out0, out1, out2, out3))
        ]
    ]
    loads += [load_part(place, weights, parts, arrived, i) for i in range(3)]
    for load in [loads[0], first, *loads[1:], later]:
        for copy in load:
            copy.start()
    member = 2 * z + core
    row = lax.broadcasted_iota(jnp.int32, (TEAM_ROWS, 1), 0)
    live = (team * TEAM_ROWS + row) < length[0]
    own = (row // ROWS) == member
    finish(first)
    finish(loads[0])
    gain = norms[2:3, :]
    bias = norms[3:4, :]
    mixed_t = mixed_rows[...].reshape(D, TEAM_ROWS)
    w_out = parts[3].reshape(D, D)
    middle = tokens[...].astype(f32) + tn(mixed_t, w_out)
    scaled, inv = norm_parts(middle)
    normed = (scaled * gain + bias).astype(bf16)
    finish(loads[1])
    w_gate = parts[0].reshape(D, FF_PART)
    gate = nn(normed, w_gate)
    finish(loads[2])
    w_up = parts[1].reshape(D, FF_PART)
    up = nn(normed, w_up)
    finish(loads[3])
    finish(later)
    w_down = parts[2].reshape(FF_PART, D)
    d_out = jnp.where(live, cot[...].astype(f32), 0.0)
    d_out_low = d_out.astype(bf16)
    d_hidden = nt(d_out_low, w_down)
    sig = jax.nn.sigmoid(gate)
    act = gate * sig
    hidden = (act * up).astype(bf16)
    out_part = nn(hidden, w_down) + jnp.where(own, middle, 0.0)
    d_up = (d_hidden * act).astype(bf16)
    d_gate = (d_hidden * up * sig * (1.0 + gate * (1.0 - sig))).astype(bf16)
    d_normed = nt(d_gate, w_gate) + nt(d_up, w_up)

    leaving = []

    def send(source, target):
        copy = pltpu.make_async_copy(source, target, left.at[len(leaving)])
        copy.start()
        leaving.append(copy)

    def send_grad(i, grad):
        low = grad.astype(bf16)
        for k in range(2):
            for x in range(4):
                at = 64 * (4 * k + x)
                own_grads[i, x, k] = low[at : at + 64]
        send(own_grads.at[i], grads.at[:, :, :, D * i : D * (i + 1)])

    send_grad(2, tn(hidden, d_out_low))
    send_grad(0, tn(normed, d_gate))
    send_grad(1, tn(normed, d_up))
    d_middle = jnp.where(own, d_out, 0.0) + norm_back(d_normed, scaled, inv, gain)
    d_middle_low = d_middle.astype(bf16)
    own_sent[...] = nt(w_out, d_middle_low).astype(bf16).reshape(HEADS, HEAD, TEAM_ROWS)
    send(own_sent, sent)
    back[...] = d_middle_low
    ahead[...] = out_part.astype(bf16)
    for one in range(2):
        for target, other in ((own_kept, core), (swapped, 1 - core)):
            here = pl.ds(pl.multiple_of((2 * (z ^ one) + other) * ROWS, ROWS), ROWS)
            target[one, :, 0:D] = back[here, :]
            target[one, :, D : 2 * D] = ahead[here, :]
    send(own_kept, kept)
    send_grad(3, nn(mixed_t, d_middle_low))
    norm_rows[0:1, :] = jnp.sum(d_normed * scaled, 0, keepdims=True)
    norm_rows[1:2, :] = jnp.sum(d_normed, 0, keepdims=True)
    norm_rows[2:8, :] = jnp.zeros((6, D), f32)
    finish(leaving)


def add_kernel(kept, arrived, own, other):
    own[...] = (kept[0].astype(f32) + arrived[0].astype(f32)).astype(bf16)
    other[...] = (kept[1].astype(f32) + arrived[1].astype(f32)).astype(bf16)


def scale_kernel(place, near, far, other, scaled):
    for index in range(8):
        source, first = (near, far)[index // 4], 2 * (index % 4)
        x = source[first : first + 2, 0:ROWS, :].reshape(2 * ROWS, D).astype(f32)
        low = norm_parts(x)[0].astype(bf16)
        for one in range(2):
            block = block_of(place, first + one, index // 4)
            scaled[block] = low[one * ROWS : (one + 1) * ROWS]


def attend_back_kernel(
    place, length, d_mixed, q_in, k_in, v_in, o_in, lse_in, cos, sin, scaled, head_cols, norm_rows,
    sent, sent0, sent1, sent2, sent3,
    d_o, probs, d_scores, dq, dk, dv, table, normal, cos_now, sin_now, cols, norms, own_sent, here_now, left,
):
    loads = [
        pltpu.make_async_copy(source, target, here_now.at[i])
        for i, (source, target) in enumerate(
            (
                (cos, cos_now),
                (sin, sin_now),
                (scaled, normal),
                (head_cols.at[0:104, :], cols),
                (norm_rows, norms),
            )
        )
    ]
    for load in loads:
        load.start()
    for y in range(LEN // TEAM_ROWS):
        total = d_mixed[TEAM * y].astype(f32)
        for t in range(1, TEAM):
            total = total + d_mixed[TEAM * y + t].astype(f32)
        d_o[:, y * TEAM_ROWS : (y + 1) * TEAM_ROWS] = total.astype(bf16)
    keys_t = k_in[...]
    keys = key_columns(keys_t.astype(f32), length[0])
    ones = jnp.ones((4, LEN), f32)
    pad = jnp.zeros((128 - HEAD - 4, LEN), f32)
    values = jnp.concatenate([v_in[...].astype(f32), ones, pad], 0).T.astype(bf16)[:, :AUG]
    d_o_t = d_o[...]
    inner = jnp.sum(d_o_t.astype(f32) * o_in[...], 0, keepdims=True)
    zero_row = jnp.zeros((1, LEN), f32)
    one_row = jnp.ones((1, LEN), f32)
    q_rows = with_rows(q_in[...], [one_row] + split3(-lse_in[...]))
    do_rows = with_rows(d_o_t, [zero_row] + split3(-inner))
    tile = 512
    for i in range(LEN // tile):
        here = slice(i * tile, (i + 1) * tile)
        p = jnp.exp2(nn(keys, q_rows[:, here]))
        ds = (p * nn(values, do_rows[:, here])).astype(bf16)
        probs[:, here] = p.astype(bf16)
        d_scores[:, here] = ds
        dq[:, here] = nn(keys_t, ds) * SCALE
    dk[...] = nt(q_in[...], d_scores[...]) * LN2
    dv[...] = nt(d_o_t, probs[...])
    finish(loads)
    c = cos_now[...]
    s = sin_now[...]
    q1, q2 = dq[0:HALF], dq[HALF:HEAD]
    k1, k2 = dk[0:HALF], dk[HALF:HEAD]
    dq_t = jnp.concatenate([q1 * c + q2 * s, q2 * c - q1 * s], 0).astype(bf16)
    dk_t = jnp.concatenate([k1 * c + k2 * s, k2 * c - k1 * s], 0).astype(bf16)
    dv_t = dv[...].astype(bf16)
    for b in range(SEQ):
        here = slice(b * ROWS, (b + 1) * ROWS)
        own_sent[b, 0:32] = dq_t[:, here]
        own_sent[b, 32:64] = dk_t[:, here]
        own_sent[b, 64:96] = dv_t[:, here]
    leaving = pltpu.make_async_copy(own_sent, sent, left.at[0])
    leaving.start()
    d_lin = jnp.concatenate([dq_t, dk_t, dv_t], 0)
    product = nn(d_lin, normal[...].reshape(LEN, D))
    total = jnp.sum(d_lin.astype(f32), 1, keepdims=True)
    weights = cols[0:96, :]
    gain = cols[96:97, :]
    bias = cols[97:98, :]
    rows = [
        product * gain + total * bias,
        jnp.sum(product * weights, 0, keepdims=True),
        jnp.sum(total * weights, 0, keepdims=True),
        norms[0:2, :],
        jnp.zeros((28, D), f32),
    ]
    table[...] = jnp.concatenate(rows, 0).T
    for step, part in enumerate((sent0, sent1, sent2, sent3)):
        x = lax.rem(place[4] + step, 4)
        for k in range(2):
            at = pl.multiple_of((4 * k + x) * 64, 64)
            part[k] = table[pl.ds(at, 64), :].astype(bf16)
    leaving.wait()


def regroup_kernel(feed, sent):
    total = feed[...].astype(f32)
    for d in range(SEQ * 2):
        sent[d, :, :FEED_LANES] = total[4 * d : 4 * d + 4].astype(bf16)
        sent[d, :, FEED_LANES:] = jnp.zeros((4, 128), bf16)


def append_kernel(part0, part1, part2, part3, given, sent, rows, left):
    heads = part0[...].astype(f32)
    for part in (part1, part2, part3):
        heads = heads + part[...].astype(f32)
    heads = heads.reshape(128, 128)
    for d in range(SEQ * 2):
        rows[d] = heads[4 * d : 4 * d + 4].astype(bf16)
    copy = pltpu.make_async_copy(rows, sent.at[:, :, FEED_LANES:], left.at[0])
    copy.start()
    copy.wait()


def input_grad_kernel(
    place, length, tokens, d_lin, weights, w0, w1, head_cols,
    grad_tokens, layer_output,
    parts, arrived,
):
    loads = [load_part(place, weights, parts, arrived, i) for i in range(3)]
    for load in loads:
        for copy in load:
            copy.start()
    seq = place[3]
    gain = head_cols[96:97, :]
    scaled, inv = norm_parts(tokens[0].astype(f32))
    d_t = jnp.zeros((D, ROWS), f32)
    for part, load in enumerate(loads):
        d_part = d_lin[:, part * HEAD : (part + 1) * HEAD, :].reshape(D, ROWS)
        finish(load)
        d_t = d_t + nn(parts[part].reshape(D, D), d_part)
    total = w0[...].astype(f32) + w1[...].astype(f32)
    grad_tokens[0] = total[:, 0:D] + norm_back(d_t.T, scaled, inv, gain)
    row = lax.broadcasted_iota(jnp.int32, (ROWS, 1), 0)
    live = (seq * ROWS + row) < length[0]
    layer_output[0] = jnp.where(live, total[:, D : 2 * D], 0.0).astype(bf16)


def sum_kernel(
    parts, gain1, bias1, grad_query, grad_key, grad_value, grad_output, gain2, bias2,
    grad_gate, grad_up, grad_down,
):
    members = []
    for t in range(TEAM):
        total = parts[t, :, :FEED_LANES].astype(f32)
        for other in range(1, 2 * SEQ // TEAM):
            total = total + parts[TEAM * other + t, :, :FEED_LANES].astype(f32)
        members.append(total)
        grad_down[4 * t : 4 * t + 4, :] = total[:, 1024:1536]
    grad_output[...] = sum(m[:, 1536:2048] for m in members)
    pieces = []
    for u in range(4):
        for at in (128 * u, 512 + 128 * u):
            pieces.append(jnp.concatenate([m[:, at : at + 128] for m in members], 1))
    wide = jnp.concatenate(pieces, 0)
    high = wide.astype(bf16)
    low = (wide - high.astype(f32)).astype(bf16)
    order = column_order()
    wide = nt(high, order) + nt(low, order)
    for u in range(4):
        here = slice(512 * u, 512 * (u + 1))
        grad_gate[:, here] = wide[8 * u : 8 * u + 4]
        grad_up[:, here] = wide[8 * u + 4 : 8 * u + 8]
    heads = [
        parts[h, :, FEED_LANES:].astype(f32) + parts[SEQ + h, :, FEED_LANES:].astype(f32)
        for h in range(HEADS)
    ]
    lane = lax.broadcasted_iota(jnp.int32, (4, 128), 1)
    row = lax.broadcasted_iota(jnp.int32, (4, 128), 0)
    for i, grad in enumerate((grad_query, grad_key, grad_value)):
        for u in range(4):
            tile = jnp.zeros((4, 128), f32)
            for r in range(4):
                moved = pltpu.roll(heads[4 * u + r], (HEAD * (r - i)) % 128, 1)
                tile = jnp.where(lane // HEAD == r, moved, tile)
            grad[:, 128 * u : 128 * (u + 1)] = tile
    norms = sum(heads)
    for n, grad in enumerate((gain1, bias1, gain2, bias2)):
        column = jnp.where(lane == row, norms[:, 96 + n : 97 + n], 0.0)
        grad[...] = jnp.sum(column, 0)[0:4]


def call(kernel, ins, outs, scratch=(), vmem=8, flops=0, aliases={}):
    places = {"V": pltpu.VMEM, "U": pltpu.VMEM, "H": pltpu.VMEM, "A": pl.ANY, "P": pl.ANY, "S": pltpu.SMEM}
    inner = pl.pallas_call(
        kernel,
        out_shape=tuple(
            (pltpu.VMEM if where == "V" else pltpu.HBM)(shape, kind) for shape, kind, where in outs
        ),
        in_specs=[pl.BlockSpec(memory_space=places[where]) for where in ins],
        out_specs=tuple(pl.BlockSpec(memory_space=places[where]) for _, _, where in outs),
        scratch_shapes=[
            pltpu.SemaphoreType.DMA((s,)) if isinstance(s, int) else pltpu.VMEM(*s) for s in scratch
        ],
        input_output_aliases=aliases,
        compiler_params=pltpu.CompilerParams(vmem_limit_bytes=vmem * 2**20),
        cost_estimate=pl.CostEstimate(flops=flops, bytes_accessed=0, transcendentals=0),
    )

    def run(*args):
        assert len(args) == len(ins)
        return inner(
            *(
                pltpu.with_memory_space_constraint(x, pltpu.HBM if where in "HA" else pltpu.VMEM)
                if where in "HAV"
                else x
                for x, where in zip(args, ins)
            )
        )

    return run


def rope_tables():
    freq = 10000.0 ** (-2.0 * np.arange(HALF) / HEAD)
    angles = freq[:, None] * np.arange(LEN)[None, :]
    return np.cos(angles).astype(np.float32), np.sin(angles).astype(np.float32)


def exchange(value, axes):
    return lax.all_to_all(value, axes, 0, 0, tiled=True)


def swap(value, axis):
    return lax.ppermute(value, axis, [(0, 1), (1, 0)])


def shift(value, by):
    return lax.ppermute(value, "x", [(i, (i + by) % 4) for i in range(4)])


def shards(
    tokens, lengths, norm1_gain, norm1_bias, w_query, w_key, w_value, w_output,
    norm2_gain, norm2_bias, w_gate, w_up, w_down, cotangent,
):
    y = lax.axis_index("y")
    z = lax.axis_index("z")
    core = lax.axis_index("core")
    place = jnp.stack([core, y, z, 4 * y + 2 * z + core, lax.axis_index("x"), lax.axis_index("z_lo")]).astype(jnp.int32)
    cos, sin = (jnp.asarray(table) for table in rope_tables())

    (packed,) = call(
        pack_kernel,
        "H" * 12,
        [((8, MSG_ROWS, D), bf16, "A")],
        [((8, MSG_ROWS - ROWS, D), bf16), 9],
    )(
        tokens, w_query, w_key, w_value, w_output, w_gate, w_up, w_down,
        norm1_gain, norm1_bias, norm2_gain, norm2_bias,
    )
    near = exchange(packed, CHIPS)
    cot_pair = jnp.concatenate([cotangent, swap(cotangent, "z")], 0)
    near = after(near, cot_pair, place=pltpu.VMEM)
    far = swap(near, "core")
    cot_far = swap(cot_pair, "core")

    feed_rows, heads, whole = call(
        unpack_kernel,
        "SPPP",
        [
            ((1, 64, FEED_LANES), bf16, "V"),
            ((DP, 64, 128), bf16, "H"),
            ((1, 64, 3 * D), bf16, "H"),
        ],
        [((2, 8, 48, D), bf16), 2],
    )(place, near, far, cot_far)
    head_cols = exchange(heads, WINDOWS).reshape(D, 128)
    feed_other = after(swap(feed_rows, "z_lo"), in_hbm(whole), place=pltpu.VMEM)
    feed_rows, out_rows = call(
        join_kernel, "UU", [((2, 64, 3 * D), bf16, "V"), ((2, 64, D), bf16, "V")]
    )(feed_rows, feed_other)
    feed_weights = lax.all_gather(feed_rows, "x")
    out_rows = [out_rows] + [shift(out_rows, step) for step in range(1, 4)]
    whole_other = swap(whole, "z_lo")

    sent, q_t, k_t, v_t, o_t, lse, head_cols = call(
        attend_kernel,
        "SSVVUHH",
        [
            ((SEQ, HEAD, TEAM_ROWS), bf16, "H"),
            ((HEAD, LEN), bf16, "A"),
            ((HEAD, LEN), bf16, "A"),
            ((HEAD, LEN), bf16, "A"),
            ((HEAD, LEN), f32, "H"),
            ((1, LEN), f32, "H"),
            ((128, D), f32, "A"),
        ],
        [
            ((HEAD, LEN), bf16),
            ((HEAD, LEN), bf16),
            ((HEAD, LEN), bf16),
            ((128, D), f32),
            4,
        ],
        vmem=24,
        flops=19 * 10**9,
    )(place, lengths, near, far, head_cols, cos, sin)
    sent = after(sent, whole_other, *out_rows[1:])
    (scaled,) = call(
        scale_kernel, "SUUA", [((SEQ, ROWS, D), bf16, "H")], vmem=12
    )(place, near, far, sent)
    mixed = exchange(sent, WINDOW)
    whole = jnp.concatenate([whole, whole_other], 0)

    d_sent, kept, swapped, grads, norm_rows = call(
        feed_kernel,
        "SSAPPAAAAAA" + "A" * 4,
        [
            ((HEADS, HEAD, TEAM_ROWS), bf16, "A"),
            ((2, ROWS, 2 * D), bf16, "A"),
            ((2, ROWS, 2 * D), bf16, "V"),
            ((4, 2, 64, FEED_LANES), bf16, "A"),
            ((8, D), f32, "H"),
        ],
        [
            ((HEADS, HEAD, TEAM_ROWS), bf16),
            ((TEAM_ROWS, D), bf16),
            ((TEAM_ROWS, D), bf16),
            ((8, D), f32),
            ((TEAM_ROWS, D), bf16),
            ((TEAM_ROWS, D), bf16),
            ((4, 2, 4, 64, 512), bf16),
            ((HEADS, HEAD, TEAM_ROWS), bf16),
            ((2, ROWS, 2 * D), bf16),
            ((4, 4, 2, 64, 512), bf16),
            32, 10, 6,
        ],
        vmem=28,
    )(
        place, lengths, mixed, near, far, cot_pair, cot_far, feed_weights, head_cols, whole, scaled,
        *out_rows,
    )
    d_mixed = exchange(d_sent, WINDOW)
    row_weights = lax.all_gather(after(whole, in_hbm(norm_rows)), "x")
    feed_grads = lax.psum_scatter(
        grads.reshape(D, FEED_LANES), "x", scatter_dimension=0, tiled=True
    )
    w0, w1 = call(
        add_kernel, "HV", [((ROWS, 2 * D), bf16, "H")] * 2
    )(kept, swap(swapped, "core"))
    w1 = swap(w1, "z")

    lin_sent, *head_grads = call(
        attend_back_kernel,
        "SSVHHHHHAAAAA",
        [((SEQ, 96, ROWS), bf16, "A")] + [((2, 64, 128), bf16, "V")] * 4,
        [
            ((HEAD, LEN), bf16),
            ((LEN, LEN), bf16),
            ((LEN, LEN), bf16),
            ((HEAD, LEN), f32),
            ((HEAD, LEN), f32),
            ((HEAD, LEN), f32),
            ((D, 128), f32),
            ((SEQ, ROWS, D), bf16),
            ((HALF, LEN), f32),
            ((HALF, LEN), f32),
            ((104, D), f32),
            ((8, D), f32),
            ((SEQ, 96, ROWS), bf16),
            5, 1,
        ],
        vmem=42,
    )(place, lengths, d_mixed, q_t, k_t, v_t, o_t, lse, cos, sin, scaled, head_cols, norm_rows)
    lin_sent = after(lin_sent, w1)
    back = exchange(lin_sent, WINDOW)
    head_grads = [head_grads[0]] + [shift(head_grads[step], step) for step in range(1, 4)]
    (grad_sent,) = call(regroup_kernel, "H", [((2 * SEQ, 4, GRAD_LANES), bf16, "H")])(feed_grads)
    (grad_sent,) = call(
        append_kernel,
        "UUUUA",
        [((2 * SEQ, 4, GRAD_LANES), bf16, "A")],
        [((2 * SEQ, 4, 128), bf16), 1],
        aliases={4: 0},
    )(*head_grads, grad_sent)
    grad_parts = exchange(after(grad_sent, back), SLICE)

    grad_tokens, layer_output = call(
        input_grad_kernel,
        "SSHVAHHH",
        [((1, ROWS, D), f32, "H"), ((1, ROWS, D), bf16, "H")],
        [((3, 2, 4, 64, 512), bf16), 24],
    )(place, lengths, tokens, back, row_weights, w0, w1, head_cols)
    weight_grads = call(
        sum_kernel,
        "V",
        [((4,), f32, "H")] * 2 + [((4, D), f32, "H")] * 4 + [((4,), f32, "H")] * 2
        + [((4, FF), f32, "H")] * 2 + [((16, D), f32, "H")],
    )(grad_parts)
    return (layer_output, grad_tokens) + tuple(weight_grads)


def solution(mesh):
    flat = P(ALL)
    rows = P(ALL, None)
    blocks = P(("z_lo", "x"), WINDOW, None)
    return jax.shard_map(
        shards,
        mesh=Mesh(mesh.devices.reshape(2, 4, 4, 2, 2), ALL),
        in_specs=(
            blocks, P(("z_lo", "x")), flat, flat, rows, rows, rows, rows, flat, flat, rows, rows, rows, blocks,
        ),
        out_specs=(
            blocks, blocks, flat, flat, rows, rows, rows, rows, flat, flat, rows, rows, rows,
        ),
        check_vma=False,
    )
```

```python
import math

import jax
import jax.numpy as jnp
import numpy as np
from jax import lax
from jax.experimental import pallas as pl
from jax.experimental.pallas import tpu as pltpu
from jax.sharding import Mesh
from jax.sharding import PartitionSpec as P

HEADS = 16
HEAD = 32
HALF = HEAD // 2
D = 512
FF = 2048
LEN = 2048
ROWS = 128
TEAM = 4
TEAM_ROWS = TEAM * ROWS
FF_PART = FF // TEAM
DEVICES = 128
SEQ = 16
DP = 8
KEY_CHUNK = 256
AUG = 48

EPS = 1e-05
MASKED = -1.0e9
SCALE = HEAD**-0.5
LOG2E = math.log2(math.e)
LN2 = math.log(2.0)

f32 = jnp.float32
bf16 = jnp.bfloat16
WINDOW = ("y", "z", "core")
CHIPS = ("y", "z")
SLICE = ("z_lo", "y", "z", "core")
WINDOWS = ("z_lo", "x")
ALL = ("z_lo", "x", "y", "z", "core")


def nn(a, b):
    return lax.dot_general(a, b, (((1,), (0,)), ((), ())), preferred_element_type=f32)


def nt(a, b):
    return lax.dot_general(a, b, (((1,), (1,)), ((), ())), preferred_element_type=f32)


def tn(a, b):
    return lax.dot_general(a, b, (((0,), (0,)), ((), ())), preferred_element_type=f32)


def norm_parts(x):
    centered = x - jnp.mean(x, -1, keepdims=True)
    inv = lax.rsqrt(jnp.mean(centered * centered, -1, keepdims=True) + EPS)
    return centered * inv, inv


def norm_back(grad, scaled, inv, gain):
    e = grad * gain
    return inv * (
        e - jnp.mean(e, -1, keepdims=True) - scaled * jnp.mean(e * scaled, -1, keepdims=True)
    )


def split3(row):
    hi = row.astype(bf16)
    rest = row - hi.astype(f32)
    mid = rest.astype(bf16)
    low = (rest - mid.astype(f32)).astype(bf16)
    return [hi.astype(f32), mid.astype(f32), low.astype(f32)]


def key_columns(keys_t, length):
    place = lax.broadcasted_iota(jnp.int32, (1, LEN), 1)
    mask = jnp.where(place < length, 0.0, MASKED).astype(f32)
    ones = jnp.ones((3, LEN), f32)
    pad = jnp.zeros((128 - HEAD - 4, LEN), f32)
    return jnp.concatenate([keys_t, mask, ones, pad], 0).T.astype(bf16)[:, :AUG]


def with_rows(data_t, rows):
    pad = jnp.zeros((AUG - HEAD - len(rows), data_t.shape[1]), f32)
    return jnp.concatenate([data_t.astype(f32)] + rows + [pad], 0).astype(bf16)


def in_hbm(value):
    return pltpu.with_memory_space_constraint(value, pltpu.HBM)


def after(value, *others, place=pltpu.HBM):
    def kernel(*refs):
        pass

    return pl.pallas_call(
        kernel,
        out_shape=place(value.shape, value.dtype),
        in_specs=[pl.BlockSpec(memory_space=pl.ANY)] * (1 + len(others)),
        out_specs=pl.BlockSpec(memory_space=pl.ANY),
        input_output_aliases={0: 0},
        compiler_params=pltpu.CompilerParams(vmem_limit_bytes=2**20),
        cost_estimate=pl.CostEstimate(flops=0, bytes_accessed=0, transcendentals=0),
    )(pltpu.with_memory_space_constraint(value, place), *others)


FEED_LANES = FF_PART * 3 + D
GRAD_LANES = FEED_LANES + 128
MSG_ROWS = ROWS + 48


def column_order():
    n = lax.broadcasted_iota(jnp.int32, (512, 1), 0)
    to = ((n >> 2) & 3) * 128 + (n >> 7) * 32 + ((n >> 4) & 7) * 4 + (n & 3)
    lane = lax.broadcasted_iota(jnp.int32, (512, 512), 1)
    return jnp.where(lane == to, 1.0, 0.0).astype(bf16)


def pack_kernel(
    tokens, w_query, w_key, w_value, w_output, w_gate, w_up, w_down, gain1, bias1, gain2, bias2,
    sent,
    rows, left,
):
    leaving = [
        pltpu.make_async_copy(tokens.at[0], sent.at[chip, 0:ROWS, :], left.at[chip])
        for chip in range(8)
    ]
    for copy in leaving:
        copy.start()
    narrow = [w[...].astype(f32) for w in (w_query, w_key, w_value)]
    gate = w_gate[...].astype(f32)
    up = w_up[...].astype(f32)
    down = w_down[...].astype(f32)
    pieces = []
    for u in range(4):
        here = slice(512 * u, 512 * (u + 1))
        pieces.append(jnp.concatenate([gate[:, here], up[:, here]], 0))
    wide = nn(jnp.concatenate(pieces, 0).astype(bf16), column_order())
    lane = lax.broadcasted_iota(jnp.int32, (4, 128), 1)
    row = lax.broadcasted_iota(jnp.int32, (4, 128), 0)
    norms = jnp.zeros((4, 128), f32)
    for n, ref in enumerate((gain1, bias1, gain2, bias2)):
        for i in range(4):
            value = ref[i : i + 1].astype(f32).reshape(1, 1)
            norms = norms + jnp.where((lane == 96 + n) & (row == i), value, 0.0)
    out = w_output[...].astype(f32)
    nothing = jnp.zeros((4, 512), f32)
    for z in range(2):
        mine = []
        for t in (2 * z, 2 * z + 1):
            cols = slice(128 * t, 128 * (t + 1))
            mine.append(jnp.concatenate([wide[8 * u : 8 * u + 4, cols] for u in range(4)], 1))
            mine.append(jnp.concatenate([wide[8 * u + 4 : 8 * u + 8, cols] for u in range(4)], 1))
            mine.append(down[4 * t : 4 * t + 4])
        mine = jnp.concatenate(mine + [out] + narrow, 0)
        for y in range(4):
            tile = slice(128 * y, 128 * (y + 1))
            heads = []
            for t in (2 * z, 2 * z + 1):
                q, k, v = (
                    pltpu.roll(w[:, tile], (HEAD * (i - t)) % 128, 1)
                    for i, w in enumerate(narrow)
                )
                heads.append(
                    jnp.where(
                        lane < 32, q, jnp.where(lane < 64, k, jnp.where(lane < 96, v, norms))
                    )
                )
            heads = jnp.concatenate(heads + [nothing[:, :256]], 1)
            low = jnp.concatenate([mine, heads, nothing], 0).astype(bf16)
            rows[2 * y + z] = low
    copy = pltpu.make_async_copy(rows, sent.at[:, ROWS:, :], left.at[8])
    copy.start()
    leaving.append(copy)
    finish(leaving)


def rows_kernel(near, rows):
    rows[...] = near[:, ROWS:, :]


def unpack_kernel(place, near, far, feed, heads, whole):
    second = place[0] == 1
    for group in range(4):
        blocks = []
        for chip in (2 * group, 2 * group + 1):
            own = near[chip].astype(f32)
            other = far[chip].astype(f32)
            blocks += [jnp.where(second, other, own), jnp.where(second, own, other)]
        here = slice(16 * group, 16 * (group + 1))
        for i in range(3):
            cols = jnp.concatenate(
                [
                    jnp.where(second, b[4 * (i + 3) : 4 * (i + 4)], b[4 * i : 4 * (i + 1)])
                    for b in blocks
                ],
                0,
            )
            feed[0, here, D * i : D * (i + 1)] = cols.astype(bf16)
        for i in range(4):
            cols = jnp.concatenate([b[4 * (i + 6) : 4 * (i + 7)] for b in blocks], 0).astype(bf16)
            if i == 0:
                feed[0, here, 3 * D : 4 * D] = cols
            else:
                whole[0, here, D * (i - 1) : D * i] = cols
        cols = jnp.concatenate(
            [jnp.where(second, b[40:44, 128:256], b[40:44, 0:128]) for b in blocks], 0
        )
        cols = cols.astype(bf16)
        for w in range(DP):
            heads[w, here, :] = cols


def join_kernel(own, other, feed, out):
    for i, rows in enumerate((own, other)):
        feed[i] = rows[0, :, 0 : 3 * D]
        out[i] = rows[0, :, 3 * D : 4 * D]


def block_of(place, chip, other):
    return 2 * chip + (place[0] ^ other)


def attend_kernel(
    place, length, near, far, head_cols, cos, sin, other,
    sent, q_out, k_out, v_out, o_out, lse_out, cols_out,
    q_t, k_t, v_t, own_cols, left,
):
    leaving = []

    def send(source, target):
        copy = pltpu.make_async_copy(source, target, left.at[len(leaving)])
        copy.start()
        leaving.append(copy)

    cols = head_cols[...].reshape(D, 128).astype(f32).T
    own_cols[...] = cols
    send(own_cols, cols_out)
    gain = cols[96:97, :]
    bias = cols[97:98, :]
    weights_t = cols[0:96, :].astype(bf16)
    for index in range(8):
        source, first = (near, far)[index // 4], 2 * (index % 4)
        x = source[first : first + 2, 0:ROWS, :].reshape(2 * ROWS, D).astype(f32)
        scaled, _ = norm_parts(x)
        normed = (scaled * gain + bias).astype(bf16)
        lin = nt(weights_t, normed)
        for one in range(2):
            block = block_of(place, first + one, index // 4)
            here = pl.ds(pl.multiple_of(block * ROWS, ROWS), ROWS)
            part = lin[:, one * ROWS : (one + 1) * ROWS]
            c = cos[:, here]
            s = sin[:, here]
            q1, q2 = part[0:16], part[16:32]
            k1, k2 = part[32:48], part[48:64]
            fold = SCALE * LOG2E
            q_t[:, here] = (
                jnp.concatenate([q1 * c - q2 * s, q2 * c + q1 * s], 0) * fold
            ).astype(bf16)
            k_t[:, here] = jnp.concatenate([k1 * c - k2 * s, k2 * c + k1 * s], 0).astype(bf16)
            v_t[:, here] = part[64:96].astype(bf16)
    send(q_t, q_out)
    send(k_t, k_out)
    send(v_t, v_out)
    keys = key_columns(k_t[...].astype(f32), length[0])
    one_row = jnp.ones((1, LEN), f32)
    values_t = with_rows(v_t[...], [one_row])
    queries_t = with_rows(q_t[...], [one_row])
    top = mixed = None
    for i in range(LEN // KEY_CHUNK):
        here = slice(i * KEY_CHUNK, (i + 1) * KEY_CHUNK)
        scores = nn(keys[here, :], queries_t)
        new_top = jnp.max(scores, axis=0, keepdims=True)
        if i:
            new_top = jnp.maximum(top, new_top)
        weights = jnp.exp2(scores - new_top).astype(bf16)
        added = nn(values_t[:, here], weights)
        mixed = mixed * jnp.exp2(top - new_top) + added if i else added
        top = new_top
    total = mixed[HEAD : HEAD + 1]
    out = mixed[:HEAD] / total
    o_out[...] = out
    lse_out[...] = top + jnp.log2(total)
    low = out.astype(bf16)
    for i in range(LEN // TEAM_ROWS):
        for t in range(TEAM):
            sent[TEAM * i + t] = low[:, i * TEAM_ROWS : (i + 1) * TEAM_ROWS]
    finish(leaving)


def load_part(place, weights, parts, arrived, i):
    return [
        pltpu.make_async_copy(
            weights.at[x, place[5] ^ k, :, 512 * i : 512 * (i + 1)],
            parts.at[i, k, x],
            arrived.at[8 * i + 4 * k + x],
        )
        for k in range(2)
        for x in range(4)
    ]


def finish(copies):
    for copy in copies:
        copy.wait()


def feed_kernel(
    place, length, mixed, near, far, cot_near, cot_far, weights, head_cols, other1, other2,
    out0, out1, out2, out3,
    sent, kept, swapped, grads, norm_rows,
    mixed_rows, tokens, cot, norms, back, ahead, parts, own_sent, own_kept, own_grads,
    arrived, tokens_arrived, left,
):
    core, team, z = place[0], place[1], place[2]
    first = [
        pltpu.make_async_copy(mixed, mixed_rows, tokens_arrived.at[8]),
        pltpu.make_async_copy(head_cols.at[96:104, :], norms, tokens_arrived.at[9]),
    ]
    later = []
    for one in range(2):
        for other in range(2):
            here = pl.ds(pl.multiple_of((2 * (z ^ one) + (core ^ other)) * ROWS, ROWS), ROWS)
            first.append(
                pltpu.make_async_copy(
                    (near, far)[other].at[2 * team + (z ^ one), 0:ROWS, :],
                    tokens.at[here, :],
                    tokens_arrived.at[2 * one + other],
                )
            )
            later.append(
                pltpu.make_async_copy(
                    (cot_near, cot_far)[other].at[one],
                    cot.at[here, :],
                    tokens_arrived.at[4 + 2 * one + other],
                )
            )
    loads = [
        [
            pltpu.make_async_copy(
                rows.at[place[5] ^ k],
                parts.at[3, k, lax.rem(place[4] + 4 - step, 4)],
                arrived.at[24 + 4 * k + step],
            )
            for k in range(2)
            for step, rows in enumerate((out0, out1, out2, out3))
        ]
    ]
    loads += [load_part(place, weights, parts, arrived, i) for i in range(3)]
    for load in [loads[0], first, *loads[1:], later]:
        for copy in load:
            copy.start()
    member = 2 * z + core
    row = lax.broadcasted_iota(jnp.int32, (TEAM_ROWS, 1), 0)
    live = (team * TEAM_ROWS + row) < length[0]
    own = (row // ROWS) == member
    finish(first)
    finish(loads[0])
    gain = norms[2:3, :]
    bias = norms[3:4, :]
    mixed_t = mixed_rows[...].reshape(D, TEAM_ROWS)
    w_out = parts[3].reshape(D, D)
    middle = tokens[...].astype(f32) + tn(mixed_t, w_out)
    scaled, inv = norm_parts(middle)
    normed = (scaled * gain + bias).astype(bf16)
    finish(loads[1])
    w_gate = parts[0].reshape(D, FF_PART)
    gate = nn(normed, w_gate)
    finish(loads[2])
    w_up = parts[1].reshape(D, FF_PART)
    up = nn(normed, w_up)
    finish(loads[3])
    finish(later)
    w_down = parts[2].reshape(FF_PART, D)
    d_out = jnp.where(live, cot[...].astype(f32), 0.0)
    d_out_low = d_out.astype(bf16)
    d_hidden = nt(d_out_low, w_down)
    sig = jax.nn.sigmoid(gate)
    act = gate * sig
    hidden = (act * up).astype(bf16)
    out_part = nn(hidden, w_down) + jnp.where(own, middle, 0.0)
    d_up = (d_hidden * act).astype(bf16)
    d_gate = (d_hidden * up * sig * (1.0 + gate * (1.0 - sig))).astype(bf16)
    d_normed = nt(d_gate, w_gate) + nt(d_up, w_up)

    leaving = []

    def send(source, target):
        copy = pltpu.make_async_copy(source, target, left.at[len(leaving)])
        copy.start()
        leaving.append(copy)

    def send_grad(i, grad):
        low = grad.astype(bf16)
        for k in range(2):
            for x in range(4):
                at = 64 * (4 * k + x)
                own_grads[i, x, k] = low[at : at + 64]
        send(own_grads.at[i], grads.at[:, :, :, D * i : D * (i + 1)])

    send_grad(2, tn(hidden, d_out_low))
    send_grad(0, tn(normed, d_gate))
    send_grad(1, tn(normed, d_up))
    d_middle = jnp.where(own, d_out, 0.0) + norm_back(d_normed, scaled, inv, gain)
    d_middle_low = d_middle.astype(bf16)
    own_sent[...] = nt(w_out, d_middle_low).astype(bf16).reshape(HEADS, HEAD, TEAM_ROWS)
    send(own_sent, sent)
    back[...] = d_middle_low
    ahead[...] = out_part.astype(bf16)
    for one in range(2):
        for target, other in ((own_kept, core), (swapped, 1 - core)):
            here = pl.ds(pl.multiple_of((2 * (z ^ one) + other) * ROWS, ROWS), ROWS)
            target[one, :, 0:D] = back[here, :]
            target[one, :, D : 2 * D] = ahead[here, :]
    send(own_kept, kept)
    send_grad(3, nn(mixed_t, d_middle_low))
    norm_rows[0:1, :] = jnp.sum(d_normed * scaled, 0, keepdims=True)
    norm_rows[1:2, :] = jnp.sum(d_normed, 0, keepdims=True)
    norm_rows[2:8, :] = jnp.zeros((6, D), f32)
    finish(leaving)


def add_kernel(kept, arrived, own, other):
    own[...] = (kept[0].astype(f32) + arrived[0].astype(f32)).astype(bf16)
    other[...] = (kept[1].astype(f32) + arrived[1].astype(f32)).astype(bf16)


def scale_kernel(place, near, far, other, scaled):
    for index in range(8):
        source, first = (near, far)[index // 4], 2 * (index % 4)
        x = source[first : first + 2, 0:ROWS, :].reshape(2 * ROWS, D).astype(f32)
        low = norm_parts(x)[0].astype(bf16)
        for one in range(2):
            block = block_of(place, first + one, index // 4)
            scaled[block] = low[one * ROWS : (one + 1) * ROWS]


def attend_back_kernel(
    place, length, d_mixed, q_in, k_in, v_in, o_in, lse_in, cos, sin, scaled, head_cols, norm_rows,
    sent, sent0, sent1, sent2, sent3,
    d_o, probs, d_scores, dq, dk, dv, table, normal, cos_now, sin_now, cols, norms, own_sent, here_now, left,
):
    loads = [
        pltpu.make_async_copy(source, target, here_now.at[i])
        for i, (source, target) in enumerate(
            (
                (cos, cos_now),
                (sin, sin_now),
                (scaled, normal),
                (head_cols.at[0:104, :], cols),
                (norm_rows, norms),
            )
        )
    ]
    for load in loads:
        load.start()
    for y in range(LEN // TEAM_ROWS):
        total = d_mixed[TEAM * y].astype(f32)
        for t in range(1, TEAM):
            total = total + d_mixed[TEAM * y + t].astype(f32)
        d_o[:, y * TEAM_ROWS : (y + 1) * TEAM_ROWS] = total.astype(bf16)
    keys_t = k_in[...]
    keys = key_columns(keys_t.astype(f32), length[0])
    ones = jnp.ones((4, LEN), f32)
    pad = jnp.zeros((128 - HEAD - 4, LEN), f32)
    values = jnp.concatenate([v_in[...].astype(f32), ones, pad], 0).T.astype(bf16)[:, :AUG]
    d_o_t = d_o[...]
    inner = jnp.sum(d_o_t.astype(f32) * o_in[...], 0, keepdims=True)
    zero_row = jnp.zeros((1, LEN), f32)
    one_row = jnp.ones((1, LEN), f32)
    q_rows = with_rows(q_in[...], [one_row] + split3(-lse_in[...]))
    do_rows = with_rows(d_o_t, [zero_row] + split3(-inner))
    tile = 512
    for i in range(LEN // tile):
        here = slice(i * tile, (i + 1) * tile)
        p = jnp.exp2(nn(keys, q_rows[:, here]))
        ds = (p * nn(values, do_rows[:, here])).astype(bf16)
        probs[:, here] = p.astype(bf16)
        d_scores[:, here] = ds
        dq[:, here] = nn(keys_t, ds) * SCALE
    dk[...] = nt(q_in[...], d_scores[...]) * LN2
    dv[...] = nt(d_o_t, probs[...])
    finish(loads)
    c = cos_now[...]
    s = sin_now[...]
    q1, q2 = dq[0:HALF], dq[HALF:HEAD]
    k1, k2 = dk[0:HALF], dk[HALF:HEAD]
    dq_t = jnp.concatenate([q1 * c + q2 * s, q2 * c - q1 * s], 0).astype(bf16)
    dk_t = jnp.concatenate([k1 * c + k2 * s, k2 * c - k1 * s], 0).astype(bf16)
    dv_t = dv[...].astype(bf16)
    for b in range(SEQ):
        here = slice(b * ROWS, (b + 1) * ROWS)
        own_sent[b, 0:32] = dq_t[:, here]
        own_sent[b, 32:64] = dk_t[:, here]
        own_sent[b, 64:96] = dv_t[:, here]
    leaving = pltpu.make_async_copy(own_sent, sent, left.at[0])
    leaving.start()
    d_lin = jnp.concatenate([dq_t, dk_t, dv_t], 0)
    product = nn(d_lin, normal[...].reshape(LEN, D))
    total = jnp.sum(d_lin.astype(f32), 1, keepdims=True)
    weights = cols[0:96, :]
    gain = cols[96:97, :]
    bias = cols[97:98, :]
    rows = [
        product * gain + total * bias,
        jnp.sum(product * weights, 0, keepdims=True),
        jnp.sum(total * weights, 0, keepdims=True),
        norms[0:2, :],
        jnp.zeros((28, D), f32),
    ]
    table[...] = jnp.concatenate(rows, 0).T
    for step, part in enumerate((sent0, sent1, sent2, sent3)):
        x = lax.rem(place[4] + step, 4)
        for k in range(2):
            at = pl.multiple_of((4 * k + x) * 64, 64)
            part[k] = table[pl.ds(at, 64), :].astype(bf16)
    leaving.wait()


def regroup_kernel(feed, sent):
    total = feed[...].astype(f32)
    for d in range(SEQ * 2):
        sent[d, :, :FEED_LANES] = total[4 * d : 4 * d + 4].astype(bf16)
        sent[d, :, FEED_LANES:] = jnp.zeros((4, 128), bf16)


def append_kernel(part0, part1, part2, part3, given, sent, rows, left):
    heads = part0[...].astype(f32)
    for part in (part1, part2, part3):
        heads = heads + part[...].astype(f32)
    heads = heads.reshape(128, 128)
    for d in range(SEQ * 2):
        rows[d] = heads[4 * d : 4 * d + 4].astype(bf16)
    copy = pltpu.make_async_copy(rows, sent.at[:, :, FEED_LANES:], left.at[0])
    copy.start()
    copy.wait()


def input_grad_kernel(
    place, length, tokens, d_lin, weights, w0, w1, head_cols,
    grad_tokens, layer_output,
    parts, arrived,
):
    loads = [load_part(place, weights, parts, arrived, i) for i in range(3)]
    for load in loads:
        for copy in load:
            copy.start()
    seq = place[3]
    gain = head_cols[96:97, :]
    scaled, inv = norm_parts(tokens[0].astype(f32))
    d_t = jnp.zeros((D, ROWS), f32)
    for part, load in enumerate(loads):
        d_part = d_lin[:, part * HEAD : (part + 1) * HEAD, :].reshape(D, ROWS)
        finish(load)
        d_t = d_t + nn(parts[part].reshape(D, D), d_part)
    total = w0[...].astype(f32) + w1[...].astype(f32)
    grad_tokens[0] = total[:, 0:D] + norm_back(d_t.T, scaled, inv, gain)
    row = lax.broadcasted_iota(jnp.int32, (ROWS, 1), 0)
    live = (seq * ROWS + row) < length[0]
    layer_output[0] = jnp.where(live, total[:, D : 2 * D], 0.0).astype(bf16)


def sum_kernel(
    parts, gain1, bias1, grad_query, grad_key, grad_value, grad_output, gain2, bias2,
    grad_gate, grad_up, grad_down,
):
    members = []
    for t in range(TEAM):
        total = parts[t, :, :FEED_LANES].astype(f32)
        for other in range(1, 2 * SEQ // TEAM):
            total = total + parts[TEAM * other + t, :, :FEED_LANES].astype(f32)
        members.append(total)
        grad_down[4 * t : 4 * t + 4, :] = total[:, 1024:1536]
    grad_output[...] = sum(m[:, 1536:2048] for m in members)
    pieces = []
    for u in range(4):
        for at in (128 * u, 512 + 128 * u):
            pieces.append(jnp.concatenate([m[:, at : at + 128] for m in members], 1))
    wide = jnp.concatenate(pieces, 0)
    high = wide.astype(bf16)
    low = (wide - high.astype(f32)).astype(bf16)
    order = column_order()
    wide = nt(high, order) + nt(low, order)
    for u in range(4):
        here = slice(512 * u, 512 * (u + 1))
        grad_gate[:, here] = wide[8 * u : 8 * u + 4]
        grad_up[:, here] = wide[8 * u + 4 : 8 * u + 8]
    heads = [
        parts[h, :, FEED_LANES:].astype(f32) + parts[SEQ + h, :, FEED_LANES:].astype(f32)
        for h in range(HEADS)
    ]
    lane = lax.broadcasted_iota(jnp.int32, (4, 128), 1)
    row = lax.broadcasted_iota(jnp.int32, (4, 128), 0)
    for i, grad in enumerate((grad_query, grad_key, grad_value)):
        for u in range(4):
            tile = jnp.zeros((4, 128), f32)
            for r in range(4):
                moved = pltpu.roll(heads[4 * u + r], (HEAD * (r - i)) % 128, 1)
                tile = jnp.where(lane // HEAD == r, moved, tile)
            grad[:, 128 * u : 128 * (u + 1)] = tile
    norms = sum(heads)
    for n, grad in enumerate((gain1, bias1, gain2, bias2)):
        column = jnp.where(lane == row, norms[:, 96 + n : 97 + n], 0.0)
        grad[...] = jnp.sum(column, 0)[0:4]


def call(kernel, ins, outs, scratch=(), vmem=8, flops=0, aliases={}):
    places = {"V": pltpu.VMEM, "U": pltpu.VMEM, "H": pltpu.VMEM, "A": pl.ANY, "P": pl.ANY, "S": pltpu.SMEM}
    inner = pl.pallas_call(
        kernel,
        out_shape=tuple(
            (pltpu.VMEM if where == "V" else pltpu.HBM)(shape, kind) for shape, kind, where in outs
        ),
        in_specs=[pl.BlockSpec(memory_space=places[where]) for where in ins],
        out_specs=tuple(pl.BlockSpec(memory_space=places[where]) for _, _, where in outs),
        scratch_shapes=[
            pltpu.SemaphoreType.DMA((s,)) if isinstance(s, int) else pltpu.VMEM(*s) for s in scratch
        ],
        input_output_aliases=aliases,
        compiler_params=pltpu.CompilerParams(vmem_limit_bytes=vmem * 2**20),
        cost_estimate=pl.CostEstimate(flops=flops, bytes_accessed=0, transcendentals=0),
    )

    def run(*args):
        assert len(args) == len(ins)
        return inner(
            *(
                pltpu.with_memory_space_constraint(x, pltpu.HBM if where in "HA" else pltpu.VMEM)
                if where in "HAV"
                else x
                for x, where in zip(args, ins)
            )
        )

    return run


def rope_tables():
    freq = 10000.0 ** (-2.0 * np.arange(HALF) / HEAD)
    angles = freq[:, None] * np.arange(LEN)[None, :]
    return np.cos(angles).astype(np.float32), np.sin(angles).astype(np.float32)


def exchange(value, axes):
    return lax.all_to_all(value, axes, 0, 0, tiled=True)


def swap(value, axis):
    return lax.ppermute(value, axis, [(0, 1), (1, 0)])


def shift(value, by):
    return lax.ppermute(value, "x", [(i, (i + by) % 4) for i in range(4)])


def shards(
    tokens, lengths, norm1_gain, norm1_bias, w_query, w_key, w_value, w_output,
    norm2_gain, norm2_bias, w_gate, w_up, w_down, cotangent,
):
    y = lax.axis_index("y")
    z = lax.axis_index("z")
    core = lax.axis_index("core")
    place = jnp.stack([core, y, z, 4 * y + 2 * z + core, lax.axis_index("x"), lax.axis_index("z_lo")]).astype(jnp.int32)
    cos, sin = (jnp.asarray(table) for table in rope_tables())

    (packed,) = call(
        pack_kernel,
        "H" * 12,
        [((8, MSG_ROWS, D), bf16, "A")],
        [((8, MSG_ROWS - ROWS, D), bf16), 9],
    )(
        tokens, w_query, w_key, w_value, w_output, w_gate, w_up, w_down,
        norm1_gain, norm1_bias, norm2_gain, norm2_bias,
    )
    near = exchange(packed, CHIPS)
    cot_pair = jnp.concatenate([cotangent, swap(cotangent, "z")], 0)
    near = after(near, cot_pair, place=pltpu.VMEM)
    (near_rows,) = call(rows_kernel, "U", [((8, MSG_ROWS - ROWS, D), bf16, "V")])(near)
    far_rows = swap(near_rows, "core")

    feed_rows, heads, whole = call(
        unpack_kernel,
        "SUU",
        [
            ((1, 64, FEED_LANES), bf16, "V"),
            ((DP, 64, 128), bf16, "H"),
            ((1, 64, 3 * D), bf16, "H"),
        ],
    )(place, near_rows, far_rows)
    near = after(near, in_hbm(heads), place=pltpu.VMEM)
    far = swap(near, "core")
    cot_far = swap(cot_pair, "core")
    head_cols = exchange(heads, WINDOWS).reshape(D, 128)
    feed_other = after(swap(feed_rows, "z_lo"), in_hbm(whole), place=pltpu.VMEM)
    feed_rows, out_rows = call(
        join_kernel, "UU", [((2, 64, 3 * D), bf16, "H"), ((2, 64, D), bf16, "H")]
    )(feed_rows, feed_other)
    feed_weights = lax.all_gather(feed_rows, "x")
    out_rows = [out_rows] + [shift(out_rows, step) for step in range(1, 4)]
    whole_other = swap(whole, "z_lo")

    sent, q_t, k_t, v_t, o_t, lse, head_cols = call(
        attend_kernel,
        "SSVVUHHP",
        [
            ((SEQ, HEAD, TEAM_ROWS), bf16, "H"),
            ((HEAD, LEN), bf16, "A"),
            ((HEAD, LEN), bf16, "A"),
            ((HEAD, LEN), bf16, "A"),
            ((HEAD, LEN), f32, "H"),
            ((1, LEN), f32, "H"),
            ((128, D), f32, "A"),
        ],
        [
            ((HEAD, LEN), bf16),
            ((HEAD, LEN), bf16),
            ((HEAD, LEN), bf16),
            ((128, D), f32),
            4,
        ],
        vmem=24,
        flops=19 * 10**9,
    )(place, lengths, near, far, head_cols, cos, sin, cot_far)
    sent = after(sent, whole_other, *out_rows[1:])
    (scaled,) = call(
        scale_kernel, "SUUA", [((SEQ, ROWS, D), bf16, "H")], vmem=12
    )(place, near, far, sent)
    mixed = exchange(sent, WINDOW)
    whole = jnp.concatenate([whole, whole_other], 0)

    d_sent, kept, swapped, grads, norm_rows = call(
        feed_kernel,
        "SSAPPAAAAAA" + "A" * 4,
        [
            ((HEADS, HEAD, TEAM_ROWS), bf16, "A"),
            ((2, ROWS, 2 * D), bf16, "A"),
            ((2, ROWS, 2 * D), bf16, "V"),
            ((4, 2, 64, FEED_LANES), bf16, "A"),
            ((8, D), f32, "H"),
        ],
        [
            ((HEADS, HEAD, TEAM_ROWS), bf16),
            ((TEAM_ROWS, D), bf16),
            ((TEAM_ROWS, D), bf16),
            ((8, D), f32),
            ((TEAM_ROWS, D), bf16),
            ((TEAM_ROWS, D), bf16),
            ((4, 2, 4, 64, 512), bf16),
            ((HEADS, HEAD, TEAM_ROWS), bf16),
            ((2, ROWS, 2 * D), bf16),
            ((4, 4, 2, 64, 512), bf16),
            32, 10, 6,
        ],
        vmem=28,
    )(
        place, lengths, mixed, near, far, cot_pair, cot_far, feed_weights, head_cols, whole, scaled,
        *out_rows,
    )
    d_mixed = exchange(d_sent, WINDOW)
    row_weights = lax.all_gather(after(whole, in_hbm(norm_rows)), "x")
    feed_grads = lax.psum_scatter(
        grads.reshape(D, FEED_LANES), "x", scatter_dimension=0, tiled=True
    )
    w0, w1 = call(
        add_kernel, "HV", [((ROWS, 2 * D), bf16, "H")] * 2
    )(kept, swap(swapped, "core"))
    w1 = swap(w1, "z")

    lin_sent, *head_grads = call(
        attend_back_kernel,
        "SSVHHHHHAAAAA",
        [((SEQ, 96, ROWS), bf16, "A")] + [((2, 64, 128), bf16, "V")] * 4,
        [
            ((HEAD, LEN), bf16),
            ((LEN, LEN), bf16),
            ((LEN, LEN), bf16),
            ((HEAD, LEN), f32),
            ((HEAD, LEN), f32),
            ((HEAD, LEN), f32),
            ((D, 128), f32),
            ((SEQ, ROWS, D), bf16),
            ((HALF, LEN), f32),
            ((HALF, LEN), f32),
            ((104, D), f32),
            ((8, D), f32),
            ((SEQ, 96, ROWS), bf16),
            5, 1,
        ],
        vmem=42,
    )(place, lengths, d_mixed, q_t, k_t, v_t, o_t, lse, cos, sin, scaled, head_cols, norm_rows)
    lin_sent = after(lin_sent, w1)
    back = exchange(lin_sent, WINDOW)
    head_grads = [head_grads[0]] + [shift(head_grads[step], step) for step in range(1, 4)]
    (grad_sent,) = call(regroup_kernel, "H", [((2 * SEQ, 4, GRAD_LANES), bf16, "H")])(feed_grads)
    (grad_sent,) = call(
        append_kernel,
        "UUUUA",
        [((2 * SEQ, 4, GRAD_LANES), bf16, "A")],
        [((2 * SEQ, 4, 128), bf16), 1],
        aliases={4: 0},
    )(*head_grads, grad_sent)
    grad_parts = exchange(after(grad_sent, back), SLICE)

    grad_tokens, layer_output = call(
        input_grad_kernel,
        "SSHVAHHH",
        [((1, ROWS, D), f32, "H"), ((1, ROWS, D), bf16, "H")],
        [((3, 2, 4, 64, 512), bf16), 24],
    )(place, lengths, tokens, back, row_weights, w0, w1, head_cols)
    weight_grads = call(
        sum_kernel,
        "V",
        [((4,), f32, "H")] * 2 + [((4, D), f32, "H")] * 4 + [((4,), f32, "H")] * 2
        + [((4, FF), f32, "H")] * 2 + [((16, D), f32, "H")],
    )(grad_parts)
    return (layer_output, grad_tokens) + tuple(weight_grads)


def solution(mesh):
    flat = P(ALL)
    rows = P(ALL, None)
    blocks = P(("z_lo", "x"), WINDOW, None)
    return jax.shard_map(
        shards,
        mesh=Mesh(mesh.devices.reshape(2, 4, 4, 2, 2), ALL),
        in_specs=(
            blocks, P(("z_lo", "x")), flat, flat, rows, rows, rows, rows, flat, flat, rows, rows, rows, blocks,
        ),
        out_specs=(
            blocks, blocks, flat, flat, rows, rows, rows, rows, flat, flat, rows, rows, rows,
        ),
        check_vma=False,
    )
```

```python
import math

import jax
import jax.numpy as jnp
import numpy as np
from jax import lax
from jax.experimental import pallas as pl
from jax.experimental.pallas import tpu as pltpu
from jax.sharding import Mesh
from jax.sharding import PartitionSpec as P

HEADS = 16
HEAD = 32
HALF = HEAD // 2
D = 512
FF = 2048
LEN = 2048
ROWS = 128
TEAM = 4
TEAM_ROWS = TEAM * ROWS
FF_PART = FF // TEAM
DEVICES = 128
SEQ = 16
DP = 8
KEY_CHUNK = 256
AUG = 48

EPS = 1e-05
MASKED = -1.0e9
SCALE = HEAD**-0.5
LOG2E = math.log2(math.e)
LN2 = math.log(2.0)

f32 = jnp.float32
bf16 = jnp.bfloat16
WINDOW = ("y", "z", "core")
CHIPS = ("y", "z")
SLICE = ("z_lo", "y", "z", "core")
WINDOWS = ("z_lo", "x")
ALL = ("z_lo", "x", "y", "z", "core")


def nn(a, b):
    return lax.dot_general(a, b, (((1,), (0,)), ((), ())), preferred_element_type=f32)


def nt(a, b):
    return lax.dot_general(a, b, (((1,), (1,)), ((), ())), preferred_element_type=f32)


def tn(a, b):
    return lax.dot_general(a, b, (((0,), (0,)), ((), ())), preferred_element_type=f32)


def norm_parts(x):
    centered = x - jnp.mean(x, -1, keepdims=True)
    inv = lax.rsqrt(jnp.mean(centered * centered, -1, keepdims=True) + EPS)
    return centered * inv, inv


def norm_back(grad, scaled, inv, gain):
    e = grad * gain
    return inv * (
        e - jnp.mean(e, -1, keepdims=True) - scaled * jnp.mean(e * scaled, -1, keepdims=True)
    )


def split3(row):
    hi = row.astype(bf16)
    rest = row - hi.astype(f32)
    mid = rest.astype(bf16)
    low = (rest - mid.astype(f32)).astype(bf16)
    return [hi.astype(f32), mid.astype(f32), low.astype(f32)]


def key_columns(keys_t, length):
    place = lax.broadcasted_iota(jnp.int32, (1, LEN), 1)
    mask = jnp.where(place < length, 0.0, MASKED).astype(f32)
    ones = jnp.ones((3, LEN), f32)
    pad = jnp.zeros((128 - HEAD - 4, LEN), f32)
    return jnp.concatenate([keys_t, mask, ones, pad], 0).T.astype(bf16)[:, :AUG]


def with_rows(data_t, rows):
    pad = jnp.zeros((AUG - HEAD - len(rows), data_t.shape[1]), f32)
    return jnp.concatenate([data_t.astype(f32)] + rows + [pad], 0).astype(bf16)


def in_hbm(value):
    return pltpu.with_memory_space_constraint(value, pltpu.HBM)


def after(value, *others, place=pltpu.HBM):
    def kernel(*refs):
        pass

    return pl.pallas_call(
        kernel,
        out_shape=place(value.shape, value.dtype),
        in_specs=[pl.BlockSpec(memory_space=pl.ANY)] * (1 + len(others)),
        out_specs=pl.BlockSpec(memory_space=pl.ANY),
        input_output_aliases={0: 0},
        compiler_params=pltpu.CompilerParams(vmem_limit_bytes=2**20),
        cost_estimate=pl.CostEstimate(flops=0, bytes_accessed=0, transcendentals=0),
    )(pltpu.with_memory_space_constraint(value, place), *others)


FEED_LANES = FF_PART * 3 + D
GRAD_LANES = FEED_LANES + 128
MSG_ROWS = ROWS + 48


def column_order():
    n = lax.broadcasted_iota(jnp.int32, (512, 1), 0)
    to = ((n >> 2) & 3) * 128 + (n >> 7) * 32 + ((n >> 4) & 7) * 4 + (n & 3)
    lane = lax.broadcasted_iota(jnp.int32, (512, 512), 1)
    return jnp.where(lane == to, 1.0, 0.0).astype(bf16)


def pack_kernel(
    tokens, w_query, w_key, w_value, w_output, w_gate, w_up, w_down, gain1, bias1, gain2, bias2,
    sent,
    rows, left,
):
    leaving = [
        pltpu.make_async_copy(tokens.at[0], sent.at[chip, 0:ROWS, :], left.at[chip])
        for chip in range(8)
    ]
    for copy in leaving:
        copy.start()
    narrow = [w[...].astype(f32) for w in (w_query, w_key, w_value)]
    gate = w_gate[...].astype(f32)
    up = w_up[...].astype(f32)
    down = w_down[...].astype(f32)
    pieces = []
    for u in range(4):
        here = slice(512 * u, 512 * (u + 1))
        pieces.append(jnp.concatenate([gate[:, here], up[:, here]], 0))
    wide = nn(jnp.concatenate(pieces, 0).astype(bf16), column_order())
    lane = lax.broadcasted_iota(jnp.int32, (4, 128), 1)
    row = lax.broadcasted_iota(jnp.int32, (4, 128), 0)
    norms = jnp.zeros((4, 128), f32)
    for n, ref in enumerate((gain1, bias1, gain2, bias2)):
        for i in range(4):
            value = ref[i : i + 1].astype(f32).reshape(1, 1)
            norms = norms + jnp.where((lane == 96 + n) & (row == i), value, 0.0)
    out = w_output[...].astype(f32)
    nothing = jnp.zeros((4, 512), f32)
    for z in range(2):
        mine = []
        for t in (2 * z, 2 * z + 1):
            cols = slice(128 * t, 128 * (t + 1))
            mine.append(jnp.concatenate([wide[8 * u : 8 * u + 4, cols] for u in range(4)], 1))
            mine.append(jnp.concatenate([wide[8 * u + 4 : 8 * u + 8, cols] for u in range(4)], 1))
            mine.append(down[4 * t : 4 * t + 4])
        mine = jnp.concatenate(mine + [out] + narrow, 0)
        for y in range(4):
            tile = slice(128 * y, 128 * (y + 1))
            heads = []
            for t in (2 * z, 2 * z + 1):
                q, k, v = (
                    pltpu.roll(w[:, tile], (HEAD * (i - t)) % 128, 1)
                    for i, w in enumerate(narrow)
                )
                heads.append(
                    jnp.where(
                        lane < 32, q, jnp.where(lane < 64, k, jnp.where(lane < 96, v, norms))
                    )
                )
            heads = jnp.concatenate(heads + [nothing[:, :256]], 1)
            low = jnp.concatenate([mine, heads, nothing], 0).astype(bf16)
            rows[2 * y + z] = low
    copy = pltpu.make_async_copy(rows, sent.at[:, ROWS:, :], left.at[8])
    copy.start()
    leaving.append(copy)
    finish(leaving)


def rows_kernel(near, rows):
    rows[...] = near[:, ROWS:, :]


def unpack_kernel(place, near, far, feed, heads, whole):
    second = place[0] == 1
    for group in range(4):
        blocks = []
        for chip in (2 * group, 2 * group + 1):
            own = near[chip].astype(f32)
            other = far[chip].astype(f32)
            blocks += [jnp.where(second, other, own), jnp.where(second, own, other)]
        here = slice(16 * group, 16 * (group + 1))
        for i in range(3):
            cols = jnp.concatenate(
                [
                    jnp.where(second, b[4 * (i + 3) : 4 * (i + 4)], b[4 * i : 4 * (i + 1)])
                    for b in blocks
                ],
                0,
            )
            feed[0, here, D * i : D * (i + 1)] = cols.astype(bf16)
        for i in range(4):
            cols = jnp.concatenate([b[4 * (i + 6) : 4 * (i + 7)] for b in blocks], 0).astype(bf16)
            if i == 0:
                feed[0, here, 3 * D : 4 * D] = cols
            else:
                whole[0, here, D * (i - 1) : D * i] = cols
        cols = jnp.concatenate(
            [jnp.where(second, b[40:44, 128:256], b[40:44, 0:128]) for b in blocks], 0
        )
        cols = cols.astype(bf16)
        for w in range(DP):
            heads[w, here, :] = cols


def join_kernel(own, other, feed):
    feed[0] = own[0]
    feed[1] = other[0]


def block_of(place, chip, other):
    return 2 * chip + (place[0] ^ other)


def attend_kernel(
    place, length, near, far, head_cols, cos, sin, other,
    sent, q_out, k_out, v_out, o_out, lse_out, cols_out,
    q_t, k_t, v_t, own_cols, left,
):
    leaving = []

    def send(source, target):
        copy = pltpu.make_async_copy(source, target, left.at[len(leaving)])
        copy.start()
        leaving.append(copy)

    cols = head_cols[...].reshape(D, 128).astype(f32).T
    own_cols[...] = cols
    send(own_cols, cols_out)
    gain = cols[96:97, :]
    bias = cols[97:98, :]
    weights_t = cols[0:96, :].astype(bf16)
    for index in range(8):
        source, first = (near, far)[index // 4], 2 * (index % 4)
        x = source[first : first + 2, 0:ROWS, :].reshape(2 * ROWS, D).astype(f32)
        scaled, _ = norm_parts(x)
        normed = (scaled * gain + bias).astype(bf16)
        lin = nt(weights_t, normed)
        for one in range(2):
            block = block_of(place, first + one, index // 4)
            here = pl.ds(pl.multiple_of(block * ROWS, ROWS), ROWS)
            part = lin[:, one * ROWS : (one + 1) * ROWS]
            c = cos[:, here]
            s = sin[:, here]
            q1, q2 = part[0:16], part[16:32]
            k1, k2 = part[32:48], part[48:64]
            fold = SCALE * LOG2E
            q_t[:, here] = (
                jnp.concatenate([q1 * c - q2 * s, q2 * c + q1 * s], 0) * fold
            ).astype(bf16)
            k_t[:, here] = jnp.concatenate([k1 * c - k2 * s, k2 * c + k1 * s], 0).astype(bf16)
            v_t[:, here] = part[64:96].astype(bf16)
    send(q_t, q_out)
    send(k_t, k_out)
    send(v_t, v_out)
    keys = key_columns(k_t[...].astype(f32), length[0])
    one_row = jnp.ones((1, LEN), f32)
    values_t = with_rows(v_t[...], [one_row])
    queries_t = with_rows(q_t[...], [one_row])
    top = mixed = None
    for i in range(LEN // KEY_CHUNK):
        here = slice(i * KEY_CHUNK, (i + 1) * KEY_CHUNK)
        scores = nn(keys[here, :], queries_t)
        new_top = jnp.max(scores, axis=0, keepdims=True)
        if i:
            new_top = jnp.maximum(top, new_top)
        weights = jnp.exp2(scores - new_top).astype(bf16)
        added = nn(values_t[:, here], weights)
        mixed = mixed * jnp.exp2(top - new_top) + added if i else added
        top = new_top
    total = mixed[HEAD : HEAD + 1]
    out = mixed[:HEAD] / total
    o_out[...] = out
    lse_out[...] = top + jnp.log2(total)
    low = out.astype(bf16)
    for i in range(LEN // TEAM_ROWS):
        for t in range(TEAM):
            sent[TEAM * i + t] = low[:, i * TEAM_ROWS : (i + 1) * TEAM_ROWS]
    finish(leaving)


def load_part(place, weights, parts, arrived, i):
    return [
        pltpu.make_async_copy(
            rows.at[place[5] ^ k, :, 512 * i : 512 * (i + 1)],
            parts.at[i, k, lax.rem(place[4] + 4 - step, 4)],
            arrived.at[8 * i + 4 * k + step],
        )
        for k in range(2)
        for step, rows in enumerate(weights)
    ]


def finish(copies):
    for copy in copies:
        copy.wait()


def feed_kernel(
    place, length, mixed, near, far, cot_near, cot_far, head_cols, other1, other2,
    rows0, rows1, rows2, rows3,
    sent, kept, swapped, grads0, grads1, grads2, grads3, norm_rows,
    mixed_rows, tokens, cot, norms, back, ahead, parts, own_sent, own_kept, own_grads,
    arrived, tokens_arrived, left,
):
    core, team, z = place[0], place[1], place[2]
    first = [
        pltpu.make_async_copy(mixed, mixed_rows, tokens_arrived.at[8]),
        pltpu.make_async_copy(head_cols.at[96:104, :], norms, tokens_arrived.at[9]),
    ]
    later = []
    for one in range(2):
        for other in range(2):
            here = pl.ds(pl.multiple_of((2 * (z ^ one) + (core ^ other)) * ROWS, ROWS), ROWS)
            first.append(
                pltpu.make_async_copy(
                    (near, far)[other].at[2 * team + (z ^ one), 0:ROWS, :],
                    tokens.at[here, :],
                    tokens_arrived.at[2 * one + other],
                )
            )
            later.append(
                pltpu.make_async_copy(
                    (cot_near, cot_far)[other].at[one],
                    cot.at[here, :],
                    tokens_arrived.at[4 + 2 * one + other],
                )
            )
    weights = (rows0, rows1, rows2, rows3)
    loads = [load_part(place, weights, parts, arrived, i) for i in (3, 0, 1, 2)]
    for load in [loads[0], first, *loads[1:], later]:
        for copy in load:
            copy.start()
    member = 2 * z + core
    row = lax.broadcasted_iota(jnp.int32, (TEAM_ROWS, 1), 0)
    live = (team * TEAM_ROWS + row) < length[0]
    own = (row // ROWS) == member
    finish(first)
    finish(loads[0])
    gain = norms[2:3, :]
    bias = norms[3:4, :]
    mixed_t = mixed_rows[...].reshape(D, TEAM_ROWS)
    w_out = parts[3].reshape(D, D)
    middle = tokens[...].astype(f32) + tn(mixed_t, w_out)
    scaled, inv = norm_parts(middle)
    normed = (scaled * gain + bias).astype(bf16)
    finish(loads[1])
    w_gate = parts[0].reshape(D, FF_PART)
    gate = nn(normed, w_gate)
    finish(loads[2])
    w_up = parts[1].reshape(D, FF_PART)
    up = nn(normed, w_up)
    finish(loads[3])
    finish(later)
    w_down = parts[2].reshape(FF_PART, D)
    d_out = jnp.where(live, cot[...].astype(f32), 0.0)
    d_out_low = d_out.astype(bf16)
    d_hidden = nt(d_out_low, w_down)
    sig = jax.nn.sigmoid(gate)
    act = gate * sig
    hidden = (act * up).astype(bf16)
    out_part = nn(hidden, w_down) + jnp.where(own, middle, 0.0)
    d_up = (d_hidden * act).astype(bf16)
    d_gate = (d_hidden * up * sig * (1.0 + gate * (1.0 - sig))).astype(bf16)
    d_normed = nt(d_gate, w_gate) + nt(d_up, w_up)

    leaving = []

    def send(source, target):
        copy = pltpu.make_async_copy(source, target, left.at[len(leaving)])
        copy.start()
        leaving.append(copy)

    def send_grad(i, grad):
        low = grad.astype(bf16)
        for k in range(2):
            for x in range(4):
                at = 64 * (4 * k + x)
                own_grads[i, x, k] = low[at : at + 64]
        for step, grads in enumerate((grads0, grads1, grads2, grads3)):
            send(
                own_grads.at[i, lax.rem(place[4] + step, 4)],
                grads.at[:, :, D * i : D * (i + 1)],
            )

    send_grad(2, tn(hidden, d_out_low))
    send_grad(0, tn(normed, d_gate))
    send_grad(1, tn(normed, d_up))
    d_middle = jnp.where(own, d_out, 0.0) + norm_back(d_normed, scaled, inv, gain)
    d_middle_low = d_middle.astype(bf16)
    own_sent[...] = nt(w_out, d_middle_low).astype(bf16).reshape(HEADS, HEAD, TEAM_ROWS)
    send(own_sent, sent)
    back[...] = d_middle_low
    ahead[...] = out_part.astype(bf16)
    for one in range(2):
        for target, other in ((own_kept, core), (swapped, 1 - core)):
            here = pl.ds(pl.multiple_of((2 * (z ^ one) + other) * ROWS, ROWS), ROWS)
            target[one, :, 0:D] = back[here, :]
            target[one, :, D : 2 * D] = ahead[here, :]
    send(own_kept, kept)
    send_grad(3, nn(mixed_t, d_middle_low))
    norm_rows[0:1, :] = jnp.sum(d_normed * scaled, 0, keepdims=True)
    norm_rows[1:2, :] = jnp.sum(d_normed, 0, keepdims=True)
    norm_rows[2:8, :] = jnp.zeros((6, D), f32)
    finish(leaving)


def add_kernel(kept, arrived, own, other):
    own[...] = (kept[0].astype(f32) + arrived[0].astype(f32)).astype(bf16)
    other[...] = (kept[1].astype(f32) + arrived[1].astype(f32)).astype(bf16)


def scale_kernel(place, near, far, other, scaled):
    for index in range(8):
        source, first = (near, far)[index // 4], 2 * (index % 4)
        x = source[first : first + 2, 0:ROWS, :].reshape(2 * ROWS, D).astype(f32)
        low = norm_parts(x)[0].astype(bf16)
        for one in range(2):
            block = block_of(place, first + one, index // 4)
            scaled[block] = low[one * ROWS : (one + 1) * ROWS]


def attend_back_kernel(
    place, length, d_mixed, q_in, k_in, v_in, o_in, lse_in, cos, sin, scaled, head_cols, norm_rows,
    sent, sent0, sent1, sent2, sent3,
    d_o, probs, d_scores, dq, dk, dv, table, normal, cos_now, sin_now, cols, norms, own_sent, here_now, left,
):
    loads = [
        pltpu.make_async_copy(source, target, here_now.at[i])
        for i, (source, target) in enumerate(
            (
                (cos, cos_now),
                (sin, sin_now),
                (scaled, normal),
                (head_cols.at[0:104, :], cols),
                (norm_rows, norms),
            )
        )
    ]
    for load in loads:
        load.start()
    for y in range(LEN // TEAM_ROWS):
        total = d_mixed[TEAM * y].astype(f32)
        for t in range(1, TEAM):
            total = total + d_mixed[TEAM * y + t].astype(f32)
        d_o[:, y * TEAM_ROWS : (y + 1) * TEAM_ROWS] = total.astype(bf16)
    keys_t = k_in[...]
    keys = key_columns(keys_t.astype(f32), length[0])
    ones = jnp.ones((4, LEN), f32)
    pad = jnp.zeros((128 - HEAD - 4, LEN), f32)
    values = jnp.concatenate([v_in[...].astype(f32), ones, pad], 0).T.astype(bf16)[:, :AUG]
    d_o_t = d_o[...]
    inner = jnp.sum(d_o_t.astype(f32) * o_in[...], 0, keepdims=True)
    zero_row = jnp.zeros((1, LEN), f32)
    one_row = jnp.ones((1, LEN), f32)
    q_rows = with_rows(q_in[...], [one_row] + split3(-lse_in[...]))
    do_rows = with_rows(d_o_t, [zero_row] + split3(-inner))
    tile = 512
    for i in range(LEN // tile):
        here = slice(i * tile, (i + 1) * tile)
        p = jnp.exp2(nn(keys, q_rows[:, here]))
        ds = (p * nn(values, do_rows[:, here])).astype(bf16)
        probs[:, here] = p.astype(bf16)
        d_scores[:, here] = ds
        dq[:, here] = nn(keys_t, ds) * SCALE
    dk[...] = nt(q_in[...], d_scores[...]) * LN2
    dv[...] = nt(d_o_t, probs[...])
    finish(loads)
    c = cos_now[...]
    s = sin_now[...]
    q1, q2 = dq[0:HALF], dq[HALF:HEAD]
    k1, k2 = dk[0:HALF], dk[HALF:HEAD]
    dq_t = jnp.concatenate([q1 * c + q2 * s, q2 * c - q1 * s], 0).astype(bf16)
    dk_t = jnp.concatenate([k1 * c + k2 * s, k2 * c - k1 * s], 0).astype(bf16)
    dv_t = dv[...].astype(bf16)
    for b in range(SEQ):
        here = slice(b * ROWS, (b + 1) * ROWS)
        own_sent[b, 0:32] = dq_t[:, here]
        own_sent[b, 32:64] = dk_t[:, here]
        own_sent[b, 64:96] = dv_t[:, here]
    leaving = pltpu.make_async_copy(own_sent, sent, left.at[0])
    leaving.start()
    d_lin = jnp.concatenate([dq_t, dk_t, dv_t], 0)
    product = nn(d_lin, normal[...].reshape(LEN, D))
    total = jnp.sum(d_lin.astype(f32), 1, keepdims=True)
    weights = cols[0:96, :]
    gain = cols[96:97, :]
    bias = cols[97:98, :]
    rows = [
        product * gain + total * bias,
        jnp.sum(product * weights, 0, keepdims=True),
        jnp.sum(total * weights, 0, keepdims=True),
        norms[0:2, :],
        jnp.zeros((28, D), f32),
    ]
    table[...] = jnp.concatenate(rows, 0).T
    for step, part in enumerate((sent0, sent1, sent2, sent3)):
        x = lax.rem(place[4] + step, 4)
        for k in range(2):
            at = pl.multiple_of((4 * k + x) * 64, 64)
            part[k] = table[pl.ds(at, 64), :].astype(bf16)
    leaving.wait()


def regroup_kernel(part0, part1, part2, part3, sent):
    total = part0[...].astype(f32)
    for part in (part1, part2, part3):
        total = total + part[...].astype(f32)
    total = total.reshape(2 * 64, FEED_LANES)
    for d in range(SEQ * 2):
        sent[d, :, :FEED_LANES] = total[4 * d : 4 * d + 4].astype(bf16)
        sent[d, :, FEED_LANES:] = jnp.zeros((4, 128), bf16)


def append_kernel(part0, part1, part2, part3, given, sent, rows, left):
    heads = part0[...].astype(f32)
    for part in (part1, part2, part3):
        heads = heads + part[...].astype(f32)
    heads = heads.reshape(128, 128)
    for d in range(SEQ * 2):
        rows[d] = heads[4 * d : 4 * d + 4].astype(bf16)
    copy = pltpu.make_async_copy(rows, sent.at[:, :, FEED_LANES:], left.at[0])
    copy.start()
    copy.wait()


def input_grad_kernel(
    place, length, tokens, d_lin, rows0, rows1, rows2, rows3, w0, w1, head_cols,
    grad_tokens, layer_output,
    parts, arrived,
):
    weights = (rows0, rows1, rows2, rows3)
    loads = [load_part(place, weights, parts, arrived, i) for i in range(3)]
    for load in loads:
        for copy in load:
            copy.start()
    seq = place[3]
    gain = head_cols[96:97, :]
    scaled, inv = norm_parts(tokens[0].astype(f32))
    d_t = jnp.zeros((D, ROWS), f32)
    for part, load in enumerate(loads):
        d_part = d_lin[:, part * HEAD : (part + 1) * HEAD, :].reshape(D, ROWS)
        finish(load)
        d_t = d_t + nn(parts[part].reshape(D, D), d_part)
    total = w0[...].astype(f32) + w1[...].astype(f32)
    grad_tokens[0] = total[:, 0:D] + norm_back(d_t.T, scaled, inv, gain)
    row = lax.broadcasted_iota(jnp.int32, (ROWS, 1), 0)
    live = (seq * ROWS + row) < length[0]
    layer_output[0] = jnp.where(live, total[:, D : 2 * D], 0.0).astype(bf16)


def sum_kernel(
    parts, gain1, bias1, grad_query, grad_key, grad_value, grad_output, gain2, bias2,
    grad_gate, grad_up, grad_down,
):
    members = []
    for t in range(TEAM):
        total = parts[t, :, :FEED_LANES].astype(f32)
        for other in range(1, 2 * SEQ // TEAM):
            total = total + parts[TEAM * other + t, :, :FEED_LANES].astype(f32)
        members.append(total)
        grad_down[4 * t : 4 * t + 4, :] = total[:, 1024:1536]
    grad_output[...] = sum(m[:, 1536:2048] for m in members)
    pieces = []
    for u in range(4):
        for at in (128 * u, 512 + 128 * u):
            pieces.append(jnp.concatenate([m[:, at : at + 128] for m in members], 1))
    wide = jnp.concatenate(pieces, 0)
    high = wide.astype(bf16)
    low = (wide - high.astype(f32)).astype(bf16)
    order = column_order()
    wide = nt(high, order) + nt(low, order)
    for u in range(4):
        here = slice(512 * u, 512 * (u + 1))
        grad_gate[:, here] = wide[8 * u : 8 * u + 4]
        grad_up[:, here] = wide[8 * u + 4 : 8 * u + 8]
    heads = [
        parts[h, :, FEED_LANES:].astype(f32) + parts[SEQ + h, :, FEED_LANES:].astype(f32)
        for h in range(HEADS)
    ]
    lane = lax.broadcasted_iota(jnp.int32, (4, 128), 1)
    row = lax.broadcasted_iota(jnp.int32, (4, 128), 0)
    for i, grad in enumerate((grad_query, grad_key, grad_value)):
        for u in range(4):
            tile = jnp.zeros((4, 128), f32)
            for r in range(4):
                moved = pltpu.roll(heads[4 * u + r], (HEAD * (r - i)) % 128, 1)
                tile = jnp.where(lane // HEAD == r, moved, tile)
            grad[:, 128 * u : 128 * (u + 1)] = tile
    norms = sum(heads)
    for n, grad in enumerate((gain1, bias1, gain2, bias2)):
        column = jnp.where(lane == row, norms[:, 96 + n : 97 + n], 0.0)
        grad[...] = jnp.sum(column, 0)[0:4]


def call(kernel, ins, outs, scratch=(), vmem=8, flops=0, aliases={}):
    places = {"V": pltpu.VMEM, "U": pltpu.VMEM, "H": pltpu.VMEM, "A": pl.ANY, "P": pl.ANY, "W": pl.ANY, "S": pltpu.SMEM}
    inner = pl.pallas_call(
        kernel,
        out_shape=tuple(
            (pltpu.VMEM if where == "V" else pltpu.HBM)(shape, kind) for shape, kind, where in outs
        ),
        in_specs=[pl.BlockSpec(memory_space=places[where]) for where in ins],
        out_specs=tuple(pl.BlockSpec(memory_space=places[where]) for _, _, where in outs),
        scratch_shapes=[
            pltpu.SemaphoreType.DMA((s,)) if isinstance(s, int) else pltpu.VMEM(*s) for s in scratch
        ],
        input_output_aliases=aliases,
        compiler_params=pltpu.CompilerParams(vmem_limit_bytes=vmem * 2**20),
        cost_estimate=pl.CostEstimate(flops=flops, bytes_accessed=0, transcendentals=0),
    )

    def run(*args):
        assert len(args) == len(ins)
        return inner(
            *(
                pltpu.with_memory_space_constraint(x, pltpu.HBM if where in "HA" else pltpu.VMEM)
                if where in "HAVW"
                else x
                for x, where in zip(args, ins)
            )
        )

    return run


def rope_tables():
    freq = 10000.0 ** (-2.0 * np.arange(HALF) / HEAD)
    angles = freq[:, None] * np.arange(LEN)[None, :]
    return np.cos(angles).astype(np.float32), np.sin(angles).astype(np.float32)


def exchange(value, axes):
    return lax.all_to_all(value, axes, 0, 0, tiled=True)


def swap(value, axis):
    return lax.ppermute(value, axis, [(0, 1), (1, 0)])


def shift(value, by):
    return lax.ppermute(value, "x", [(i, (i + by) % 4) for i in range(4)])


def shards(
    tokens, lengths, norm1_gain, norm1_bias, w_query, w_key, w_value, w_output,
    norm2_gain, norm2_bias, w_gate, w_up, w_down, cotangent,
):
    y = lax.axis_index("y")
    z = lax.axis_index("z")
    core = lax.axis_index("core")
    place = jnp.stack([core, y, z, 4 * y + 2 * z + core, lax.axis_index("x"), lax.axis_index("z_lo")]).astype(jnp.int32)
    cos, sin = (jnp.asarray(table) for table in rope_tables())

    (packed,) = call(
        pack_kernel,
        "H" * 12,
        [((8, MSG_ROWS, D), bf16, "A")],
        [((8, MSG_ROWS - ROWS, D), bf16), 9],
    )(
        tokens, w_query, w_key, w_value, w_output, w_gate, w_up, w_down,
        norm1_gain, norm1_bias, norm2_gain, norm2_bias,
    )
    near = exchange(packed, CHIPS)
    cot_pair = jnp.concatenate([cotangent, swap(cotangent, "z")], 0)
    near = after(near, cot_pair, place=pltpu.VMEM)
    (near_rows,) = call(rows_kernel, "U", [((8, MSG_ROWS - ROWS, D), bf16, "V")])(near)
    far_rows = swap(near_rows, "core")

    feed_rows, heads, whole = call(
        unpack_kernel,
        "SUU",
        [
            ((1, 64, FEED_LANES), bf16, "V"),
            ((DP, 64, 128), bf16, "H"),
            ((1, 64, 3 * D), bf16, "H"),
        ],
    )(place, near_rows, far_rows)
    near = after(near, in_hbm(heads), place=pltpu.VMEM)
    far = swap(near, "core")
    cot_far = swap(cot_pair, "core")
    head_cols = exchange(heads, WINDOWS).reshape(D, 128)
    feed_other = after(swap(feed_rows, "z_lo"), in_hbm(whole), place=pltpu.VMEM)
    (feed_rows,) = call(join_kernel, "UU", [((2, 64, FEED_LANES), bf16, "H")])(feed_rows, feed_other)
    feed_rows = [feed_rows] + [shift(feed_rows, step) for step in range(1, 4)]
    whole_other = swap(whole, "z_lo")

    sent, q_t, k_t, v_t, o_t, lse, head_cols = call(
        attend_kernel,
        "SSVVUHHP",
        [
            ((SEQ, HEAD, TEAM_ROWS), bf16, "H"),
            ((HEAD, LEN), bf16, "A"),
            ((HEAD, LEN), bf16, "A"),
            ((HEAD, LEN), bf16, "A"),
            ((HEAD, LEN), f32, "H"),
            ((1, LEN), f32, "H"),
            ((128, D), f32, "A"),
        ],
        [
            ((HEAD, LEN), bf16),
            ((HEAD, LEN), bf16),
            ((HEAD, LEN), bf16),
            ((128, D), f32),
            4,
        ],
        vmem=24,
        flops=19 * 10**9,
    )(place, lengths, near, far, head_cols, cos, sin, cot_far)
    sent = after(sent, whole_other)
    (scaled,) = call(
        scale_kernel, "SUUA", [((SEQ, ROWS, D), bf16, "H")], vmem=12
    )(place, near, far, sent)
    mixed = exchange(sent, WINDOW)
    (whole,) = call(join_kernel, "HU", [((2, 64, 3 * D), bf16, "H")])(whole, whole_other)

    d_sent, kept, swapped, *grads, norm_rows = call(
        feed_kernel,
        "SSPPPAAAAA" + "A" * 4,
        [
            ((HEADS, HEAD, TEAM_ROWS), bf16, "A"),
            ((2, ROWS, 2 * D), bf16, "A"),
            ((2, ROWS, 2 * D), bf16, "V"),
            *[((2, 64, FEED_LANES), bf16, "A")] * 4,
            ((8, D), f32, "H"),
        ],
        [
            ((HEADS, HEAD, TEAM_ROWS), bf16),
            ((TEAM_ROWS, D), bf16),
            ((TEAM_ROWS, D), bf16),
            ((8, D), f32),
            ((TEAM_ROWS, D), bf16),
            ((TEAM_ROWS, D), bf16),
            ((4, 2, 4, 64, 512), bf16),
            ((HEADS, HEAD, TEAM_ROWS), bf16),
            ((2, ROWS, 2 * D), bf16),
            ((4, 4, 2, 64, 512), bf16),
            32, 10, 18,
        ],
        vmem=28,
    )(
        place, lengths, mixed, near, far, cot_pair, cot_far, head_cols, whole, scaled,
        *feed_rows,
    )
    row_weights = [whole] + [shift(whole, step) for step in range(1, 4)]
    d_mixed = exchange(after(d_sent, row_weights[1], row_weights[3]), WINDOW)
    grads[3] = after(grads[3], row_weights[2])
    feed_grads = [grads[0]] + [shift(grads[step], step) for step in range(1, 4)]
    w0, w1 = call(
        add_kernel, "HV", [((ROWS, 2 * D), bf16, "H")] * 2
    )(kept, swap(swapped, "core"))
    w1 = swap(w1, "z")

    lin_sent, *head_grads = call(
        attend_back_kernel,
        "SSVHHHHHAAAAA",
        [((SEQ, 96, ROWS), bf16, "A")] + [((2, 64, 128), bf16, "V")] * 4,
        [
            ((HEAD, LEN), bf16),
            ((LEN, LEN), bf16),
            ((LEN, LEN), bf16),
            ((HEAD, LEN), f32),
            ((HEAD, LEN), f32),
            ((HEAD, LEN), f32),
            ((D, 128), f32),
            ((SEQ, ROWS, D), bf16),
            ((HALF, LEN), f32),
            ((HALF, LEN), f32),
            ((104, D), f32),
            ((8, D), f32),
            ((SEQ, 96, ROWS), bf16),
            5, 1,
        ],
        vmem=42,
    )(place, lengths, d_mixed, q_t, k_t, v_t, o_t, lse, cos, sin, scaled, head_cols, norm_rows)
    lin_sent = after(lin_sent, w1)
    back = exchange(lin_sent, WINDOW)
    head_grads = [head_grads[0]] + [shift(head_grads[step], step) for step in range(1, 4)]
    (grad_sent,) = call(regroup_kernel, "HUUU", [((2 * SEQ, 4, GRAD_LANES), bf16, "H")])(*feed_grads)
    (grad_sent,) = call(
        append_kernel,
        "UUUUA",
        [((2 * SEQ, 4, GRAD_LANES), bf16, "A")],
        [((2 * SEQ, 4, 128), bf16), 1],
        aliases={4: 0},
    )(*head_grads, grad_sent)
    grad_parts = exchange(after(grad_sent, back), SLICE)

    grad_tokens, layer_output = call(
        input_grad_kernel,
        "SSHVAPPPHHH",
        [((1, ROWS, D), f32, "H"), ((1, ROWS, D), bf16, "H")],
        [((3, 2, 4, 64, 512), bf16), 24],
    )(place, lengths, tokens, back, *row_weights, w0, w1, head_cols)
    weight_grads = call(
        sum_kernel,
        "V",
        [((4,), f32, "H")] * 2 + [((4, D), f32, "H")] * 4 + [((4,), f32, "H")] * 2
        + [((4, FF), f32, "H")] * 2 + [((16, D), f32, "H")],
    )(grad_parts)
    return (layer_output, grad_tokens) + tuple(weight_grads)


def solution(mesh):
    flat = P(ALL)
    rows = P(ALL, None)
    blocks = P(("z_lo", "x"), WINDOW, None)
    return jax.shard_map(
        shards,
        mesh=Mesh(mesh.devices.reshape(2, 4, 4, 2, 2), ALL),
        in_specs=(
            blocks, P(("z_lo", "x")), flat, flat, rows, rows, rows, rows, flat, flat, rows, rows, rows, blocks,
        ),
        out_specs=(
            blocks, blocks, flat, flat, rows, rows, rows, rows, flat, flat, rows, rows, rows,
        ),
        check_vma=False,
    )
```

```python
import math

import jax
import jax.numpy as jnp
import numpy as np
from jax import lax
from jax.experimental import pallas as pl
from jax.experimental.pallas import tpu as pltpu
from jax.sharding import Mesh
from jax.sharding import PartitionSpec as P

HEADS = 16
HEAD = 32
HALF = HEAD // 2
D = 512
FF = 2048
LEN = 2048
ROWS = 128
TEAM = 4
TEAM_ROWS = TEAM * ROWS
FF_PART = FF // TEAM
DEVICES = 128
SEQ = 16
DP = 8
KEY_CHUNK = 256
AUG = 48

EPS = 1e-05
MASKED = -1.0e9
SCALE = HEAD**-0.5
LOG2E = math.log2(math.e)
LN2 = math.log(2.0)

f32 = jnp.float32
bf16 = jnp.bfloat16
WINDOW = ("y", "z", "core")
CHIPS = ("y", "z")
SLICE = ("z_lo", "y", "z", "core")
WINDOWS = ("z_lo", "x")
ALL = ("z_lo", "x", "y", "z", "core")


def nn(a, b):
    return lax.dot_general(a, b, (((1,), (0,)), ((), ())), preferred_element_type=f32)


def nt(a, b):
    return lax.dot_general(a, b, (((1,), (1,)), ((), ())), preferred_element_type=f32)


def tn(a, b):
    return lax.dot_general(a, b, (((0,), (0,)), ((), ())), preferred_element_type=f32)


def norm_parts(x):
    centered = x - jnp.mean(x, -1, keepdims=True)
    inv = lax.rsqrt(jnp.mean(centered * centered, -1, keepdims=True) + EPS)
    return centered * inv, inv


def norm_back(grad, scaled, inv, gain):
    e = grad * gain
    return inv * (
        e - jnp.mean(e, -1, keepdims=True) - scaled * jnp.mean(e * scaled, -1, keepdims=True)
    )


def split3(row):
    hi = row.astype(bf16)
    rest = row - hi.astype(f32)
    mid = rest.astype(bf16)
    low = (rest - mid.astype(f32)).astype(bf16)
    return [hi.astype(f32), mid.astype(f32), low.astype(f32)]


def key_columns(keys_t, length):
    place = lax.broadcasted_iota(jnp.int32, (1, LEN), 1)
    mask = jnp.where(place < length, 0.0, MASKED).astype(f32)
    ones = jnp.ones((3, LEN), f32)
    pad = jnp.zeros((128 - HEAD - 4, LEN), f32)
    return jnp.concatenate([keys_t, mask, ones, pad], 0).T.astype(bf16)[:, :AUG]


def with_rows(data_t, rows):
    pad = jnp.zeros((AUG - HEAD - len(rows), data_t.shape[1]), f32)
    return jnp.concatenate([data_t.astype(f32)] + rows + [pad], 0).astype(bf16)


def in_hbm(value):
    return pltpu.with_memory_space_constraint(value, pltpu.HBM)


def after(value, *others, place=pltpu.HBM):
    def kernel(*refs):
        pass

    return pl.pallas_call(
        kernel,
        out_shape=place(value.shape, value.dtype),
        in_specs=[pl.BlockSpec(memory_space=pl.ANY)] * (1 + len(others)),
        out_specs=pl.BlockSpec(memory_space=pl.ANY),
        input_output_aliases={0: 0},
        compiler_params=pltpu.CompilerParams(vmem_limit_bytes=2**20),
        cost_estimate=pl.CostEstimate(flops=0, bytes_accessed=0, transcendentals=0),
    )(pltpu.with_memory_space_constraint(value, place), *others)


FEED_LANES = FF_PART * 3 + D
GRAD_LANES = FEED_LANES + 128
MSG_ROWS = ROWS + 48


def column_order():
    n = lax.broadcasted_iota(jnp.int32, (512, 1), 0)
    to = ((n >> 2) & 3) * 128 + (n >> 7) * 32 + ((n >> 4) & 7) * 4 + (n & 3)
    lane = lax.broadcasted_iota(jnp.int32, (512, 512), 1)
    return jnp.where(lane == to, 1.0, 0.0).astype(bf16)


def pack_kernel(
    tokens, w_query, w_key, w_value, w_output, w_gate, w_up, w_down, gain1, bias1, gain2, bias2,
    sent,
    rows, left,
):
    leaving = [
        pltpu.make_async_copy(tokens.at[0], sent.at[chip, 0:ROWS, :], left.at[chip])
        for chip in range(8)
    ]
    for copy in leaving:
        copy.start()
    narrow = [w[...].astype(f32) for w in (w_query, w_key, w_value)]
    gate = w_gate[...].astype(f32)
    up = w_up[...].astype(f32)
    down = w_down[...].astype(f32)
    pieces = []
    for u in range(4):
        here = slice(512 * u, 512 * (u + 1))
        pieces.append(jnp.concatenate([gate[:, here], up[:, here]], 0))
    wide = nn(jnp.concatenate(pieces, 0).astype(bf16), column_order())
    lane = lax.broadcasted_iota(jnp.int32, (4, 128), 1)
    row = lax.broadcasted_iota(jnp.int32, (4, 128), 0)
    norms = jnp.zeros((4, 128), f32)
    for n, ref in enumerate((gain1, bias1, gain2, bias2)):
        for i in range(4):
            value = ref[i : i + 1].astype(f32).reshape(1, 1)
            norms = norms + jnp.where((lane == 96 + n) & (row == i), value, 0.0)
    out = w_output[...].astype(f32)
    nothing = jnp.zeros((4, 512), f32)
    for z in range(2):
        mine = []
        for t in (2 * z, 2 * z + 1):
            cols = slice(128 * t, 128 * (t + 1))
            mine.append(jnp.concatenate([wide[8 * u : 8 * u + 4, cols] for u in range(4)], 1))
            mine.append(jnp.concatenate([wide[8 * u + 4 : 8 * u + 8, cols] for u in range(4)], 1))
            mine.append(down[4 * t : 4 * t + 4])
        mine = jnp.concatenate(mine + [out] + narrow, 0)
        for y in range(4):
            tile = slice(128 * y, 128 * (y + 1))
            heads = []
            for t in (2 * z, 2 * z + 1):
                q, k, v = (
                    pltpu.roll(w[:, tile], (HEAD * (i - t)) % 128, 1)
                    for i, w in enumerate(narrow)
                )
                heads.append(
                    jnp.where(
                        lane < 32, q, jnp.where(lane < 64, k, jnp.where(lane < 96, v, norms))
                    )
                )
            heads = jnp.concatenate(heads + [nothing[:, :256]], 1)
            low = jnp.concatenate([mine, heads, nothing], 0).astype(bf16)
            rows[2 * y + z] = low
    copy = pltpu.make_async_copy(rows, sent.at[:, ROWS:, :], left.at[8])
    copy.start()
    leaving.append(copy)
    finish(leaving)


def rows_kernel(near, rows):
    rows[...] = near[:, ROWS:, :]


def unpack_kernel(place, near, far, feed, heads, whole):
    second = place[0] == 1
    for group in range(4):
        blocks = []
        for chip in (2 * group, 2 * group + 1):
            own = near[chip].astype(f32)
            other = far[chip].astype(f32)
            blocks += [jnp.where(second, other, own), jnp.where(second, own, other)]
        here = slice(16 * group, 16 * (group + 1))
        for i in range(3):
            cols = jnp.concatenate(
                [
                    jnp.where(second, b[4 * (i + 3) : 4 * (i + 4)], b[4 * i : 4 * (i + 1)])
                    for b in blocks
                ],
                0,
            )
            feed[0, here, D * i : D * (i + 1)] = cols.astype(bf16)
        for i in range(4):
            cols = jnp.concatenate([b[4 * (i + 6) : 4 * (i + 7)] for b in blocks], 0).astype(bf16)
            if i == 0:
                feed[0, here, 3 * D : 4 * D] = cols
            else:
                whole[0, here, D * (i - 1) : D * i] = cols
        cols = jnp.concatenate(
            [jnp.where(second, b[40:44, 128:256], b[40:44, 0:128]) for b in blocks], 0
        )
        cols = cols.astype(bf16)
        for w in range(DP):
            heads[w, here, :] = cols


def join_kernel(own, other, feed):
    feed[0] = own[0]
    feed[1] = other[0]


def block_of(place, chip, other):
    return 2 * chip + (place[0] ^ other)


def attend_kernel(
    place, length, near, far, head_cols, cos, sin, other,
    sent, q_out, k_out, v_out, o_out, lse_out, cols_out,
    q_t, k_t, v_t, own_cols, left,
):
    leaving = []

    def send(source, target):
        copy = pltpu.make_async_copy(source, target, left.at[len(leaving)])
        copy.start()
        leaving.append(copy)

    cols = head_cols[...].reshape(D, 128).astype(f32).T
    own_cols[...] = cols
    send(own_cols, cols_out)
    gain = cols[96:97, :]
    bias = cols[97:98, :]
    weights_t = cols[0:96, :].astype(bf16)
    for index in range(8):
        source, first = (near, far)[index // 4], 2 * (index % 4)
        x = source[first : first + 2, 0:ROWS, :].reshape(2 * ROWS, D).astype(f32)
        scaled, _ = norm_parts(x)
        normed = (scaled * gain + bias).astype(bf16)
        lin = nt(weights_t, normed)
        for one in range(2):
            block = block_of(place, first + one, index // 4)
            here = pl.ds(pl.multiple_of(block * ROWS, ROWS), ROWS)
            part = lin[:, one * ROWS : (one + 1) * ROWS]
            c = cos[:, here]
            s = sin[:, here]
            q1, q2 = part[0:16], part[16:32]
            k1, k2 = part[32:48], part[48:64]
            fold = SCALE * LOG2E
            q_t[:, here] = (
                jnp.concatenate([q1 * c - q2 * s, q2 * c + q1 * s], 0) * fold
            ).astype(bf16)
            k_t[:, here] = jnp.concatenate([k1 * c - k2 * s, k2 * c + k1 * s], 0).astype(bf16)
            v_t[:, here] = part[64:96].astype(bf16)
    send(q_t, q_out)
    send(k_t, k_out)
    send(v_t, v_out)
    keys = key_columns(k_t[...].astype(f32), length[0])
    one_row = jnp.ones((1, LEN), f32)
    values_t = with_rows(v_t[...], [one_row])
    queries_t = with_rows(q_t[...], [one_row])
    top = mixed = None
    for i in range(LEN // KEY_CHUNK):
        here = slice(i * KEY_CHUNK, (i + 1) * KEY_CHUNK)
        scores = nn(keys[here, :], queries_t)
        new_top = jnp.max(scores, axis=0, keepdims=True)
        if i:
            new_top = jnp.maximum(top, new_top)
        weights = jnp.exp2(scores - new_top).astype(bf16)
        added = nn(values_t[:, here], weights)
        mixed = mixed * jnp.exp2(top - new_top) + added if i else added
        top = new_top
    total = mixed[HEAD : HEAD + 1]
    out = mixed[:HEAD] / total
    o_out[...] = out
    lse_out[...] = top + jnp.log2(total)
    low = out.astype(bf16)
    for i in range(LEN // TEAM_ROWS):
        for t in range(TEAM):
            sent[TEAM * i + t] = low[:, i * TEAM_ROWS : (i + 1) * TEAM_ROWS]
    finish(leaving)


def load_part(place, weights, parts, arrived, i):
    return [
        pltpu.make_async_copy(
            rows.at[place[5] ^ k, :, 512 * i : 512 * (i + 1)],
            parts.at[i, k, lax.rem(place[4] + 4 - step, 4)],
            arrived.at[8 * i + 4 * k + step],
        )
        for k in range(2)
        for step, rows in enumerate(weights)
    ]


def finish(copies):
    for copy in copies:
        copy.wait()


def feed_kernel(
    place, length, mixed, near, far, cot_near, cot_far, head_cols, other1, other2,
    rows0, rows1, rows2, rows3,
    sent, kept, swapped, grads0, grads1, grads2, grads3, norm_rows,
    mixed_rows, tokens, cot, norms, back, ahead, parts, own_sent, own_kept, own_grads,
    arrived, tokens_arrived, left,
):
    core, team, z = place[0], place[1], place[2]
    first = [
        pltpu.make_async_copy(mixed, mixed_rows, tokens_arrived.at[8]),
        pltpu.make_async_copy(head_cols.at[96:104, :], norms, tokens_arrived.at[9]),
    ]
    later = []
    for one in range(2):
        for other in range(2):
            here = pl.ds(pl.multiple_of((2 * (z ^ one) + (core ^ other)) * ROWS, ROWS), ROWS)
            first.append(
                pltpu.make_async_copy(
                    (near, far)[other].at[2 * team + (z ^ one), 0:ROWS, :],
                    tokens.at[here, :],
                    tokens_arrived.at[2 * one + other],
                )
            )
            later.append(
                pltpu.make_async_copy(
                    (cot_near, cot_far)[other].at[one],
                    cot.at[here, :],
                    tokens_arrived.at[4 + 2 * one + other],
                )
            )
    weights = (rows0, rows1, rows2, rows3)
    loads = [load_part(place, weights, parts, arrived, i) for i in (3, 0, 1, 2)]
    for load in [loads[0], first, *loads[1:], later]:
        for copy in load:
            copy.start()
    member = 2 * z + core
    row = lax.broadcasted_iota(jnp.int32, (TEAM_ROWS, 1), 0)
    live = (team * TEAM_ROWS + row) < length[0]
    own = (row // ROWS) == member
    finish(first)
    finish(loads[0])
    gain = norms[2:3, :]
    bias = norms[3:4, :]
    mixed_t = mixed_rows[...].reshape(D, TEAM_ROWS)
    w_out = parts[3].reshape(D, D)
    middle = tokens[...].astype(f32) + tn(mixed_t, w_out)
    scaled, inv = norm_parts(middle)
    normed = (scaled * gain + bias).astype(bf16)
    finish(loads[1])
    w_gate = parts[0].reshape(D, FF_PART)
    gate = nn(normed, w_gate)
    finish(loads[2])
    w_up = parts[1].reshape(D, FF_PART)
    up = nn(normed, w_up)
    finish(loads[3])
    finish(later)
    w_down = parts[2].reshape(FF_PART, D)
    d_out = jnp.where(live, cot[...].astype(f32), 0.0)
    d_out_low = d_out.astype(bf16)
    d_hidden = nt(d_out_low, w_down)
    sig = jax.nn.sigmoid(gate)
    act = gate * sig
    hidden = (act * up).astype(bf16)
    out_part = nn(hidden, w_down) + jnp.where(own, middle, 0.0)
    d_up = (d_hidden * act).astype(bf16)
    d_gate = (d_hidden * up * sig * (1.0 + gate * (1.0 - sig))).astype(bf16)
    d_normed = nt(d_gate, w_gate) + nt(d_up, w_up)

    leaving = []

    def send(source, target):
        copy = pltpu.make_async_copy(source, target, left.at[len(leaving)])
        copy.start()
        leaving.append(copy)

    def send_grad(i, grad):
        low = grad.astype(bf16)
        for k in range(2):
            for x in range(4):
                at = 64 * (4 * k + x)
                own_grads[i, x, k] = low[at : at + 64]
        for step, grads in enumerate((grads0, grads1, grads2, grads3)):
            send(
                own_grads.at[i, lax.rem(place[4] + step, 4)],
                grads.at[:, :, D * i : D * (i + 1)],
            )

    send_grad(2, tn(hidden, d_out_low))
    send_grad(0, tn(normed, d_gate))
    send_grad(1, tn(normed, d_up))
    d_middle = jnp.where(own, d_out, 0.0) + norm_back(d_normed, scaled, inv, gain)
    d_middle_low = d_middle.astype(bf16)
    own_sent[...] = nt(w_out, d_middle_low).astype(bf16).reshape(HEADS, HEAD, TEAM_ROWS)
    send(own_sent, sent)
    back[...] = d_middle_low
    ahead[...] = out_part.astype(bf16)
    for one in range(2):
        for target, other in ((own_kept, core), (swapped, 1 - core)):
            here = pl.ds(pl.multiple_of((2 * (z ^ one) + other) * ROWS, ROWS), ROWS)
            target[one, :, 0:D] = back[here, :]
            target[one, :, D : 2 * D] = ahead[here, :]
    send(own_kept, kept)
    send_grad(3, nn(mixed_t, d_middle_low))
    norm_rows[0:1, :] = jnp.sum(d_normed * scaled, 0, keepdims=True)
    norm_rows[1:2, :] = jnp.sum(d_normed, 0, keepdims=True)
    norm_rows[2:8, :] = jnp.zeros((6, D), f32)
    finish(leaving)


def add_kernel(kept, arrived, own, other):
    own[...] = (kept[0].astype(f32) + arrived[0].astype(f32)).astype(bf16)
    other[...] = (kept[1].astype(f32) + arrived[1].astype(f32)).astype(bf16)


def scale_kernel(place, near, far, other, scaled):
    for index in range(8):
        source, first = (near, far)[index // 4], 2 * (index % 4)
        x = source[first : first + 2, 0:ROWS, :].reshape(2 * ROWS, D).astype(f32)
        low = norm_parts(x)[0].astype(bf16)
        for one in range(2):
            block = block_of(place, first + one, index // 4)
            scaled[block] = low[one * ROWS : (one + 1) * ROWS]


def attend_back_kernel(
    place, length, d_mixed, q_in, k_in, v_in, o_in, lse_in, cos, sin, scaled, head_cols, norm_rows,
    sent, sent0, sent1, sent2, sent3,
    d_o, probs, d_scores, dq, dk, dv, table, normal, cos_now, sin_now, cols, norms, own_sent, here_now, left,
):
    loads = [
        pltpu.make_async_copy(source, target, here_now.at[i])
        for i, (source, target) in enumerate(
            (
                (cos, cos_now),
                (sin, sin_now),
                (scaled, normal),
                (head_cols.at[0:104, :], cols),
                (norm_rows, norms),
            )
        )
    ]
    for load in loads:
        load.start()
    for y in range(LEN // TEAM_ROWS):
        total = d_mixed[TEAM * y].astype(f32)
        for t in range(1, TEAM):
            total = total + d_mixed[TEAM * y + t].astype(f32)
        d_o[:, y * TEAM_ROWS : (y + 1) * TEAM_ROWS] = total.astype(bf16)
    keys_t = k_in[...]
    keys = key_columns(keys_t.astype(f32), length[0])
    ones = jnp.ones((4, LEN), f32)
    pad = jnp.zeros((128 - HEAD - 4, LEN), f32)
    values = jnp.concatenate([v_in[...].astype(f32), ones, pad], 0).T.astype(bf16)[:, :AUG]
    d_o_t = d_o[...]
    inner = jnp.sum(d_o_t.astype(f32) * o_in[...], 0, keepdims=True)
    zero_row = jnp.zeros((1, LEN), f32)
    one_row = jnp.ones((1, LEN), f32)
    q_rows = with_rows(q_in[...], [one_row] + split3(-lse_in[...]))
    do_rows = with_rows(d_o_t, [zero_row] + split3(-inner))
    tile = 512
    for i in range(LEN // tile):
        here = slice(i * tile, (i + 1) * tile)
        p = jnp.exp2(nn(keys, q_rows[:, here]))
        ds = (p * nn(values, do_rows[:, here])).astype(bf16)
        probs[:, here] = p.astype(bf16)
        d_scores[:, here] = ds
        dq[:, here] = nn(keys_t, ds) * SCALE
    dk[...] = nt(q_in[...], d_scores[...]) * LN2
    dv[...] = nt(d_o_t, probs[...])
    finish(loads)
    c = cos_now[...]
    s = sin_now[...]
    q1, q2 = dq[0:HALF], dq[HALF:HEAD]
    k1, k2 = dk[0:HALF], dk[HALF:HEAD]
    dq_t = jnp.concatenate([q1 * c + q2 * s, q2 * c - q1 * s], 0).astype(bf16)
    dk_t = jnp.concatenate([k1 * c + k2 * s, k2 * c - k1 * s], 0).astype(bf16)
    dv_t = dv[...].astype(bf16)
    for b in range(SEQ):
        here = slice(b * ROWS, (b + 1) * ROWS)
        own_sent[b, 0:32] = dq_t[:, here]
        own_sent[b, 32:64] = dk_t[:, here]
        own_sent[b, 64:96] = dv_t[:, here]
    leaving = pltpu.make_async_copy(own_sent, sent, left.at[0])
    leaving.start()
    d_lin = jnp.concatenate([dq_t, dk_t, dv_t], 0)
    product = nn(d_lin, normal[...].reshape(LEN, D))
    total = jnp.sum(d_lin.astype(f32), 1, keepdims=True)
    weights = cols[0:96, :]
    gain = cols[96:97, :]
    bias = cols[97:98, :]
    rows = [
        product * gain + total * bias,
        jnp.sum(product * weights, 0, keepdims=True),
        jnp.sum(total * weights, 0, keepdims=True),
        norms[0:2, :],
        jnp.zeros((28, D), f32),
    ]
    table[...] = jnp.concatenate(rows, 0).T
    for step, part in enumerate((sent0, sent1, sent2, sent3)):
        x = lax.rem(place[4] + step, 4)
        for k in range(2):
            at = pl.multiple_of((4 * k + x) * 64, 64)
            part[k] = table[pl.ds(at, 64), :].astype(bf16)
    leaving.wait()


def regroup_kernel(part0, part1, part2, part3, sent):
    total = part0[...].astype(f32)
    for part in (part1, part2, part3):
        total = total + part[...].astype(f32)
    total = total.reshape(2 * 64, FEED_LANES)
    for d in range(SEQ * 2):
        sent[d, :, :FEED_LANES] = total[4 * d : 4 * d + 4].astype(bf16)


def append_kernel(part0, part1, part2, part3, given, sent, rows, left):
    heads = part0[...].astype(f32)
    for part in (part1, part2, part3):
        heads = heads + part[...].astype(f32)
    heads = heads.reshape(128, 128)
    for d in range(SEQ * 2):
        rows[d] = heads[4 * d : 4 * d + 4].astype(bf16)
    copy = pltpu.make_async_copy(rows, sent.at[:, :, FEED_LANES:], left.at[0])
    copy.start()
    copy.wait()


def input_grad_kernel(
    place, length, tokens, d_lin, rows0, rows1, rows2, rows3, w0, w1, head_cols,
    grad_tokens, layer_output,
    parts, arrived,
):
    weights = (rows0, rows1, rows2, rows3)
    loads = [load_part(place, weights, parts, arrived, i) for i in range(3)]
    for load in loads:
        for copy in load:
            copy.start()
    seq = place[3]
    gain = head_cols[96:97, :]
    scaled, inv = norm_parts(tokens[0].astype(f32))
    d_t = jnp.zeros((D, ROWS), f32)
    for part, load in enumerate(loads):
        d_part = d_lin[:, part * HEAD : (part + 1) * HEAD, :].reshape(D, ROWS)
        finish(load)
        d_t = d_t + nn(parts[part].reshape(D, D), d_part)
    total = w0[...].astype(f32) + w1[...].astype(f32)
    grad_tokens[0] = total[:, 0:D] + norm_back(d_t.T, scaled, inv, gain)
    row = lax.broadcasted_iota(jnp.int32, (ROWS, 1), 0)
    live = (seq * ROWS + row) < length[0]
    layer_output[0] = jnp.where(live, total[:, D : 2 * D], 0.0).astype(bf16)


def sum_kernel(
    parts, gain1, bias1, grad_query, grad_key, grad_value, grad_output, gain2, bias2,
    grad_gate, grad_up, grad_down,
):
    members = []
    for t in range(TEAM):
        total = parts[t, :, :FEED_LANES].astype(f32)
        for other in range(1, 2 * SEQ // TEAM):
            total = total + parts[TEAM * other + t, :, :FEED_LANES].astype(f32)
        members.append(total)
        grad_down[4 * t : 4 * t + 4, :] = total[:, 1024:1536]
    grad_output[...] = sum(m[:, 1536:2048] for m in members)
    pieces = []
    for u in range(4):
        for at in (128 * u, 512 + 128 * u):
            pieces.append(jnp.concatenate([m[:, at : at + 128] for m in members], 1))
    wide = jnp.concatenate(pieces, 0)
    high = wide.astype(bf16)
    low = (wide - high.astype(f32)).astype(bf16)
    order = column_order()
    wide = nt(high, order) + nt(low, order)
    for u in range(4):
        here = slice(512 * u, 512 * (u + 1))
        grad_gate[:, here] = wide[8 * u : 8 * u + 4]
        grad_up[:, here] = wide[8 * u + 4 : 8 * u + 8]
    heads = [
        parts[h, :, FEED_LANES:].astype(f32) + parts[SEQ + h, :, FEED_LANES:].astype(f32)
        for h in range(HEADS)
    ]
    lane = lax.broadcasted_iota(jnp.int32, (4, 128), 1)
    row = lax.broadcasted_iota(jnp.int32, (4, 128), 0)
    for i, grad in enumerate((grad_query, grad_key, grad_value)):
        for u in range(4):
            tile = jnp.zeros((4, 128), f32)
            for r in range(4):
                moved = pltpu.roll(heads[4 * u + r], (HEAD * (r - i)) % 128, 1)
                tile = jnp.where(lane // HEAD == r, moved, tile)
            grad[:, 128 * u : 128 * (u + 1)] = tile
    norms = sum(heads)
    for n, grad in enumerate((gain1, bias1, gain2, bias2)):
        column = jnp.where(lane == row, norms[:, 96 + n : 97 + n], 0.0)
        grad[...] = jnp.sum(column, 0)[0:4]


def call(kernel, ins, outs, scratch=(), vmem=8, flops=0, aliases={}):
    places = {"V": pltpu.VMEM, "U": pltpu.VMEM, "H": pltpu.VMEM, "A": pl.ANY, "P": pl.ANY, "W": pl.ANY, "S": pltpu.SMEM}
    inner = pl.pallas_call(
        kernel,
        out_shape=tuple(
            (pltpu.VMEM if where == "V" else pltpu.HBM)(shape, kind) for shape, kind, where in outs
        ),
        in_specs=[pl.BlockSpec(memory_space=places[where]) for where in ins],
        out_specs=tuple(pl.BlockSpec(memory_space=places[where]) for _, _, where in outs),
        scratch_shapes=[
            pltpu.SemaphoreType.DMA((s,)) if isinstance(s, int) else pltpu.VMEM(*s) for s in scratch
        ],
        input_output_aliases=aliases,
        compiler_params=pltpu.CompilerParams(vmem_limit_bytes=vmem * 2**20),
        cost_estimate=pl.CostEstimate(flops=flops, bytes_accessed=0, transcendentals=0),
    )

    def run(*args):
        assert len(args) == len(ins)
        return inner(
            *(
                pltpu.with_memory_space_constraint(x, pltpu.HBM if where in "HA" else pltpu.VMEM)
                if where in "HAVW"
                else x
                for x, where in zip(args, ins)
            )
        )

    return run


def rope_tables():
    freq = 10000.0 ** (-2.0 * np.arange(HALF) / HEAD)
    angles = freq[:, None] * np.arange(LEN)[None, :]
    return np.cos(angles).astype(np.float32), np.sin(angles).astype(np.float32)


def exchange(value, axes):
    return lax.all_to_all(value, axes, 0, 0, tiled=True)


def swap(value, axis):
    return lax.ppermute(value, axis, [(0, 1), (1, 0)])


def shift(value, by):
    return lax.ppermute(value, "x", [(i, (i + by) % 4) for i in range(4)])


def shards(
    tokens, lengths, norm1_gain, norm1_bias, w_query, w_key, w_value, w_output,
    norm2_gain, norm2_bias, w_gate, w_up, w_down, cotangent,
):
    y = lax.axis_index("y")
    z = lax.axis_index("z")
    core = lax.axis_index("core")
    place = jnp.stack([core, y, z, 4 * y + 2 * z + core, lax.axis_index("x"), lax.axis_index("z_lo")]).astype(jnp.int32)
    cos, sin = (jnp.asarray(table) for table in rope_tables())

    (packed,) = call(
        pack_kernel,
        "H" * 12,
        [((8, MSG_ROWS, D), bf16, "A")],
        [((8, MSG_ROWS - ROWS, D), bf16), 9],
    )(
        tokens, w_query, w_key, w_value, w_output, w_gate, w_up, w_down,
        norm1_gain, norm1_bias, norm2_gain, norm2_bias,
    )
    near = exchange(packed, CHIPS)
    cot_pair = jnp.concatenate([cotangent, swap(cotangent, "z")], 0)
    near = after(near, cot_pair, place=pltpu.VMEM)
    (near_rows,) = call(rows_kernel, "U", [((8, MSG_ROWS - ROWS, D), bf16, "V")])(near)
    far_rows = swap(near_rows, "core")

    feed_rows, heads, whole = call(
        unpack_kernel,
        "SUU",
        [
            ((1, 64, FEED_LANES), bf16, "V"),
            ((DP, 64, 128), bf16, "H"),
            ((1, 64, 3 * D), bf16, "H"),
        ],
    )(place, near_rows, far_rows)
    near = after(near, in_hbm(heads), place=pltpu.VMEM)
    far = swap(near, "core")
    cot_far = swap(cot_pair, "core")
    head_cols = exchange(heads, WINDOWS).reshape(D, 128)
    feed_other = after(swap(feed_rows, "z_lo"), in_hbm(whole), place=pltpu.VMEM)
    (feed_rows,) = call(join_kernel, "UU", [((2, 64, FEED_LANES), bf16, "H")])(feed_rows, feed_other)
    feed_rows = [feed_rows] + [shift(feed_rows, step) for step in range(1, 4)]
    whole_other = swap(whole, "z_lo")

    sent, q_t, k_t, v_t, o_t, lse, head_cols = call(
        attend_kernel,
        "SSVVUHHP",
        [
            ((SEQ, HEAD, TEAM_ROWS), bf16, "H"),
            ((HEAD, LEN), bf16, "A"),
            ((HEAD, LEN), bf16, "A"),
            ((HEAD, LEN), bf16, "A"),
            ((HEAD, LEN), f32, "H"),
            ((1, LEN), f32, "H"),
            ((128, D), f32, "A"),
        ],
        [
            ((HEAD, LEN), bf16),
            ((HEAD, LEN), bf16),
            ((HEAD, LEN), bf16),
            ((128, D), f32),
            4,
        ],
        vmem=24,
        flops=19 * 10**9,
    )(place, lengths, near, far, head_cols, cos, sin, cot_far)
    sent = after(sent, whole_other)
    (scaled,) = call(
        scale_kernel, "SUUA", [((SEQ, ROWS, D), bf16, "H")], vmem=12
    )(place, near, far, sent)
    mixed = exchange(sent, WINDOW)
    (whole,) = call(join_kernel, "HU", [((2, 64, 3 * D), bf16, "H")])(whole, whole_other)

    d_sent, kept, swapped, *grads, norm_rows = call(
        feed_kernel,
        "SSPPPAAAAA" + "A" * 4,
        [
            ((HEADS, HEAD, TEAM_ROWS), bf16, "A"),
            ((2, ROWS, 2 * D), bf16, "A"),
            ((2, ROWS, 2 * D), bf16, "V"),
            *[((2, 64, FEED_LANES), bf16, "A")] * 4,
            ((8, D), f32, "H"),
        ],
        [
            ((HEADS, HEAD, TEAM_ROWS), bf16),
            ((TEAM_ROWS, D), bf16),
            ((TEAM_ROWS, D), bf16),
            ((8, D), f32),
            ((TEAM_ROWS, D), bf16),
            ((TEAM_ROWS, D), bf16),
            ((4, 2, 4, 64, 512), bf16),
            ((HEADS, HEAD, TEAM_ROWS), bf16),
            ((2, ROWS, 2 * D), bf16),
            ((4, 4, 2, 64, 512), bf16),
            32, 10, 18,
        ],
        vmem=28,
    )(
        place, lengths, mixed, near, far, cot_pair, cot_far, head_cols, whole, scaled,
        *feed_rows,
    )
    row_weights = [whole] + [shift(whole, step) for step in range(1, 4)]
    d_mixed = exchange(after(d_sent, row_weights[1], row_weights[3]), WINDOW)
    grads[3] = after(grads[3], row_weights[2])
    feed_grads = [grads[0]] + [shift(grads[step], step) for step in range(1, 4)]
    w0, w1 = call(
        add_kernel, "HV", [((ROWS, 2 * D), bf16, "H")] * 2
    )(kept, swap(swapped, "core"))
    w1 = swap(w1, "z")

    lin_sent, *head_grads = call(
        attend_back_kernel,
        "SSVHHHHHAAAAA",
        [((SEQ, 96, ROWS), bf16, "A")] + [((2, 64, 128), bf16, "V")] * 4,
        [
            ((HEAD, LEN), bf16),
            ((LEN, LEN), bf16),
            ((LEN, LEN), bf16),
            ((HEAD, LEN), f32),
            ((HEAD, LEN), f32),
            ((HEAD, LEN), f32),
            ((D, 128), f32),
            ((SEQ, ROWS, D), bf16),
            ((HALF, LEN), f32),
            ((HALF, LEN), f32),
            ((104, D), f32),
            ((8, D), f32),
            ((SEQ, 96, ROWS), bf16),
            5, 1,
        ],
        vmem=42,
    )(place, lengths, d_mixed, q_t, k_t, v_t, o_t, lse, cos, sin, scaled, head_cols, norm_rows)
    lin_sent = after(lin_sent, w1)
    back = exchange(lin_sent, WINDOW)
    head_grads = [head_grads[0]] + [shift(head_grads[step], step) for step in range(1, 4)]
    (grad_sent,) = call(regroup_kernel, "HUUU", [((2 * SEQ, 4, GRAD_LANES), bf16, "H")])(*feed_grads)
    (grad_sent,) = call(
        append_kernel,
        "UUUUA",
        [((2 * SEQ, 4, GRAD_LANES), bf16, "A")],
        [((2 * SEQ, 4, 128), bf16), 1],
        aliases={4: 0},
    )(*head_grads, grad_sent)
    grad_parts = exchange(after(grad_sent, back), SLICE)

    grad_tokens, layer_output = call(
        input_grad_kernel,
        "SSHVAPPPHHH",
        [((1, ROWS, D), f32, "H"), ((1, ROWS, D), bf16, "H")],
        [((3, 2, 4, 64, 512), bf16), 24],
    )(place, lengths, tokens, back, *row_weights, w0, w1, head_cols)
    weight_grads = call(
        sum_kernel,
        "V",
        [((4,), f32, "H")] * 2 + [((4, D), f32, "H")] * 4 + [((4,), f32, "H")] * 2
        + [((4, FF), f32, "H")] * 2 + [((16, D), f32, "H")],
    )(grad_parts)
    return (layer_output, grad_tokens) + tuple(weight_grads)


def solution(mesh):
    flat = P(ALL)
    rows = P(ALL, None)
    blocks = P(("z_lo", "x"), WINDOW, None)
    return jax.shard_map(
        shards,
        mesh=Mesh(mesh.devices.reshape(2, 4, 4, 2, 2), ALL),
        in_specs=(
            blocks, P(("z_lo", "x")), flat, flat, rows, rows, rows, rows, flat, flat, rows, rows, rows, blocks,
        ),
        out_specs=(
            blocks, blocks, flat, flat, rows, rows, rows, rows, flat, flat, rows, rows, rows,
        ),
        check_vma=False,
    )
```
